128 devices in a mesh: var: 16 (over y, x), tile: 8 (over z, core).
Axes of the slice: x: 4, y: 4, z: 4, core: 2. Of those that a mesh axis runs over, the one named last changes fastest.
Arguments:
- tokens: bfloat16 [96, 96, 64, 512], P(None, 'tile', 'var'), may hold values from -6 to 6
- latent_queries: bfloat16 [3, 512], replicated, may hold values from -6 to 6
- perc_query: bfloat16 [512, 512], replicated, may hold values from -0.25 to 0.25
- perc_key: bfloat16 [512, 512], replicated
- perc_value: bfloat16 [512, 512], replicated, may hold values from -0.25 to 0.25
- perc_out: bfloat16 [512, 512], replicated, may hold values from -0.25 to 0.25
- norm_gains: float32 [2, 512], replicated, may hold values from 0.1 to 1.9
- swin_query: bfloat16 [512, 512], replicated
- swin_keyvalue: bfloat16 [512, 1024], replicated, may hold values from -0.25 to 0.25
- swin_out: bfloat16 [512, 512], replicated, may hold values from -0.25 to 0.25
- mlp_up: bfloat16 [512, 2048], replicated, may hold values from -0.25 to 0.25
- mlp_down: bfloat16 [2048, 512], replicated, may hold values from -0.125 to 0.125
Outputs:
- encoded: bfloat16 [96, 96, 3, 512], P('var', 'tile')
The draws below stay inside these ranges and needn't reach their ends.
All inputs are finite; a program needn't handle non-finite values.
Results may differ from the reference program's by a relative error of at most 0.04.
The reference program's roundings to bfloat16 on the way count: a program that leaves them out, or rounds other values in their place, can miss the bound.
Values may be sent and summed in bfloat16 or wider, within the bound.
A program may use at most 512 MiB of HBM per device.

```python
import math
import jax
import jax.numpy as jnp
from jax import lax

D = 512
HEADS = 16
FF = 2048
HD = 32
LATENT = 3
LEVS = 4
WLAT = 6
WLON = 12
TOKENS = 64
LAT = 96
LON = 96
N_VAR = 16


def head_scaled(key, log_top):
    first_key, second_key = jax.random.split(key)
    values = jax.random.normal(first_key, (D, D), jnp.float32) * D ** (-0.5)
    factors = jnp.exp(jax.random.uniform(second_key, (HEADS,), jnp.float32, 0.0, 1.0) * log_top)
    return (values * jnp.repeat(factors, HD)[None, :]).astype(jnp.bfloat16)


def draw_perc_key(key, part):
    key = jax.random.fold_in(key, 17)
    return head_scaled(key, 0.0)


def draw_swin_query(key, part):
    key = jax.random.fold_in(key, 29)
    return head_scaled(key, 0.0)


def shard_levels(rng, dims, cuts, low, top_value):
    def one(axis_at, shards_of):
        heights = jax.random.uniform(jax.random.fold_in(jax.random.fold_in(rng, 6), axis_at), (shards_of,), jnp.float32, low / len(cuts), top_value / len(cuts))
        return jnp.repeat(jnp.exp(heights), dims[axis_at] // shards_of).reshape((-1,) + (1,) * (len(dims) - axis_at - 1))

    factor_of = one(*cuts[0])
    for cut in cuts[1:]:
        factor_of = factor_of * one(*cut)
    return factor_of


def scatter_about(stream_key, shape, scale, most, cuts=(), kind=jnp.bfloat16):
    array = jax.random.normal(stream_key, shape, jnp.float32) * scale
    if len(cuts) > 0:
        array = shard_levels(stream_key, shape, cuts, -0.22, 0.18) * array
    return jnp.clip(array, min=-most, max=most).astype(kind)


def setup_inputs(seed: int = 0) -> dict:
    streams_of = jax.random.split(jax.random.key(seed), 13)
    tokens = scatter_about(streams_of[0], (LAT, LON, TOKENS, D), 1.0, 6.0, ((1, 8), (2, 16)))
    latent_queries = scatter_about(streams_of[1], (LATENT, D), 1.0, 6.0)
    perc_query = scatter_about(streams_of[2], (D, D), D ** -0.5, 0.25)
    perc_key = draw_perc_key(jax.random.fold_in(streams_of[12], 71), 0)
    perc_value = scatter_about(streams_of[4], (D, D), D ** -0.5, 0.25)
    perc_out = scatter_about(streams_of[5], (D, D), D ** -0.5, 0.25)
    norm_gains = jnp.clip(1.0 + 0.18 * jax.random.normal(streams_of[6], (2, D), jnp.float32), 0.1, 1.9)
    swin_query = draw_swin_query(jax.random.fold_in(streams_of[12], 71), 0)
    swin_keyvalue = scatter_about(streams_of[8], (D, 2 * D), D ** -0.5, 0.25)
    swin_out = scatter_about(streams_of[9], (D, D), D ** -0.5, 0.25)
    mlp_up = scatter_about(streams_of[10], (D, FF), D ** -0.5, 0.25)
    mlp_down = scatter_about(streams_of[11], (FF, D), FF ** -0.5, 0.125)
    return dict(tokens=tokens, latent_queries=latent_queries, perc_query=perc_query, perc_key=perc_key, perc_value=perc_value, perc_out=perc_out, norm_gains=norm_gains, swin_query=swin_query, swin_keyvalue=swin_keyvalue, swin_out=swin_out, mlp_up=mlp_up, mlp_down=mlp_down)


epsilon = 1e-05

def layer_norm(values, gain_row):
    average = lax.optimization_barrier(jnp.mean(values, axis=-1, keepdims=True))
    centred = values - average
    spread = lax.optimization_barrier(jnp.mean(centred * centred, axis=-1, keepdims=True))
    return centred * lax.rsqrt(spread + epsilon) * gain_row

def stored(values):
    return lax.optimization_barrier(values.astype(jnp.bfloat16)).astype(jnp.float32)

def probe_matrix(latent_queries, perc_query, perc_key):
    queries = jnp.dot(latent_queries, perc_query, preferred_element_type=jnp.float32)
    key_heads = perc_key.astype(jnp.float32).reshape(D, HEADS, HD)
    query_heads = queries.reshape(LATENT, HEADS, HD)
    key_probe = lax.optimization_barrier(jnp.sum(key_heads[:, None, :, :] * query_heads[None, :, :, :], axis=-1))
    return (key_probe / math.sqrt(HD)).reshape(D, LATENT * HEADS).astype(jnp.bfloat16)

def perceiver_row(lat_row, key_probe, value_heads, latent_queries, perc_out):
    grouped = lat_row.astype(jnp.float32).reshape(LON, N_VAR, LEVS, D)
    scores = jnp.einsum('cgtd,dk->cgtk', grouped, key_probe.astype(jnp.float32))
    maxima = lax.optimization_barrier(jnp.max(scores, axis=2))
    exponent = jnp.exp(scores - maxima[:, :, None, :])
    totals = lax.optimization_barrier(jnp.sum(exponent, axis=2))
    blended = stored(jnp.einsum('cgtk,cgtd->cgkd', stored(exponent), grouped))
    numerators = jnp.einsum('cgjhd,dhe->cgjhe', blended.reshape(LON, N_VAR, LATENT, HEADS, D), value_heads)
    global_max = lax.optimization_barrier(jnp.max(maxima, axis=1))
    scales = jnp.exp(maxima - global_max[:, None, :])
    denominator = lax.optimization_barrier(jnp.sum(totals * scales, axis=1))
    numerator_sum = lax.optimization_barrier(jnp.sum(numerators * scales.reshape(LON, N_VAR, LATENT, HEADS, 1), axis=1))
    shares = numerator_sum / denominator.reshape(LON, LATENT, HEADS, 1)
    attention = shares.astype(jnp.bfloat16).reshape(LON, LATENT, D)
    latent = latent_queries.astype(jnp.float32) + jnp.dot(attention, perc_out, preferred_element_type=jnp.float32)
    return latent.astype(jnp.bfloat16)

def swin_windows(windows, labels, norm_gains, swin_query, swin_keyvalue, swin_out, mlp_up, mlp_down):
    window_count, length, model_width = windows.shape
    residual = windows.astype(jnp.float32)
    normed = layer_norm(residual, norm_gains[0]).astype(jnp.bfloat16)
    queries = stored(jnp.dot(normed, swin_query, preferred_element_type=jnp.float32))
    keyvals = stored(jnp.dot(normed, swin_keyvalue, preferred_element_type=jnp.float32))
    queries = queries.reshape(window_count, length, HEADS, HD)
    key_part = keyvals[..., :model_width].reshape(window_count, length, HEADS, HD)
    value_part = keyvals[..., model_width:].reshape(window_count, length, HEADS, HD)
    logits = jnp.einsum('wqhe,wkhe->whqk', queries, key_part) / math.sqrt(HD)
    allowed = labels[:, :, None] == labels[:, None, :]
    logits = jnp.where(allowed[:, None, :, :], logits, -jnp.inf)
    row_max = lax.optimization_barrier(jnp.max(logits, axis=-1, keepdims=True))
    exponent = jnp.exp(logits - row_max)
    probs = stored(exponent / lax.optimization_barrier(jnp.sum(exponent, axis=-1, keepdims=True)))
    mixed = jnp.einsum('whqk,wkhe->wqhe', probs, value_part).astype(jnp.bfloat16)
    mixed = mixed.reshape(window_count, length, model_width)
    residual = residual + jnp.dot(mixed, swin_out, preferred_element_type=jnp.float32)
    normed_two = layer_norm(residual, norm_gains[1]).astype(jnp.bfloat16)
    hidden = jax.nn.gelu(jnp.dot(normed_two, mlp_up, preferred_element_type=jnp.float32), approximate=False).astype(jnp.bfloat16)
    return (residual + jnp.dot(hidden, mlp_down, preferred_element_type=jnp.float32)).astype(jnp.bfloat16)

def reference(tokens, latent_queries, perc_query, perc_key, perc_value, perc_out, norm_gains, swin_query, swin_keyvalue, swin_out, mlp_up, mlp_down):
    key_probe = probe_matrix(latent_queries, perc_query, perc_key)
    value_heads = perc_value.astype(jnp.float32).reshape(D, HEADS, HD)
    latent = lax.map(lambda lat_row: perceiver_row(lat_row, key_probe, value_heads, latent_queries, perc_out), tokens)
    half_lat = WLAT // 2
    half_lon = WLON // 2
    shifted = jnp.roll(latent, (-half_lat, -half_lon), axis=(0, 1))
    window_cols = LON // WLON
    length = WLAT * WLON * LATENT

    def window_row(block_index):
        window_band = lax.dynamic_slice_in_dim(shifted, block_index * WLAT, WLAT, 0)
        windows = window_band.reshape(WLAT, window_cols, WLON, LATENT, D).transpose(1, 0, 2, 3, 4).reshape(window_cols, length, D)
        lat_index = block_index * WLAT + jnp.arange(WLAT, dtype=jnp.int32)
        wrapped = (lat_index >= LAT - half_lat).astype(jnp.int32)
        labels = jnp.broadcast_to(wrapped[:, None, None], (WLAT, WLON, LATENT)).reshape(length)
        labels = jnp.broadcast_to(labels[None, :], (window_cols, length))
        result = swin_windows(windows, labels, norm_gains, swin_query, swin_keyvalue, swin_out, mlp_up, mlp_down)
        return result.reshape(window_cols, WLAT, WLON, LATENT, D).transpose(1, 0, 2, 3, 4).reshape(WLAT, LON, LATENT, D)
    all_bands = lax.map(window_row, jnp.arange(LAT // WLAT, dtype=jnp.int32))
    return all_bands.reshape(LAT, LON, LATENT, D)
```

```python
import functools
import math

import jax
import jax.numpy as jnp
from jax import lax
from jax.experimental import pallas as pl
from jax.experimental.pallas import tpu as pltpu
from jax.sharding import PartitionSpec as P

F32 = jnp.float32
BF16 = jnp.bfloat16
D = 512
HEADS = 16
HD = 32
LATENT = 3
LEVS = 4
WLAT = 6
HALF = 6
RING = 4
N_VAR = RING * RING
N_TILE = 8
FF = 2048
PATCHES = WLAT * HALF
PAD = 40
SENT = 48
ROWS = 2 * LATENT * PAD
STATS = 128
MESH = pl.DeviceIdType.MESH
epsilon = 1e-05


def last_by_last(a, b):
    return lax.dot_general(a, b, (((1,), (1,)), ((), ())), preferred_element_type=F32)


def dot(a, b):
    return jnp.dot(a, b, preferred_element_type=F32)


def layer_norm(values, gain_row):
    average = jnp.mean(values, axis=-1, keepdims=True)
    centred = values - average
    spread = jnp.mean(centred * centred, axis=-1, keepdims=True)
    return centred * lax.rsqrt(spread + epsilon) * gain_row


def split(values, terms):
    parts = []
    for _ in range(terms):
        part = values.astype(BF16)
        parts.append(part)
        values = values - part.astype(F32)
    return parts


def gather_kernel(
    tokens, w_pq, w_pk, w_pv, w_po, lq_ref,
    out_ref,
    buf, pq, pk, pv, po,
    kp_scr, ex_scr, s_scr, v_scr, p_scr, px_scr, sc_scr, snum, rnum, sstat, rstat, att_scr,
    w_sem, tok_send, tok_recv, num_send, num_recv, stat_send, stat_recv,
):
    var = lax.axis_index("var")
    tile = lax.axis_index("tile")
    y, x = var // RING, var % RING
    west = lax.rem(tile + N_TILE - 1, N_TILE)
    east = lax.rem(tile + 1, N_TILE)

    barrier = pltpu.get_barrier_semaphore()
    for d in range(1, RING):
        for there in (y * RING + lax.rem(x + d, RING), lax.rem(y + d, RING) * RING + x):
            pl.semaphore_signal(
                barrier, inc=1, device_id={"var": there, "tile": tile}, device_id_type=MESH
            )
    for d in range(RING):
        there = y * RING + lax.rem(x + d, RING)
        pl.semaphore_signal(
            barrier, inc=1, device_id={"var": there, "tile": east}, device_id_type=MESH
        )
    pl.semaphore_wait(barrier, 3 * RING - 2)

    def slot_of(half, k):
        return lax.rem((y if half == 0 else x) + 1 + k, RING)

    def send_piece(half, k):
        slot = slot_of(half, k)
        mine = x if half == 0 else y
        lon = HALF if half == 0 else 0
        for d in (1, 3, 2, 0):
            other = lax.rem(mine + d, RING)
            if half == 0:
                band, there = slot * RING + other, y * RING + other
            else:
                band, there = other * RING + slot, other * RING + x
            first = WLAT * band + WLAT // 2
            second = lax.rem(WLAT * band + WLAT, WLAT * N_VAR)
            for part, row in ((0, first), (1, second)):
                src = tokens.at[pl.ds(row, WLAT // 2), pl.ds(lon, HALF)]
                dst = buf.at[half, slot, mine, pl.ds(part * (WLAT // 2), WLAT // 2)]
                if d == 0:
                    pltpu.make_async_copy(src, dst, tok_recv.at[half, slot]).start()
                else:
                    pltpu.make_async_remote_copy(
                        src_ref=src,
                        dst_ref=dst,
                        send_sem=tok_send.at[half, slot],
                        recv_sem=tok_recv.at[half, slot],
                        device_id={"var": there, "tile": tile},
                        device_id_type=MESH,
                    ).start()

    for k in range(2):
        for half in range(2):
            send_piece(half, k)

    weights = ((w_pq, pq), (w_pk, pk), (w_pv, pv), (w_po, po))
    loads = [pltpu.make_async_copy(src, dst, w_sem.at[i]) for i, (src, dst) in enumerate(weights)]
    for load in loads:
        load.start()

    row = lax.broadcasted_iota(jnp.int32, (STATS, LATENT * D), 0)
    col = lax.broadcasted_iota(jnp.int32, (STATS, LATENT * D), 1)
    ex_scr[...] = jnp.where(
        row == (col >> 9) * HEADS + ((col & (D - 1)) >> 5), 1.0, 0.0
    ).astype(BF16)
    loads[0].wait()
    queries = dot(lq_ref[...], pq[...])
    head_row = lax.broadcasted_iota(jnp.int32, (HEADS, D), 0)
    head_col = lax.broadcasted_iota(jnp.int32, (HEADS, D), 1) >> 5
    spread = jnp.concatenate(
        [jnp.where(head_row == head_col, queries[j : j + 1], 0.0) for j in range(LATENT)]
        + [jnp.zeros((STATS - LATENT * HEADS, D), F32)],
        axis=0,
    )
    loads[1].wait()
    probe = sum(last_by_last(part, pk[...]) for part in split(spread, 3))
    kp_scr[...] = (probe / math.sqrt(HD)).astype(BF16)
    loads[2].wait()

    def work_piece(half, k):
        slot = slot_of(half, k)
        index = half * RING + k
        pltpu.make_async_copy(buf.at[half, slot], buf.at[half, slot], tok_recv.at[half, slot]).wait()
        rows = buf[half, slot].reshape(RING * PATCHES * LEVS, D)
        s_scr[...] = last_by_last(rows, kp_scr[...])
        values = dot(rows, pv[...])
        for lanes in range(D // 128):
            v_scr[lanes] = values[:, lanes * 128 : (lanes + 1) * 128]
        maxima, totals = [], []
        for src in range(RING):
            scores = [
                s_scr[pl.ds(src * PATCHES * LEVS + t, PATCHES, stride=LEVS), :]
                for t in range(LEVS)
            ]
            top = functools.reduce(jnp.maximum, scores)
            total = jnp.zeros_like(top)
            for t in range(LEVS):
                weight = jnp.exp(scores[t] - top)
                total = total + weight
                p_scr[pl.ds((src * LEVS + t) * PAD, PATCHES), :] = weight
            maxima.append(top)
            totals.append(total)
        top = functools.reduce(jnp.maximum, maxima)
        total = jnp.zeros_like(top)
        for src in range(RING):
            scale = jnp.exp(maxima[src] - top)
            total = total + totals[src] * scale
            sc_scr[pl.ds(src * PAD, PATCHES), :] = scale
        lane = lax.broadcasted_iota(jnp.int32, (PATCHES, STATS), 1)
        sstat[index, 0:PATCHES, :] = jnp.where(
            lane < STATS // 2, top, pltpu.roll(total, STATS // 2, 1)
        )
        px_scr[0 : RING * LEVS * PAD] = dot(p_scr[...].astype(BF16), ex_scr[...])
        px_scr[RING * LEVS * PAD :] = sum(dot(part, ex_scr[...]) for part in split(sc_scr[...], 2))
        for lanes in range(D // 128):
            at = lanes * 128
            sums = [jnp.zeros((PATCHES, 128), F32) for _ in range(LATENT)]
            for src in range(RING):
                inner = [jnp.zeros((PATCHES, 128), F32) for _ in range(LATENT)]
                for t in range(LEVS):
                    value = v_scr[lanes, pl.ds(src * PATCHES * LEVS + t, PATCHES, stride=LEVS), :]
                    for j in range(LATENT):
                        inner[j] += value * px_scr[
                            pl.ds((src * LEVS + t) * PAD, PATCHES), j * D + at : j * D + at + 128
                        ]
                for j in range(LATENT):
                    sums[j] += inner[j] * px_scr[
                        pl.ds((RING * LEVS + src) * PAD, PATCHES), j * D + at : j * D + at + 128
                    ]
            for j in range(LATENT):
                snum[index, 0:PATCHES, j * D + at : j * D + at + 128] = sums[j].astype(BF16)
        mine = y if half == 0 else x
        there = slot * RING + x if half == 0 else y * RING + slot
        for src, dst, send, recv in (
            (snum, rnum, num_send, num_recv), (sstat, rstat, stat_send, stat_recv)
        ):
            if half == 0 and k == RING - 1:
                pltpu.make_async_copy(src.at[index], dst.at[half, mine], recv.at[half]).start()
            else:
                pltpu.make_async_remote_copy(
                    src_ref=src.at[index],
                    dst_ref=dst.at[half, mine],
                    send_sem=send.at[index],
                    recv_sem=recv.at[half],
                    device_id={"var": there, "tile": tile if half == 0 else west},
                    device_id_type=MESH,
                ).start()

    for k in range(RING):
        for half in range(2):
            work_piece(half, k)
            if k + 2 < RING:
                send_piece(half, k + 2)

    lane = lax.broadcasted_iota(jnp.int32, (PAD, STATS), 1)
    inside = lax.broadcasted_iota(jnp.int32, (PAD, STATS), 0) < PATCHES
    for half in range(2):
        pltpu.make_async_copy(rnum.at[half], rnum.at[half], num_recv.at[half]).wait()
        pltpu.make_async_copy(rstat.at[half], rstat.at[half], stat_recv.at[half]).wait()
        stats = [rstat[half, src] for src in range(RING)]
        top = functools.reduce(jnp.maximum, stats)
        scales = [jnp.exp(stat - top) for stat in stats]
        denominator = sum(
            pltpu.roll(stat, STATS // 2, 1) * scale for stat, scale in zip(stats, scales)
        )
        keep = (lane < LATENT * HEADS) & inside
        for src in range(RING):
            sc_scr[pl.ds(src * PAD, PAD), :] = jnp.where(keep, scales[src] / denominator, 0.0)
        px_scr[0 : RING * PAD] = sum(dot(part, ex_scr[...]) for part in split(sc_scr[...], 3))
        inside_wide = lax.broadcasted_iota(jnp.int32, (PAD, D), 0) < PATCHES
        for j in range(LATENT):
            share = sum(
                rnum[half, src, :, j * D : (j + 1) * D].astype(F32)[:PAD]
                * px_scr[pl.ds(src * PAD, PAD), j * D : (j + 1) * D]
                for src in range(RING)
            )
            att_scr[pl.ds((half * LATENT + j) * PAD, PAD), :] = jnp.where(inside_wide, share, 0.0)

    loads[3].wait()
    latent = dot(att_scr[...].astype(BF16), po[...])
    start = jnp.concatenate(
        [
            jnp.broadcast_to(lq_ref[j : j + 1, :].astype(F32), (PAD, D))
            for _ in range(2)
            for j in range(LATENT)
        ],
        axis=0,
    )
    out_ref[...] = (start + latent).astype(BF16)

    for half in range(2):
        for k in range(RING):
            slot = slot_of(half, k)
            sent = buf.at[half, slot, pl.ds(0, RING - 1)]
            pltpu.make_async_copy(sent, sent, tok_send.at[half, slot]).wait()
            if half == 1 or k < RING - 1:
                index = half * RING + k
                pltpu.make_async_copy(snum.at[index], snum.at[index], num_send.at[index]).wait()
                pltpu.make_async_copy(sstat.at[index], sstat.at[index], stat_send.at[index]).wait()


def window_kernel(
    latent_ref, gains_ref, w_sq, w_skv, w_so, w_up, w_down, out_ref,
    sq, skv, so, up, down, vt_scr, mix_scr, turn_scr, w_sem,
):
    weights = ((w_sq, sq), (w_skv, skv), (w_so, so), (w_up, up), (w_down, down))
    loads = [pltpu.make_async_copy(src, dst, w_sem.at[i]) for i, (src, dst) in enumerate(weights)]
    for load in loads:
        load.start()
    var = lax.axis_index("var")
    residual = latent_ref[...].astype(F32)
    normed = layer_norm(residual, gains_ref[0:1, :]).astype(BF16)
    loads[0].wait()
    queries = dot(normed, sq[...]).astype(BF16)
    loads[1].wait()
    keyvals = dot(normed, skv[...])
    keys = keyvals[:, :D]
    vt_scr[...] = jnp.transpose(keyvals[:, D:]).astype(BF16)

    def place(shape, axis):
        index = lax.broadcasted_iota(jnp.int32, shape, axis)
        for b in range(2 * LATENT - 1, 0, -1):
            index = jnp.where(index >= b * PAD, index - b * PAD, index)
        return index

    key_at = place((ROWS, ROWS), 0)
    query_at = place((ROWS, ROWS), 1)
    cut = WLAT // 2 * HALF
    apart = (key_at >= cut) != (query_at >= cut)
    excluded = (key_at >= PATCHES) | (apart & (var == N_VAR - 1))
    bias = jnp.where(excluded, -jnp.inf, 0.0)
    lane_head = lax.broadcasted_iota(jnp.int32, (ROWS, 256), 1) >> 5
    for h in range(HEADS):
        at = h // 8 * 256
        key_part = jnp.where(lane_head == h % 8, keys[:, at : at + 256], 0.0).astype(BF16)
        logits = last_by_last(key_part, queries[:, at : at + 256]) / math.sqrt(HD) + bias
        exponent = jnp.exp(logits - jnp.max(logits, axis=0, keepdims=True))
        probs = (exponent / jnp.sum(exponent, axis=0, keepdims=True)).astype(BF16)
        mix_scr[h * HD : (h + 1) * HD, :] = dot(vt_scr[h * HD : (h + 1) * HD, :], probs)
    mixed = jnp.transpose(mix_scr[...]).astype(BF16)
    loads[2].wait()
    residual = residual + dot(mixed, so[...])
    normed = layer_norm(residual, gains_ref[1:2, :]).astype(BF16)
    loads[3].wait()
    loads[4].wait()
    chunk = 512
    for c in range(0, FF, chunk):
        wide = dot(normed, up[:, c : c + chunk])
        hidden = (0.5 * wide * (1.0 + lax.erf(wide * math.sqrt(0.5)))).astype(BF16)
        residual = residual + dot(hidden, down[c : c + chunk, :])
    lanes = D // 128
    for b in range(2 * LATENT):
        half, j = b // LATENT, b % LATENT
        for l in range(lanes):
            turn_scr[l, pl.ds(half * PATCHES * 4 + j, PATCHES, stride=4), :] = residual[
                b * PAD : b * PAD + PATCHES, l * 128 : (l + 1) * 128
            ]
    for half in range(2):
        for r in range(WLAT):
            for l in range(lanes):
                rows = turn_scr[l, pl.ds((half * PATCHES + r * HALF) * 4, HALF * 4), :]
                rows = rows.reshape(HALF, 4, 128)[:, :LATENT]
                out_ref[r, half * HALF : (half + 1) * HALF, :, l * 128 : (l + 1) * 128] = rows.astype(BF16)


def body(
    tokens, latent_queries, perc_query, perc_key, perc_value, perc_out, norm_gains, swin_query,
    swin_keyvalue, swin_out, mlp_up, mlp_down,
):
    whole = pl.BlockSpec(memory_space=pltpu.HBM)
    near = pl.BlockSpec(memory_space=pltpu.VMEM)
    matrices = (perc_query, perc_key, perc_value, perc_out)
    pairs = RING * LEVS * PAD
    latent = pl.pallas_call(
        gather_kernel,
        out_shape=jax.ShapeDtypeStruct((ROWS, D), BF16),
        in_specs=[whole] * (1 + len(matrices)) + [near],
        out_specs=near,
        scratch_shapes=[
            pltpu.VMEM((2, RING, RING, WLAT, HALF, LEVS, D), BF16),
            *[pltpu.VMEM(m.shape, m.dtype) for m in matrices],
            pltpu.VMEM((STATS, D), BF16),
            pltpu.VMEM((STATS, LATENT * D), BF16),
            pltpu.VMEM((RING * PATCHES * LEVS, STATS), F32),
            pltpu.VMEM((D // 128, RING * PATCHES * LEVS, 128), F32),
            pltpu.VMEM((pairs, STATS), F32),
            pltpu.VMEM((pairs + RING * PAD, LATENT * D), F32),
            pltpu.VMEM((RING * PAD, STATS), F32),
            pltpu.VMEM((2 * RING, SENT, LATENT * D), BF16),
            pltpu.VMEM((2, RING, SENT, LATENT * D), BF16),
            pltpu.VMEM((2 * RING, PAD, STATS), F32),
            pltpu.VMEM((2, RING, PAD, STATS), F32),
            pltpu.VMEM((ROWS, D), F32),
            pltpu.SemaphoreType.DMA((len(matrices),)),
            pltpu.SemaphoreType.DMA((2, RING)),
            pltpu.SemaphoreType.DMA((2, RING)),
            pltpu.SemaphoreType.DMA((2 * RING,)),
            pltpu.SemaphoreType.DMA((2,)),
            pltpu.SemaphoreType.DMA((2 * RING,)),
            pltpu.SemaphoreType.DMA((2,)),
        ],
        compiler_params=pltpu.CompilerParams(
            collective_id=0, has_side_effects=True, vmem_limit_bytes=113 * 512 * 1024
        ),
        cost_estimate=pl.CostEstimate(
            flops=8_000_000_000, bytes_accessed=100_000_000, transcendentals=0
        ),
    )(tokens, *matrices, latent_queries)
    block = (swin_query, swin_keyvalue, swin_out, mlp_up, mlp_down)
    return pl.pallas_call(
        window_kernel,
        out_shape=jax.ShapeDtypeStruct((WLAT, 2 * HALF, LATENT, D), BF16),
        in_specs=[near, near] + [whole] * len(block),
        out_specs=near,
        scratch_shapes=[
            *[pltpu.VMEM(m.shape, m.dtype) for m in block],
            pltpu.VMEM((D, ROWS), BF16),
            pltpu.VMEM((D, ROWS), F32),
            pltpu.VMEM((D // 128, 2 * PATCHES * 4, 128), F32),
            pltpu.SemaphoreType.DMA((len(block),)),
        ],
        compiler_params=pltpu.CompilerParams(vmem_limit_bytes=40 * 1024 * 1024),
        cost_estimate=pl.CostEstimate(
            flops=2_000_000_000, bytes_accessed=7_000_000, transcendentals=0
        ),
    )(latent, norm_gains, *block)


def solution(mesh):
    placed = (P(None, "tile", "var", None), P(), P(), P(), P(), P(), P(), P(), P(), P(), P(), P())
    return jax.shard_map(
        body, mesh=mesh, in_specs=placed, out_specs=P("var", "tile", None, None), check_vma=False
    )
```

```python
import functools
import math

import jax
import jax.numpy as jnp
from jax import lax
from jax.experimental import pallas as pl
from jax.experimental.pallas import tpu as pltpu
from jax.sharding import PartitionSpec as P

F32 = jnp.float32
BF16 = jnp.bfloat16
D = 512
HEADS = 16
HD = 32
LATENT = 3
LEVS = 4
WLAT = 6
HALF = 6
RING = 4
N_VAR = RING * RING
N_TILE = 8
FF = 2048
PATCHES = WLAT * HALF
BOTH = 2 * PATCHES
GATHERED = 2 * BOTH * LEVS
PAD = 40
ROWS = 2 * LATENT * PAD
STATS = 128
MESH = pl.DeviceIdType.MESH
epsilon = 1e-05


def last_by_last(a, b):
    return lax.dot_general(a, b, (((1,), (1,)), ((), ())), preferred_element_type=F32)


def dot(a, b):
    return jnp.dot(a, b, preferred_element_type=F32)


def layer_norm(values, gain_row):
    average = jnp.mean(values, axis=-1, keepdims=True)
    centred = values - average
    spread = jnp.mean(centred * centred, axis=-1, keepdims=True)
    return centred * lax.rsqrt(spread + epsilon) * gain_row


def split(values, terms):
    parts = []
    for _ in range(terms):
        part = values.astype(BF16)
        parts.append(part)
        values = values - part.astype(F32)
    return parts


def gather_kernel(
    tokens, w_pq, w_pk, w_pv, w_po, lq_ref,
    out_ref,
    buf, pq, pk, pv, po,
    kp_scr, ex_scr, s_scr, v_scr, p_scr, px_scr, sc_scr, keep, kstat, snum, rnum, sstat, rstat,
    fnum, gnum, fstat, gstat, att_scr,
    w_sem, tok_send, tok_recv, num_send, num_recv, stat_send, stat_recv,
    far_send, far_recv, fst_send, fst_recv,
):
    var = lax.axis_index("var")
    tile = lax.axis_index("tile")
    y, x = var // RING, var % RING
    west = lax.rem(tile + N_TILE - 1, N_TILE)
    east = lax.rem(tile + 1, N_TILE)

    barrier = pltpu.get_barrier_semaphore()

    def greet(there, at):
        pl.semaphore_signal(
            barrier, inc=1, device_id={"var": there, "tile": at}, device_id_type=MESH
        )

    for d in (1, 3):
        greet(y * RING + lax.rem(x + d, RING), tile)
    for d in (1, 2, 3):
        greet(lax.rem(y + d, RING) * RING + x, tile)
    for d in range(RING):
        greet(y * RING + lax.rem(x + d, RING), east)
    pl.semaphore_wait(barrier, 9)

    def slot_of(half, k):
        return lax.rem((y if half == 0 else x) + 1 + k, RING)

    def partners(half, slot):
        a = x if half == 0 else y
        odd = lax.rem(slot, 2)
        one, three = a + 1 - 2 * lax.rem(a, 2), 3 - a
        return one + odd * (three - one), three + odd * (one - three)

    def along(half, place):
        return y * RING + place if half == 0 else place * RING + x

    def send_tokens(half, k):
        slot = slot_of(half, k)
        a = x if half == 0 else y
        lon = HALF if half == 0 else 0
        first, second = partners(half, slot)
        for which, src_at, owner in (
            (0, 1, first), (1, 1, lax.rem(a + 2, RING)), (0, 0, a), (1, 0, second)
        ):
            band = slot * RING + owner if half == 0 else owner * RING + slot
            upper = WLAT * band + WLAT // 2
            lower = lax.rem(WLAT * band + WLAT, WLAT * N_VAR)
            for part, row in ((0, upper), (1, lower)):
                src = tokens.at[pl.ds(row, WLAT // 2), pl.ds(lon, HALF)]
                dst = buf.at[half, slot, src_at, which, pl.ds(part * (WLAT // 2), WLAT // 2)]
                if src_at == 0:
                    pltpu.make_async_copy(src, dst, tok_recv.at[half, slot]).start()
                else:
                    pltpu.make_async_remote_copy(
                        src_ref=src,
                        dst_ref=dst,
                        send_sem=tok_send.at[half, slot],
                        recv_sem=tok_recv.at[half, slot],
                        device_id={"var": along(half, first), "tile": tile},
                        device_id_type=MESH,
                    ).start()

    for k in range(2):
        for half in (1, 0):
            send_tokens(half, k)

    weights = ((w_pq, pq), (w_pk, pk), (w_pv, pv), (w_po, po))
    loads = [pltpu.make_async_copy(src, dst, w_sem.at[i]) for i, (src, dst) in enumerate(weights)]
    for load in loads:
        load.start()

    row = lax.broadcasted_iota(jnp.int32, (STATS, LATENT * D), 0)
    col = lax.broadcasted_iota(jnp.int32, (STATS, LATENT * D), 1)
    ex_scr[...] = jnp.where(
        row == (col >> 9) * HEADS + ((col & (D - 1)) >> 5), 1.0, 0.0
    ).astype(BF16)
    loads[0].wait()
    queries = dot(lq_ref[...], pq[...])
    head_row = lax.broadcasted_iota(jnp.int32, (HEADS, D), 0)
    head_col = lax.broadcasted_iota(jnp.int32, (HEADS, D), 1) >> 5
    spread = jnp.concatenate(
        [jnp.where(head_row == head_col, queries[j : j + 1], 0.0) for j in range(LATENT)]
        + [jnp.zeros((STATS - LATENT * HEADS, D), F32)],
        axis=0,
    )
    loads[1].wait()
    probe = sum(last_by_last(part, pk[...]) for part in split(spread, 3))
    kp_scr[...] = (probe / math.sqrt(HD)).astype(BF16)
    loads[2].wait()

    lane = lax.broadcasted_iota(jnp.int32, (PAD, STATS), 1)
    lane_wide = lax.broadcasted_iota(jnp.int32, (BOTH, STATS), 1)

    def work(half, k):
        slot = slot_of(half, k)
        index = half * RING + k
        pltpu.make_async_copy(buf.at[half, slot], buf.at[half, slot], tok_recv.at[half, slot]).wait()
        rows = buf[half, slot].reshape(GATHERED, D)
        s_scr[...] = last_by_last(rows, kp_scr[...])
        values = dot(rows, pv[...])
        for lanes in range(D // 128):
            v_scr[lanes] = values[:, lanes * 128 : (lanes + 1) * 128]
        members = [pl.ds(src * BOTH * LEVS + t, BOTH, stride=LEVS) for src in range(2) for t in range(LEVS)]
        scores = [s_scr[member, :] for member in members]
        top = functools.reduce(jnp.maximum, scores)
        total = jnp.zeros_like(top)
        for n, score in enumerate(scores):
            weight = jnp.exp(score - top)
            total = total + weight
            p_scr[n * BOTH : (n + 1) * BOTH, :] = weight.astype(BF16)
        stats = jnp.where(lane_wide < STATS // 2, top, pltpu.roll(total, STATS // 2, 1))
        kstat[index, 0:PATCHES, :] = stats[:PATCHES]
        sstat[index, 0:PATCHES, :] = stats[PATCHES:]
        px_scr[...] = dot(p_scr[...], ex_scr[...])
        for lanes in range(D // 128):
            at = lanes * 128
            sums = [jnp.zeros((BOTH, 128), F32) for _ in range(LATENT)]
            for n, member in enumerate(members):
                value = v_scr[lanes, member, :]
                for j in range(LATENT):
                    sums[j] += value * px_scr[
                        n * BOTH : (n + 1) * BOTH, j * D + at : j * D + at + 128
                    ]
            for j in range(LATENT):
                keep[index, 0:PATCHES, j * D + at : j * D + at + 128] = sums[j][:PATCHES]
                snum[index, 0:PATCHES, j * D + at : j * D + at + 128] = sums[j][PATCHES:].astype(BF16)
        _, second = partners(half, slot)
        for src, dst, send, recv in (
            (snum, rnum, num_send, num_recv), (sstat, rstat, stat_send, stat_recv)
        ):
            pltpu.make_async_remote_copy(
                src_ref=src.at[index],
                dst_ref=dst.at[index],
                send_sem=send.at[index],
                recv_sem=recv.at[index],
                device_id={"var": along(half, second), "tile": tile},
                device_id_type=MESH,
            ).start()

    def merge(half, k):
        slot = slot_of(half, k)
        index = half * RING + k
        pltpu.make_async_copy(rstat.at[index], rstat.at[index], stat_recv.at[index]).wait()
        mine, theirs = kstat[index], rstat[index]
        top = jnp.maximum(mine, theirs)
        my_scale, their_scale = jnp.exp(mine - top), jnp.exp(theirs - top)
        total = (
            pltpu.roll(mine, STATS // 2, 1) * my_scale
            + pltpu.roll(theirs, STATS // 2, 1) * their_scale
        )
        fstat[index] = jnp.where(lane < STATS // 2, top, pltpu.roll(total, STATS // 2, 1))
        scales = jnp.concatenate([my_scale, their_scale], axis=0)
        scales = sum(dot(part, ex_scr[...]) for part in split(scales, 2))
        pltpu.make_async_copy(rnum.at[index], rnum.at[index], num_recv.at[index]).wait()
        fnum[index] = (
            keep[index] * scales[:PAD] + rnum[index].astype(F32) * scales[PAD:]
        ).astype(BF16)
        source = y if half == 0 else x
        there = slot * RING + x if half == 0 else y * RING + slot
        for src, dst, send, recv in (
            (fnum, gnum, far_send, far_recv), (fstat, gstat, fst_send, fst_recv)
        ):
            if half == 0 and k == RING - 1:
                pltpu.make_async_copy(src.at[index], dst.at[half, source], recv.at[half]).start()
            else:
                pltpu.make_async_remote_copy(
                    src_ref=src.at[index],
                    dst_ref=dst.at[half, source],
                    send_sem=send.at[index],
                    recv_sem=recv.at[half],
                    device_id={"var": there, "tile": tile if half == 0 else west},
                    device_id_type=MESH,
                ).start()

    for k in range(RING):
        for half in (1, 0):
            work(half, k)
            if k + 2 < RING:
                send_tokens(half, k + 2)
            if k > 0:
                merge(half, k - 1)
    for half in (1, 0):
        merge(half, RING - 1)

    inside = lax.broadcasted_iota(jnp.int32, (PAD, STATS), 0) < PATCHES
    for half in range(2):
        pltpu.make_async_copy(gnum.at[half], gnum.at[half], far_recv.at[half]).wait()
        pltpu.make_async_copy(gstat.at[half], gstat.at[half], fst_recv.at[half]).wait()
        stats = [gstat[half, src] for src in range(RING)]
        top = functools.reduce(jnp.maximum, stats)
        scales = [jnp.exp(stat - top) for stat in stats]
        denominator = sum(
            pltpu.roll(stat, STATS // 2, 1) * scale for stat, scale in zip(stats, scales)
        )
        valid = (lane < LATENT * HEADS) & inside
        for src in range(RING):
            sc_scr[pl.ds(src * PAD, PAD), :] = jnp.where(valid, scales[src] / denominator, 0.0)
        px_scr[0 : RING * PAD] = sum(dot(part, ex_scr[...]) for part in split(sc_scr[...], 3))
        inside_wide = lax.broadcasted_iota(jnp.int32, (PAD, D), 0) < PATCHES
        for j in range(LATENT):
            share = sum(
                gnum[half, src, :, j * D : (j + 1) * D].astype(F32)
                * px_scr[pl.ds(src * PAD, PAD), j * D : (j + 1) * D]
                for src in range(RING)
            )
            att_scr[pl.ds((half * LATENT + j) * PAD, PAD), :] = jnp.where(inside_wide, share, 0.0)

    loads[3].wait()
    latent = dot(att_scr[...].astype(BF16), po[...])
    start = jnp.concatenate(
        [
            jnp.broadcast_to(lq_ref[j : j + 1, :].astype(F32), (PAD, D))
            for _ in range(2)
            for j in range(LATENT)
        ],
        axis=0,
    )
    out_ref[...] = (start + latent).astype(BF16)

    for half in range(2):
        for k in range(RING):
            slot = slot_of(half, k)
            index = half * RING + k
            sent = buf.at[half, slot, 1]
            pltpu.make_async_copy(sent, sent, tok_send.at[half, slot]).wait()
            pltpu.make_async_copy(snum.at[index], snum.at[index], num_send.at[index]).wait()
            pltpu.make_async_copy(sstat.at[index], sstat.at[index], stat_send.at[index]).wait()
            if half == 1 or k < RING - 1:
                pltpu.make_async_copy(fnum.at[index], fnum.at[index], far_send.at[index]).wait()
                pltpu.make_async_copy(fstat.at[index], fstat.at[index], fst_send.at[index]).wait()


def window_kernel(
    latent_ref, gains_ref, w_sq, w_skv, w_so, w_up, w_down, out_ref,
    sq, skv, so, up, down, vt_scr, mix_scr, turn_scr, w_sem,
):
    weights = ((w_sq, sq), (w_skv, skv), (w_so, so), (w_up, up), (w_down, down))
    loads = [pltpu.make_async_copy(src, dst, w_sem.at[i]) for i, (src, dst) in enumerate(weights)]
    for load in loads:
        load.start()
    var = lax.axis_index("var")
    residual = latent_ref[...].astype(F32)
    normed = layer_norm(residual, gains_ref[0:1, :]).astype(BF16)
    loads[0].wait()
    queries = dot(normed, sq[...]).astype(BF16)
    loads[1].wait()
    keyvals = dot(normed, skv[...])
    keys = keyvals[:, :D]
    vt_scr[...] = jnp.transpose(keyvals[:, D:]).astype(BF16)

    def place(shape, axis):
        index = lax.broadcasted_iota(jnp.int32, shape, axis)
        for b in range(2 * LATENT - 1, 0, -1):
            index = jnp.where(index >= b * PAD, index - b * PAD, index)
        return index

    key_at = place((ROWS, ROWS), 0)
    query_at = place((ROWS, ROWS), 1)
    cut = WLAT // 2 * HALF
    apart = (key_at >= cut) != (query_at >= cut)
    excluded = (key_at >= PATCHES) | (apart & (var == N_VAR - 1))
    bias = jnp.where(excluded, -jnp.inf, 0.0)
    lane_head = lax.broadcasted_iota(jnp.int32, (ROWS, 256), 1) >> 5
    for h in range(HEADS):
        at = h // 8 * 256
        key_part = jnp.where(lane_head == h % 8, keys[:, at : at + 256], 0.0).astype(BF16)
        logits = last_by_last(key_part, queries[:, at : at + 256]) / math.sqrt(HD) + bias
        exponent = jnp.exp(logits - jnp.max(logits, axis=0, keepdims=True))
        probs = (exponent / jnp.sum(exponent, axis=0, keepdims=True)).astype(BF16)
        mix_scr[h * HD : (h + 1) * HD, :] = dot(vt_scr[h * HD : (h + 1) * HD, :], probs)
    mixed = jnp.transpose(mix_scr[...]).astype(BF16)
    loads[2].wait()
    residual = residual + dot(mixed, so[...])
    normed = layer_norm(residual, gains_ref[1:2, :]).astype(BF16)
    loads[3].wait()
    loads[4].wait()
    chunk = 512
    for c in range(0, FF, chunk):
        wide = dot(normed, up[:, c : c + chunk])
        hidden = (0.5 * wide * (1.0 + lax.erf(wide * math.sqrt(0.5)))).astype(BF16)
        residual = residual + dot(hidden, down[c : c + chunk, :])
    lanes = D // 128
    for b in range(2 * LATENT):
        half, j = b // LATENT, b % LATENT
        for l in range(lanes):
            turn_scr[l, pl.ds(half * PATCHES * 4 + j, PATCHES, stride=4), :] = residual[
                b * PAD : b * PAD + PATCHES, l * 128 : (l + 1) * 128
            ]
    for half in range(2):
        for r in range(WLAT):
            for l in range(lanes):
                rows = turn_scr[l, pl.ds((half * PATCHES + r * HALF) * 4, HALF * 4), :]
                rows = rows.reshape(HALF, 4, 128)[:, :LATENT]
                out_ref[r, half * HALF : (half + 1) * HALF, :, l * 128 : (l + 1) * 128] = rows.astype(BF16)


def body(
    tokens, latent_queries, perc_query, perc_key, perc_value, perc_out, norm_gains, swin_query,
    swin_keyvalue, swin_out, mlp_up, mlp_down,
):
    whole = pl.BlockSpec(memory_space=pltpu.HBM)
    near = pl.BlockSpec(memory_space=pltpu.VMEM)
    matrices = (perc_query, perc_key, perc_value, perc_out)
    pieces = 2 * RING
    latent = pl.pallas_call(
        gather_kernel,
        out_shape=jax.ShapeDtypeStruct((ROWS, D), BF16),
        in_specs=[whole] * (1 + len(matrices)) + [near],
        out_specs=near,
        scratch_shapes=[
            pltpu.VMEM((2, RING, 2, 2, WLAT, HALF, LEVS, D), BF16),
            *[pltpu.VMEM(m.shape, m.dtype) for m in matrices],
            pltpu.VMEM((STATS, D), BF16),
            pltpu.VMEM((STATS, LATENT * D), BF16),
            pltpu.VMEM((GATHERED, STATS), F32),
            pltpu.VMEM((D // 128, GATHERED, 128), F32),
            pltpu.VMEM((GATHERED, STATS), BF16),
            pltpu.VMEM((GATHERED, LATENT * D), F32),
            pltpu.VMEM((RING * PAD, STATS), F32),
            pltpu.VMEM((pieces, PAD, LATENT * D), F32),
            pltpu.VMEM((pieces, PAD, STATS), F32),
            pltpu.VMEM((pieces, PAD, LATENT * D), BF16),
            pltpu.VMEM((pieces, PAD, LATENT * D), BF16),
            pltpu.VMEM((pieces, PAD, STATS), F32),
            pltpu.VMEM((pieces, PAD, STATS), F32),
            pltpu.VMEM((pieces, PAD, LATENT * D), BF16),
            pltpu.VMEM((2, RING, PAD, LATENT * D), BF16),
            pltpu.VMEM((pieces, PAD, STATS), F32),
            pltpu.VMEM((2, RING, PAD, STATS), F32),
            pltpu.VMEM((ROWS, D), F32),
            pltpu.SemaphoreType.DMA((len(matrices),)),
            pltpu.SemaphoreType.DMA((2, RING)),
            pltpu.SemaphoreType.DMA((2, RING)),
            pltpu.SemaphoreType.DMA((pieces,)),
            pltpu.SemaphoreType.DMA((pieces,)),
            pltpu.SemaphoreType.DMA((pieces,)),
            pltpu.SemaphoreType.DMA((pieces,)),
            pltpu.SemaphoreType.DMA((pieces,)),
            pltpu.SemaphoreType.DMA((2,)),
            pltpu.SemaphoreType.DMA((pieces,)),
            pltpu.SemaphoreType.DMA((2,)),
        ],
        compiler_params=pltpu.CompilerParams(
            collective_id=0, has_side_effects=True, vmem_limit_bytes=113 * 512 * 1024
        ),
        cost_estimate=pl.CostEstimate(
            flops=8_000_000_000, bytes_accessed=100_000_000, transcendentals=0
        ),
    )(tokens, *matrices, latent_queries)
    block = (swin_query, swin_keyvalue, swin_out, mlp_up, mlp_down)
    return pl.pallas_call(
        window_kernel,
        out_shape=jax.ShapeDtypeStruct((WLAT, 2 * HALF, LATENT, D), BF16),
        in_specs=[near, near] + [whole] * len(block),
        out_specs=near,
        scratch_shapes=[
            *[pltpu.VMEM(m.shape, m.dtype) for m in block],
            pltpu.VMEM((D, ROWS), BF16),
            pltpu.VMEM((D, ROWS), F32),
            pltpu.VMEM((D // 128, 2 * PATCHES * 4, 128), F32),
            pltpu.SemaphoreType.DMA((len(block),)),
        ],
        compiler_params=pltpu.CompilerParams(vmem_limit_bytes=40 * 1024 * 1024),
        cost_estimate=pl.CostEstimate(
            flops=2_000_000_000, bytes_accessed=7_000_000, transcendentals=0
        ),
    )(latent, norm_gains, *block)


def solution(mesh):
    placed = (P(None, "tile", "var", None), P(), P(), P(), P(), P(), P(), P(), P(), P(), P(), P())
    return jax.shard_map(
        body, mesh=mesh, in_specs=placed, out_specs=P("var", "tile", None, None), check_vma=False
    )
```

```python
import functools
import math

import jax
import jax.numpy as jnp
from jax import lax
from jax.experimental import pallas as pl
from jax.experimental.pallas import tpu as pltpu
from jax.sharding import PartitionSpec as P

F32 = jnp.float32
BF16 = jnp.bfloat16
D = 512
HEADS = 16
HD = 32
LATENT = 3
LEVS = 4
WLAT = 6
HALF = 6
RING = 4
N_VAR = RING * RING
N_TILE = 8
FF = 2048
PATCHES = WLAT * HALF
BOTH = 2 * PATCHES
GATHERED = 2 * BOTH * LEVS
PAD = 40
ROWS = 2 * LATENT * PAD
STATS = 128
MESH = pl.DeviceIdType.MESH
epsilon = 1e-05


def last_by_last(a, b):
    return lax.dot_general(a, b, (((1,), (1,)), ((), ())), preferred_element_type=F32)


def dot(a, b):
    return jnp.dot(a, b, preferred_element_type=F32)


def layer_norm(values, gain_row):
    average = jnp.mean(values, axis=-1, keepdims=True)
    centred = values - average
    spread = jnp.mean(centred * centred, axis=-1, keepdims=True)
    return centred * lax.rsqrt(spread + epsilon) * gain_row


def split(values, terms):
    parts = []
    for _ in range(terms):
        part = values.astype(BF16)
        parts.append(part)
        values = values - part.astype(F32)
    return parts


def gather_kernel(
    tokens, w_pq, w_pk, w_pv, w_po, lq_ref,
    out_ref,
    buf, pq, pk, pv, po,
    kp_scr, ex_scr, s_scr, v_scr, p_scr, px_scr, sc_scr, keep, kstat, snum, rnum, sstat, rstat,
    fnum, gnum, fstat, gstat, att_scr,
    w_sem, own_sem, tok_send, tok_recv, num_send, num_recv, stat_send, stat_recv,
    far_send, far_recv, fst_send, fst_recv,
):
    var = lax.axis_index("var")
    tile = lax.axis_index("tile")
    y, x = var // RING, var % RING
    west = lax.rem(tile + N_TILE - 1, N_TILE)
    east = lax.rem(tile + 1, N_TILE)

    barrier = pltpu.get_barrier_semaphore()

    def greet(there, at):
        pl.semaphore_signal(
            barrier, inc=1, device_id={"var": there, "tile": at}, device_id_type=MESH
        )

    for d in (1, 3):
        greet(y * RING + lax.rem(x + d, RING), tile)
    for d in (1, 2, 3):
        greet(lax.rem(y + d, RING) * RING + x, tile)
    for d in range(RING):
        greet(y * RING + lax.rem(x + d, RING), east)

    def slot_of(half, k):
        return lax.rem((y if half == 0 else x) + 1 + k, RING)

    def partners(half, slot):
        a = x if half == 0 else y
        odd = lax.rem(slot, 2)
        one, three = a + 1 - 2 * lax.rem(a, 2), 3 - a
        return one + odd * (three - one), three + odd * (one - three)

    def along(half, place):
        return y * RING + place if half == 0 else place * RING + x

    def send_tokens(half, k, own=False):
        slot = slot_of(half, k)
        a = x if half == 0 else y
        lon = HALF if half == 0 else 0
        first, second = partners(half, slot)
        for which, owner in ((0, a), (1, second)) if own else ((0, first), (1, lax.rem(a + 2, RING))):
            src_at = 0 if own else 1
            band = slot * RING + owner if half == 0 else owner * RING + slot
            upper = WLAT * band + WLAT // 2
            lower = lax.rem(WLAT * band + WLAT, WLAT * N_VAR)
            for part, row in ((0, upper), (1, lower)):
                src = tokens.at[pl.ds(row, WLAT // 2), pl.ds(lon, HALF)]
                dst = buf.at[half, slot, src_at, which, pl.ds(part * (WLAT // 2), WLAT // 2)]
                if own:
                    pltpu.make_async_copy(src, dst, own_sem.at[half, slot]).start()
                else:
                    pltpu.make_async_remote_copy(
                        src_ref=src,
                        dst_ref=dst,
                        send_sem=tok_send.at[half, slot],
                        recv_sem=tok_recv.at[half, slot],
                        device_id={"var": along(half, first), "tile": tile},
                        device_id_type=MESH,
                    ).start()

    weights = ((w_pq, pq), (w_pk, pk), (w_pv, pv), (w_po, po))
    loads = [pltpu.make_async_copy(src, dst, w_sem.at[i]) for i, (src, dst) in enumerate(weights)]
    for load in loads:
        load.start()
    order = [(half, k) for k in range(RING) for half in (1, 0)]
    for half, k in order:
        send_tokens(half, k, own=True)
    pl.semaphore_wait(barrier, 9)
    for half, k in order[:4]:
        send_tokens(half, k)

    row = lax.broadcasted_iota(jnp.int32, (STATS, LATENT * D), 0)
    col = lax.broadcasted_iota(jnp.int32, (STATS, LATENT * D), 1)
    ex_scr[...] = jnp.where(
        row == (col >> 9) * HEADS + ((col & (D - 1)) >> 5), 1.0, 0.0
    ).astype(BF16)
    loads[0].wait()
    queries = dot(lq_ref[...], pq[...])
    head_row = lax.broadcasted_iota(jnp.int32, (HEADS, D), 0)
    head_col = lax.broadcasted_iota(jnp.int32, (HEADS, D), 1) >> 5
    spread = jnp.concatenate(
        [jnp.where(head_row == head_col, queries[j : j + 1], 0.0) for j in range(LATENT)]
        + [jnp.zeros((STATS - LATENT * HEADS, D), F32)],
        axis=0,
    )
    loads[1].wait()
    probe = sum(last_by_last(part, pk[...]) for part in split(spread, 3))
    kp_scr[...] = (probe / math.sqrt(HD)).astype(BF16)
    loads[2].wait()

    lane = lax.broadcasted_iota(jnp.int32, (PAD, STATS), 1)
    lane_wide = lax.broadcasted_iota(jnp.int32, (BOTH, STATS), 1)

    def products(half, k, src):
        index = half * RING + k
        rows = buf[half, slot_of(half, k), src].reshape(BOTH * LEVS, D)
        at = src * BOTH * LEVS
        s_scr[index, at : at + BOTH * LEVS, :] = last_by_last(rows, kp_scr[...])
        values = dot(rows, pv[...])
        for lanes in range(D // 128):
            v_scr[index, lanes, at : at + BOTH * LEVS, :] = values[:, lanes * 128 : (lanes + 1) * 128]

    def work(half, k):
        slot = slot_of(half, k)
        index = half * RING + k
        arrived = buf.at[half, slot, 1]
        pltpu.make_async_copy(arrived, arrived, tok_recv.at[half, slot]).wait()
        if k + 2 < RING:
            send_tokens(half, k + 2)
        products(half, k, 1)
        members = [
            pl.ds(src * BOTH * LEVS + t, BOTH, stride=LEVS)
            for src in range(2)
            for t in range(LEVS)
        ]
        scores = [s_scr[index, member, :] for member in members]
        top = functools.reduce(jnp.maximum, scores)
        total = jnp.zeros_like(top)
        for n, score in enumerate(scores):
            weight = jnp.exp(score - top)
            total = total + weight
            p_scr[n * BOTH : (n + 1) * BOTH, :] = weight.astype(BF16)
        stats = jnp.where(lane_wide < STATS // 2, top, pltpu.roll(total, STATS // 2, 1))
        kstat[index, 0:PATCHES, :] = stats[:PATCHES]
        sstat[index, 0:PATCHES, :] = stats[PATCHES:]
        for at in range(0, LATENT * D, 256):
            wide = dot(p_scr[...], ex_scr[:, at : at + 256])
            for side in range(2):
                lanes = (at % D) // 128 + side
                here = sum(
                    v_scr[index, lanes, member, :]
                    * wide[n * BOTH : (n + 1) * BOTH, side * 128 : (side + 1) * 128]
                    for n, member in enumerate(members)
                )
                columns = slice(at + side * 128, at + (side + 1) * 128)
                keep[index, 0:PATCHES, columns] = here[:PATCHES]
                snum[index, 0:PATCHES, columns] = here[PATCHES:].astype(BF16)
        _, second = partners(half, slot)
        for src, dst, send, recv in (
            (snum, rnum, num_send, num_recv), (sstat, rstat, stat_send, stat_recv)
        ):
            pltpu.make_async_remote_copy(
                src_ref=src.at[index],
                dst_ref=dst.at[index],
                send_sem=send.at[index],
                recv_sem=recv.at[index],
                device_id={"var": along(half, second), "tile": tile},
                device_id_type=MESH,
            ).start()

    def merge(half, k):
        slot = slot_of(half, k)
        index = half * RING + k
        pltpu.make_async_copy(rstat.at[index], rstat.at[index], stat_recv.at[index]).wait()
        mine, theirs = kstat[index], rstat[index]
        top = jnp.maximum(mine, theirs)
        my_scale, their_scale = jnp.exp(mine - top), jnp.exp(theirs - top)
        total = (
            pltpu.roll(mine, STATS // 2, 1) * my_scale
            + pltpu.roll(theirs, STATS // 2, 1) * their_scale
        )
        fstat[index] = jnp.where(lane < STATS // 2, top, pltpu.roll(total, STATS // 2, 1))
        scales = jnp.concatenate([my_scale, their_scale], axis=0)
        scales = sum(dot(part, ex_scr[...]) for part in split(scales, 2))
        pltpu.make_async_copy(rnum.at[index], rnum.at[index], num_recv.at[index]).wait()
        fnum[index] = (
            keep[index] * scales[:PAD] + rnum[index].astype(F32) * scales[PAD:]
        ).astype(BF16)
        source = y if half == 0 else x
        there = slot * RING + x if half == 0 else y * RING + slot
        for src, dst, send, recv in (
            (fnum, gnum, far_send, far_recv), (fstat, gstat, fst_send, fst_recv)
        ):
            if half == 0 and k == RING - 1:
                pltpu.make_async_copy(src.at[index], dst.at[half, source], recv.at[half]).start()
            else:
                pltpu.make_async_remote_copy(
                    src_ref=src.at[index],
                    dst_ref=dst.at[half, source],
                    send_sem=send.at[index],
                    recv_sem=recv.at[half],
                    device_id={"var": there, "tile": tile if half == 0 else west},
                    device_id_type=MESH,
                ).start()

    for half, k in order:
        own = buf.at[half, slot_of(half, k), 0]
        pltpu.make_async_copy(own, own, own_sem.at[half, slot_of(half, k)]).wait()
        products(half, k, 0)
    for half, k in order:
        work(half, k)
        if k > 0:
            merge(half, k - 1)
    for half in (1, 0):
        merge(half, RING - 1)

    inside = lax.broadcasted_iota(jnp.int32, (PAD, STATS), 0) < PATCHES
    for half in range(2):
        pltpu.make_async_copy(gnum.at[half], gnum.at[half], far_recv.at[half]).wait()
        pltpu.make_async_copy(gstat.at[half], gstat.at[half], fst_recv.at[half]).wait()
        stats = [gstat[half, src] for src in range(RING)]
        top = functools.reduce(jnp.maximum, stats)
        scales = [jnp.exp(stat - top) for stat in stats]
        denominator = sum(
            pltpu.roll(stat, STATS // 2, 1) * scale for stat, scale in zip(stats, scales)
        )
        valid = (lane < LATENT * HEADS) & inside
        for src in range(RING):
            sc_scr[pl.ds(src * PAD, PAD), :] = jnp.where(valid, scales[src] / denominator, 0.0)
        px_scr[0 : RING * PAD] = sum(dot(part, ex_scr[...]) for part in split(sc_scr[...], 3))
        inside_wide = lax.broadcasted_iota(jnp.int32, (PAD, D), 0) < PATCHES
        for j in range(LATENT):
            share = sum(
                gnum[half, src, :, j * D : (j + 1) * D].astype(F32)
                * px_scr[pl.ds(src * PAD, PAD), j * D : (j + 1) * D]
                for src in range(RING)
            )
            att_scr[pl.ds((half * LATENT + j) * PAD, PAD), :] = jnp.where(inside_wide, share, 0.0)

    loads[3].wait()
    latent = dot(att_scr[...].astype(BF16), po[...])
    start = jnp.concatenate(
        [
            jnp.broadcast_to(lq_ref[j : j + 1, :].astype(F32), (PAD, D))
            for _ in range(2)
            for j in range(LATENT)
        ],
        axis=0,
    )
    out_ref[...] = (start + latent).astype(BF16)

    for half in range(2):
        for k in range(RING):
            slot = slot_of(half, k)
            index = half * RING + k
            sent = buf.at[half, slot, 1]
            pltpu.make_async_copy(sent, sent, tok_send.at[half, slot]).wait()
            pltpu.make_async_copy(snum.at[index], snum.at[index], num_send.at[index]).wait()
            pltpu.make_async_copy(sstat.at[index], sstat.at[index], stat_send.at[index]).wait()
            if half == 1 or k < RING - 1:
                pltpu.make_async_copy(fnum.at[index], fnum.at[index], far_send.at[index]).wait()
                pltpu.make_async_copy(fstat.at[index], fstat.at[index], fst_send.at[index]).wait()


def window_kernel(
    latent_ref, gains_ref, w_sq, w_skv, w_so, w_up, w_down, out_ref,
    sq, skv, so, up, down, vt_scr, mix_scr, turn_scr, w_sem,
):
    weights = ((w_sq, sq), (w_skv, skv), (w_so, so), (w_up, up), (w_down, down))
    loads = [pltpu.make_async_copy(src, dst, w_sem.at[i]) for i, (src, dst) in enumerate(weights)]
    for load in loads:
        load.start()
    var = lax.axis_index("var")
    residual = latent_ref[...].astype(F32)
    normed = layer_norm(residual, gains_ref[0:1, :]).astype(BF16)
    loads[0].wait()
    queries = dot(normed, sq[...]).astype(BF16)
    loads[1].wait()
    keyvals = dot(normed, skv[...])
    keys = keyvals[:, :D]
    vt_scr[...] = jnp.transpose(keyvals[:, D:]).astype(BF16)

    def place(shape, axis):
        index = lax.broadcasted_iota(jnp.int32, shape, axis)
        for b in range(2 * LATENT - 1, 0, -1):
            index = jnp.where(index >= b * PAD, index - b * PAD, index)
        return index

    key_at = place((ROWS, ROWS), 0)
    query_at = place((ROWS, ROWS), 1)
    cut = WLAT // 2 * HALF
    apart = (key_at >= cut) != (query_at >= cut)
    excluded = (key_at >= PATCHES) | (apart & (var == N_VAR - 1))
    bias = jnp.where(excluded, -jnp.inf, 0.0)
    lane_head = lax.broadcasted_iota(jnp.int32, (ROWS, 256), 1) >> 5
    for h in range(HEADS):
        at = h // 8 * 256
        key_part = jnp.where(lane_head == h % 8, keys[:, at : at + 256], 0.0).astype(BF16)
        logits = last_by_last(key_part, queries[:, at : at + 256]) / math.sqrt(HD) + bias
        exponent = jnp.exp(logits - jnp.max(logits, axis=0, keepdims=True))
        probs = (exponent / jnp.sum(exponent, axis=0, keepdims=True)).astype(BF16)
        mix_scr[h * HD : (h + 1) * HD, :] = dot(vt_scr[h * HD : (h + 1) * HD, :], probs)
    mixed = jnp.transpose(mix_scr[...]).astype(BF16)
    loads[2].wait()
    residual = residual + dot(mixed, so[...])
    normed = layer_norm(residual, gains_ref[1:2, :]).astype(BF16)
    loads[3].wait()
    loads[4].wait()
    chunk = 512
    for c in range(0, FF, chunk):
        wide = dot(normed, up[:, c : c + chunk])
        hidden = (0.5 * wide * (1.0 + lax.erf(wide * math.sqrt(0.5)))).astype(BF16)
        residual = residual + dot(hidden, down[c : c + chunk, :])
    lanes = D // 128
    for b in range(2 * LATENT):
        half, j = b // LATENT, b % LATENT
        for l in range(lanes):
            turn_scr[l, pl.ds(half * PATCHES * 4 + j, PATCHES, stride=4), :] = residual[
                b * PAD : b * PAD + PATCHES, l * 128 : (l + 1) * 128
            ]
    for half in range(2):
        for r in range(WLAT):
            for l in range(lanes):
                rows = turn_scr[l, pl.ds((half * PATCHES + r * HALF) * 4, HALF * 4), :]
                rows = rows.reshape(HALF, 4, 128)[:, :LATENT]
                out_ref[r, half * HALF : (half + 1) * HALF, :, l * 128 : (l + 1) * 128] = rows.astype(BF16)


def body(
    tokens, latent_queries, perc_query, perc_key, perc_value, perc_out, norm_gains, swin_query,
    swin_keyvalue, swin_out, mlp_up, mlp_down,
):
    whole = pl.BlockSpec(memory_space=pltpu.HBM)
    near = pl.BlockSpec(memory_space=pltpu.VMEM)
    matrices = (perc_query, perc_key, perc_value, perc_out)
    pieces = 2 * RING
    latent = pl.pallas_call(
        gather_kernel,
        out_shape=jax.ShapeDtypeStruct((ROWS, D), BF16),
        in_specs=[whole] * (1 + len(matrices)) + [near],
        out_specs=near,
        scratch_shapes=[
            pltpu.VMEM((2, RING, 2, 2, WLAT, HALF, LEVS, D), BF16),
            *[pltpu.VMEM(m.shape, m.dtype) for m in matrices],
            pltpu.VMEM((STATS, D), BF16),
            pltpu.VMEM((STATS, LATENT * D), BF16),
            pltpu.VMEM((pieces, GATHERED, STATS), F32),
            pltpu.VMEM((pieces, D // 128, GATHERED, 128), F32),
            pltpu.VMEM((GATHERED, STATS), BF16),
            pltpu.VMEM((RING * PAD, LATENT * D), F32),
            pltpu.VMEM((RING * PAD, STATS), F32),
            pltpu.VMEM((pieces, PAD, LATENT * D), F32),
            pltpu.VMEM((pieces, PAD, STATS), F32),
            pltpu.VMEM((pieces, PAD, LATENT * D), BF16),
            pltpu.VMEM((pieces, PAD, LATENT * D), BF16),
            pltpu.VMEM((pieces, PAD, STATS), F32),
            pltpu.VMEM((pieces, PAD, STATS), F32),
            pltpu.VMEM((pieces, PAD, LATENT * D), BF16),
            pltpu.VMEM((2, RING, PAD, LATENT * D), BF16),
            pltpu.VMEM((pieces, PAD, STATS), F32),
            pltpu.VMEM((2, RING, PAD, STATS), F32),
            pltpu.VMEM((ROWS, D), F32),
            pltpu.SemaphoreType.DMA((len(matrices),)),
            pltpu.SemaphoreType.DMA((2, RING)),
            pltpu.SemaphoreType.DMA((2, RING)),
            pltpu.SemaphoreType.DMA((2, RING)),
            pltpu.SemaphoreType.DMA((pieces,)),
            pltpu.SemaphoreType.DMA((pieces,)),
            pltpu.SemaphoreType.DMA((pieces,)),
            pltpu.SemaphoreType.DMA((pieces,)),
            pltpu.SemaphoreType.DMA((pieces,)),
            pltpu.SemaphoreType.DMA((2,)),
            pltpu.SemaphoreType.DMA((pieces,)),
            pltpu.SemaphoreType.DMA((2,)),
        ],
        compiler_params=pltpu.CompilerParams(
            collective_id=0, has_side_effects=True, vmem_limit_bytes=113 * 512 * 1024
        ),
        cost_estimate=pl.CostEstimate(
            flops=8_000_000_000, bytes_accessed=100_000_000, transcendentals=0
        ),
    )(tokens, *matrices, latent_queries)
    block = (swin_query, swin_keyvalue, swin_out, mlp_up, mlp_down)
    return pl.pallas_call(
        window_kernel,
        out_shape=jax.ShapeDtypeStruct((WLAT, 2 * HALF, LATENT, D), BF16),
        in_specs=[near, near] + [whole] * len(block),
        out_specs=near,
        scratch_shapes=[
            *[pltpu.VMEM(m.shape, m.dtype) for m in block],
            pltpu.VMEM((D, ROWS), BF16),
            pltpu.VMEM((D, ROWS), F32),
            pltpu.VMEM((D // 128, 2 * PATCHES * 4, 128), F32),
            pltpu.SemaphoreType.DMA((len(block),)),
        ],
        compiler_params=pltpu.CompilerParams(vmem_limit_bytes=40 * 1024 * 1024),
        cost_estimate=pl.CostEstimate(
            flops=2_000_000_000, bytes_accessed=7_000_000, transcendentals=0
        ),
    )(latent, norm_gains, *block)


def solution(mesh):
    placed = (P(None, "tile", "var", None), P(), P(), P(), P(), P(), P(), P(), P(), P(), P(), P())
    return jax.shard_map(
        body, mesh=mesh, in_specs=placed, out_specs=P("var", "tile", None, None), check_vma=False
    )
```

```python
import functools
import math

import jax
import jax.numpy as jnp
from jax import lax
from jax.experimental import pallas as pl
from jax.experimental.pallas import tpu as pltpu
from jax.sharding import PartitionSpec as P

F32 = jnp.float32
BF16 = jnp.bfloat16
D = 512
HEADS = 16
HD = 32
LATENT = 3
LEVS = 4
WLAT = 6
HALF = 6
RING = 4
N_VAR = RING * RING
N_TILE = 8
FF = 2048
PATCHES = WLAT * HALF
BOTH = 2 * PATCHES
GATHERED = 2 * BOTH * LEVS
PAD = 40
ROWS = 2 * LATENT * PAD
STATS = 128
MESH = pl.DeviceIdType.MESH
epsilon = 1e-05


def last_by_last(a, b):
    return lax.dot_general(a, b, (((1,), (1,)), ((), ())), preferred_element_type=F32)


def dot(a, b):
    return jnp.dot(a, b, preferred_element_type=F32)


def layer_norm(values, gain_row):
    average = jnp.mean(values, axis=-1, keepdims=True)
    centred = values - average
    spread = jnp.mean(centred * centred, axis=-1, keepdims=True)
    return centred * lax.rsqrt(spread + epsilon) * gain_row


def gelu(x):
    size = jnp.abs(x)
    t = 1.0 / (1.0 + (0.3275911 * math.sqrt(0.5)) * size)
    tail = 1.061405429
    for term in (-1.453152027, 1.421413741, -0.284496736, 0.254829592):
        tail = tail * t + term
    tail = tail * t * jnp.exp2(x * x * (-0.5 * math.log2(math.e)))
    return jnp.maximum(x, 0.0) - 0.5 * size * tail


def split(values, terms):
    parts = []
    for _ in range(terms):
        part = values.astype(BF16)
        parts.append(part)
        values = values - part.astype(F32)
    return parts


def gather_kernel(
    tokens, w_pq, w_pk, w_pv, w_po, lq_ref,
    out_ref,
    buf, pq, pk, pv, po,
    kp_scr, ex_scr, s_scr, v_scr, s_nat, v_nat, p_scr, px_scr, sc_scr, keep, kstat, snum, rnum, sstat, rstat,
    fnum, gnum, fstat, gstat, att_scr,
    w_sem, own_sem, tok_send, tok_recv, num_send, num_recv, stat_send, stat_recv,
    far_send, far_recv, fst_send, fst_recv,
):
    var = lax.axis_index("var")
    tile = lax.axis_index("tile")
    y, x = var // RING, var % RING
    west = lax.rem(tile + N_TILE - 1, N_TILE)
    east = lax.rem(tile + 1, N_TILE)

    barrier = pltpu.get_barrier_semaphore()

    def greet(there, at):
        pl.semaphore_signal(
            barrier, inc=1, device_id={"var": there, "tile": at}, device_id_type=MESH
        )

    for d in (1, 3):
        greet(y * RING + lax.rem(x + d, RING), tile)
    for d in (1, 2, 3):
        greet(lax.rem(y + d, RING) * RING + x, tile)
    for d in range(RING):
        greet(y * RING + lax.rem(x + d, RING), east)

    def slot_of(half, k):
        return lax.rem((y if half == 0 else x) + 1 + k, RING)

    def partners(half, slot):
        a = x if half == 0 else y
        odd = lax.rem(slot, 2)
        one, three = a + 1 - 2 * lax.rem(a, 2), 3 - a
        return one + odd * (three - one), three + odd * (one - three)

    def along(half, place):
        return y * RING + place if half == 0 else place * RING + x

    def send_tokens(half, k, own=False):
        slot = slot_of(half, k)
        a = x if half == 0 else y
        lon = HALF if half == 0 else 0
        first, second = partners(half, slot)
        for which, owner in ((0, a), (1, second)) if own else ((0, first), (1, lax.rem(a + 2, RING))):
            src_at = 0 if own else 1
            band = slot * RING + owner if half == 0 else owner * RING + slot
            upper = WLAT * band + WLAT // 2
            lower = lax.rem(WLAT * band + WLAT, WLAT * N_VAR)
            for part, row in ((0, upper), (1, lower)):
                src = tokens.at[pl.ds(row, WLAT // 2), pl.ds(lon, HALF)]
                dst = buf.at[half, slot, src_at, which, pl.ds(part * (WLAT // 2), WLAT // 2)]
                if own:
                    pltpu.make_async_copy(src, dst, own_sem.at[half, slot]).start()
                else:
                    pltpu.make_async_remote_copy(
                        src_ref=src,
                        dst_ref=dst,
                        send_sem=tok_send.at[half, slot],
                        recv_sem=tok_recv.at[half, slot],
                        device_id={"var": along(half, first), "tile": tile},
                        device_id_type=MESH,
                    ).start()

    weights = ((w_pq, pq), (w_pk, pk), (w_pv, pv), (w_po, po))
    loads = [pltpu.make_async_copy(src, dst, w_sem.at[i]) for i, (src, dst) in enumerate(weights)]
    for load in loads:
        load.start()
    order = [(half, k) for k in range(RING) for half in (1, 0)]
    for half, k in order:
        send_tokens(half, k, own=True)
    pl.semaphore_wait(barrier, 9)
    for half, k in order[:4]:
        send_tokens(half, k)

    row = lax.broadcasted_iota(jnp.int32, (STATS, LATENT * D), 0)
    col = lax.broadcasted_iota(jnp.int32, (STATS, LATENT * D), 1)
    ex_scr[...] = jnp.where(
        row == (col >> 9) * HEADS + ((col & (D - 1)) >> 5), 1.0, 0.0
    ).astype(BF16)
    loads[0].wait()
    queries = dot(lq_ref[...], pq[...])
    head_row = lax.broadcasted_iota(jnp.int32, (HEADS, D), 0)
    head_col = lax.broadcasted_iota(jnp.int32, (HEADS, D), 1) >> 5
    spread = jnp.concatenate(
        [jnp.where(head_row == head_col, queries[j : j + 1], 0.0) for j in range(LATENT)]
        + [jnp.zeros((STATS - LATENT * HEADS, D), F32)],
        axis=0,
    )
    loads[1].wait()
    probe = sum(last_by_last(part, pk[...]) for part in split(spread, 3))
    kp_scr[...] = (probe / math.sqrt(HD)).astype(BF16)
    loads[2].wait()

    lane = lax.broadcasted_iota(jnp.int32, (PAD, STATS), 1)
    lane_wide = lax.broadcasted_iota(jnp.int32, (BOTH, STATS), 1)

    def products(half, k, src):
        index = half * RING + k
        rows = buf[half, slot_of(half, k), src].reshape(BOTH * LEVS, D)
        s_nat[...] = last_by_last(rows, kp_scr[...])
        values = dot(rows, pv[...])
        for lanes in range(D // 128):
            v_nat[lanes] = values[:, lanes * 128 : (lanes + 1) * 128]
        for t in range(LEVS):
            member = pl.ds(t, BOTH, stride=LEVS)
            at = (src * LEVS + t) * BOTH
            s_scr[index, at : at + BOTH, :] = s_nat[member, :]
            for lanes in range(D // 128):
                v_scr[index, at : at + BOTH, lanes * 128 : (lanes + 1) * 128] = v_nat[lanes, member, :]

    def work(half, k):
        slot = slot_of(half, k)
        index = half * RING + k
        arrived = buf.at[half, slot, 1]
        pltpu.make_async_copy(arrived, arrived, tok_recv.at[half, slot]).wait()
        if k + 2 < RING:
            send_tokens(half, k + 2)
        products(half, k, 1)
        members = [slice(n * BOTH, (n + 1) * BOTH) for n in range(2 * LEVS)]
        scores = [s_scr[index, member, :] for member in members]
        top = functools.reduce(jnp.maximum, scores)
        total = jnp.zeros_like(top)
        for n, score in enumerate(scores):
            weight = jnp.exp(score - top)
            total = total + weight
            p_scr[n * BOTH : (n + 1) * BOTH, :] = weight.astype(BF16)
        stats = jnp.where(lane_wide < STATS // 2, top, pltpu.roll(total, STATS // 2, 1))
        kstat[index, 0:PATCHES, :] = stats[:PATCHES]
        sstat[index, 0:PATCHES, :] = stats[PATCHES:]
        for at in range(0, LATENT * D, 256):
            wide = dot(p_scr[...], ex_scr[:, at : at + 256])
            columns = slice(at, at + 256)
            lanes = slice(at % D, at % D + 256)
            here = sum(v_scr[index, member, lanes] * wide[member] for member in members)
            keep[index, 0:PATCHES, columns] = here[:PATCHES]
            snum[index, 0:PATCHES, columns] = here[PATCHES:].astype(BF16)
        _, second = partners(half, slot)
        for src, dst, send, recv in (
            (snum, rnum, num_send, num_recv), (sstat, rstat, stat_send, stat_recv)
        ):
            pltpu.make_async_remote_copy(
                src_ref=src.at[index],
                dst_ref=dst.at[index],
                send_sem=send.at[index],
                recv_sem=recv.at[index],
                device_id={"var": along(half, second), "tile": tile},
                device_id_type=MESH,
            ).start()

    def merge(half, k):
        slot = slot_of(half, k)
        index = half * RING + k
        pltpu.make_async_copy(rstat.at[index], rstat.at[index], stat_recv.at[index]).wait()
        mine, theirs = kstat[index], rstat[index]
        top = jnp.maximum(mine, theirs)
        my_scale, their_scale = jnp.exp(mine - top), jnp.exp(theirs - top)
        total = (
            pltpu.roll(mine, STATS // 2, 1) * my_scale
            + pltpu.roll(theirs, STATS // 2, 1) * their_scale
        )
        fstat[index] = jnp.where(lane < STATS // 2, top, pltpu.roll(total, STATS // 2, 1))
        scales = jnp.concatenate([my_scale, their_scale], axis=0)
        scales = sum(dot(part, ex_scr[...]) for part in split(scales, 2))
        pltpu.make_async_copy(rnum.at[index], rnum.at[index], num_recv.at[index]).wait()
        fnum[index] = (
            keep[index] * scales[:PAD] + rnum[index].astype(F32) * scales[PAD:]
        ).astype(BF16)
        source = y if half == 0 else x
        there = slot * RING + x if half == 0 else y * RING + slot
        for src, dst, send, recv in (
            (fnum, gnum, far_send, far_recv), (fstat, gstat, fst_send, fst_recv)
        ):
            if half == 0 and k == RING - 1:
                pltpu.make_async_copy(src.at[index], dst.at[half, source], recv.at[half]).start()
            else:
                pltpu.make_async_remote_copy(
                    src_ref=src.at[index],
                    dst_ref=dst.at[half, source],
                    send_sem=send.at[index],
                    recv_sem=recv.at[half],
                    device_id={"var": there, "tile": tile if half == 0 else west},
                    device_id_type=MESH,
                ).start()

    for half, k in order:
        own = buf.at[half, slot_of(half, k), 0]
        pltpu.make_async_copy(own, own, own_sem.at[half, slot_of(half, k)]).wait()
        products(half, k, 0)
    for half, k in order:
        work(half, k)
        if k > 0:
            merge(half, k - 1)
    for half in (1, 0):
        merge(half, RING - 1)

    inside = lax.broadcasted_iota(jnp.int32, (PAD, STATS), 0) < PATCHES
    for half in range(2):
        pltpu.make_async_copy(gnum.at[half], gnum.at[half], far_recv.at[half]).wait()
        pltpu.make_async_copy(gstat.at[half], gstat.at[half], fst_recv.at[half]).wait()
        stats = [gstat[half, src] for src in range(RING)]
        top = functools.reduce(jnp.maximum, stats)
        scales = [jnp.exp(stat - top) for stat in stats]
        denominator = sum(
            pltpu.roll(stat, STATS // 2, 1) * scale for stat, scale in zip(stats, scales)
        )
        valid = (lane < LATENT * HEADS) & inside
        for src in range(RING):
            sc_scr[pl.ds(src * PAD, PAD), :] = jnp.where(valid, scales[src] / denominator, 0.0)
        px_scr[0 : RING * PAD] = sum(dot(part, ex_scr[...]) for part in split(sc_scr[...], 3))
        inside_wide = lax.broadcasted_iota(jnp.int32, (PAD, D), 0) < PATCHES
        for j in range(LATENT):
            share = sum(
                gnum[half, src, :, j * D : (j + 1) * D].astype(F32)
                * px_scr[pl.ds(src * PAD, PAD), j * D : (j + 1) * D]
                for src in range(RING)
            )
            att_scr[pl.ds((half * LATENT + j) * PAD, PAD), :] = jnp.where(inside_wide, share, 0.0)

    loads[3].wait()
    latent = dot(att_scr[...].astype(BF16), po[...])
    start = jnp.concatenate(
        [
            jnp.broadcast_to(lq_ref[j : j + 1, :].astype(F32), (PAD, D))
            for _ in range(2)
            for j in range(LATENT)
        ],
        axis=0,
    )
    out_ref[...] = (start + latent).astype(BF16)

    for half in range(2):
        for k in range(RING):
            slot = slot_of(half, k)
            index = half * RING + k
            sent = buf.at[half, slot, 1]
            pltpu.make_async_copy(sent, sent, tok_send.at[half, slot]).wait()
            pltpu.make_async_copy(snum.at[index], snum.at[index], num_send.at[index]).wait()
            pltpu.make_async_copy(sstat.at[index], sstat.at[index], stat_send.at[index]).wait()
            if half == 1 or k < RING - 1:
                pltpu.make_async_copy(fnum.at[index], fnum.at[index], far_send.at[index]).wait()
                pltpu.make_async_copy(fstat.at[index], fstat.at[index], fst_send.at[index]).wait()


def window_kernel(
    w_latent, gains_ref, w_sq, w_skv, w_so, w_up, w_down, out_ref,
    latent_ref, sq, skv, so, up, down, vt_scr, mix_scr, turn_scr, w_sem,
):
    weights = (
        (w_latent, latent_ref), (w_sq, sq), (w_skv, skv), (w_so, so), (w_up, up), (w_down, down)
    )
    first, *loads = [
        pltpu.make_async_copy(src, dst, w_sem.at[i]) for i, (src, dst) in enumerate(weights)
    ]
    for load in (first, *loads):
        load.start()
    first.wait()
    var = lax.axis_index("var")
    residual = latent_ref[...].astype(F32)
    normed = layer_norm(residual, gains_ref[0:1, :]).astype(BF16)
    loads[0].wait()
    queries = dot(normed, sq[...]).astype(BF16)
    loads[1].wait()
    keyvals = dot(normed, skv[...])
    keys = keyvals[:, :D]
    vt_scr[...] = jnp.transpose(keyvals[:, D:]).astype(BF16)

    def place(shape, axis):
        index = lax.broadcasted_iota(jnp.int32, shape, axis)
        for b in range(2 * LATENT - 1, 0, -1):
            index = jnp.where(index >= b * PAD, index - b * PAD, index)
        return index

    key_at = place((ROWS, ROWS), 0)
    query_at = place((ROWS, ROWS), 1)
    cut = WLAT // 2 * HALF
    apart = (key_at >= cut) != (query_at >= cut)
    excluded = (key_at >= PATCHES) | (apart & (var == N_VAR - 1))
    bias = jnp.where(excluded, -jnp.inf, 0.0)
    lane_head = lax.broadcasted_iota(jnp.int32, (ROWS, 256), 1) >> 5
    for h in range(HEADS):
        at = h // 8 * 256
        key_part = jnp.where(lane_head == h % 8, keys[:, at : at + 256], 0.0).astype(BF16)
        logits = last_by_last(key_part, queries[:, at : at + 256]) + bias
        top = jnp.max(logits, axis=0, keepdims=True)
        exponent = jnp.exp2((logits - top) * (math.log2(math.e) / math.sqrt(HD)))
        probs = (exponent * (1.0 / jnp.sum(exponent, axis=0, keepdims=True))).astype(BF16)
        mix_scr[h * HD : (h + 1) * HD, :] = dot(vt_scr[h * HD : (h + 1) * HD, :], probs)
    mixed = jnp.transpose(mix_scr[...]).astype(BF16)
    loads[2].wait()
    residual = residual + dot(mixed, so[...])
    normed = layer_norm(residual, gains_ref[1:2, :]).astype(BF16)
    loads[3].wait()
    loads[4].wait()
    chunk = 512
    for c in range(0, FF, chunk):
        wide = dot(normed, up[:, c : c + chunk])
        hidden = gelu(wide).astype(BF16)
        residual = residual + dot(hidden, down[c : c + chunk, :])
    lanes = D // 128
    for b in range(2 * LATENT):
        half, j = b // LATENT, b % LATENT
        for l in range(lanes):
            turn_scr[l, pl.ds(half * PATCHES * 4 + j, PATCHES, stride=4), :] = residual[
                b * PAD : b * PAD + PATCHES, l * 128 : (l + 1) * 128
            ]
    for half in range(2):
        for r in range(WLAT):
            for l in range(lanes):
                rows = turn_scr[l, pl.ds((half * PATCHES + r * HALF) * 4, HALF * 4), :]
                rows = rows.reshape(HALF, 4, 128)[:, :LATENT]
                out_ref[r, half * HALF : (half + 1) * HALF, :, l * 128 : (l + 1) * 128] = rows.astype(BF16)


def body(
    tokens, latent_queries, perc_query, perc_key, perc_value, perc_out, norm_gains, swin_query,
    swin_keyvalue, swin_out, mlp_up, mlp_down,
):
    whole = pl.BlockSpec(memory_space=pltpu.HBM)
    near = pl.BlockSpec(memory_space=pltpu.VMEM)
    matrices = (perc_query, perc_key, perc_value, perc_out)
    pieces = 2 * RING
    latent = pl.pallas_call(
        gather_kernel,
        out_shape=jax.ShapeDtypeStruct((ROWS, D), BF16),
        in_specs=[whole] * (1 + len(matrices)) + [near],
        out_specs=near,
        scratch_shapes=[
            pltpu.VMEM((2, RING, 2, 2, WLAT, HALF, LEVS, D), BF16),
            *[pltpu.VMEM(m.shape, m.dtype) for m in matrices],
            pltpu.VMEM((STATS, D), BF16),
            pltpu.VMEM((STATS, LATENT * D), BF16),
            pltpu.VMEM((pieces, GATHERED, STATS), F32),
            pltpu.VMEM((pieces, GATHERED, D), F32),
            pltpu.VMEM((BOTH * LEVS, STATS), F32),
            pltpu.VMEM((D // 128, BOTH * LEVS, 128), F32),
            pltpu.VMEM((GATHERED, STATS), BF16),
            pltpu.VMEM((RING * PAD, LATENT * D), F32),
            pltpu.VMEM((RING * PAD, STATS), F32),
            pltpu.VMEM((pieces, PAD, LATENT * D), F32),
            pltpu.VMEM((pieces, PAD, STATS), F32),
            pltpu.VMEM((pieces, PAD, LATENT * D), BF16),
            pltpu.VMEM((pieces, PAD, LATENT * D), BF16),
            pltpu.VMEM((pieces, PAD, STATS), F32),
            pltpu.VMEM((pieces, PAD, STATS), F32),
            pltpu.VMEM((pieces, PAD, LATENT * D), BF16),
            pltpu.VMEM((2, RING, PAD, LATENT * D), BF16),
            pltpu.VMEM((pieces, PAD, STATS), F32),
            pltpu.VMEM((2, RING, PAD, STATS), F32),
            pltpu.VMEM((ROWS, D), F32),
            pltpu.SemaphoreType.DMA((len(matrices),)),
            pltpu.SemaphoreType.DMA((2, RING)),
            pltpu.SemaphoreType.DMA((2, RING)),
            pltpu.SemaphoreType.DMA((2, RING)),
            pltpu.SemaphoreType.DMA((pieces,)),
            pltpu.SemaphoreType.DMA((pieces,)),
            pltpu.SemaphoreType.DMA((pieces,)),
            pltpu.SemaphoreType.DMA((pieces,)),
            pltpu.SemaphoreType.DMA((pieces,)),
            pltpu.SemaphoreType.DMA((2,)),
            pltpu.SemaphoreType.DMA((pieces,)),
            pltpu.SemaphoreType.DMA((2,)),
        ],
        compiler_params=pltpu.CompilerParams(
            collective_id=0, has_side_effects=True, vmem_limit_bytes=113 * 512 * 1024
        ),
        cost_estimate=pl.CostEstimate(
            flops=8_000_000_000, bytes_accessed=100_000_000, transcendentals=0
        ),
    )(tokens, *matrices, latent_queries)
    block = (swin_query, swin_keyvalue, swin_out, mlp_up, mlp_down)
    return pl.pallas_call(
        window_kernel,
        out_shape=jax.ShapeDtypeStruct((WLAT, 2 * HALF, LATENT, D), BF16),
        in_specs=[whole, near] + [whole] * len(block),
        out_specs=near,
        scratch_shapes=[
            pltpu.VMEM((ROWS, D), BF16),
            *[pltpu.VMEM(m.shape, m.dtype) for m in block],
            pltpu.VMEM((D, ROWS), BF16),
            pltpu.VMEM((D, ROWS), F32),
            pltpu.VMEM((D // 128, 2 * PATCHES * 4, 128), F32),
            pltpu.SemaphoreType.DMA((1 + len(block),)),
        ],
        compiler_params=pltpu.CompilerParams(vmem_limit_bytes=40 * 1024 * 1024),
        cost_estimate=pl.CostEstimate(
            flops=2_000_000_000, bytes_accessed=7_000_000, transcendentals=0
        ),
    )(latent, norm_gains, *block)


def solution(mesh):
    placed = (P(None, "tile", "var", None), P(), P(), P(), P(), P(), P(), P(), P(), P(), P(), P())
    return jax.shard_map(
        body, mesh=mesh, in_specs=placed, out_specs=P("var", "tile", None, None), check_vma=False
    )
```

```python
import functools
import math

import jax
import jax.numpy as jnp
from jax import lax
from jax.experimental import pallas as pl
from jax.experimental.pallas import tpu as pltpu
from jax.sharding import PartitionSpec as P

F32 = jnp.float32
BF16 = jnp.bfloat16
D = 512
HEADS = 16
HD = 32
LATENT = 3
LEVS = 4
WLAT = 6
HALF = 6
RING = 4
N_VAR = RING * RING
N_TILE = 8
FF = 2048
PATCHES = WLAT * HALF
BOTH = 2 * PATCHES
GATHERED = 2 * BOTH * LEVS
PAD = 40
ROWS = 2 * LATENT * PAD
STATS = 128
MESH = pl.DeviceIdType.MESH
epsilon = 1e-05


def last_by_last(a, b):
    return lax.dot_general(a, b, (((1,), (1,)), ((), ())), preferred_element_type=F32)


def dot(a, b):
    return jnp.dot(a, b, preferred_element_type=F32)


def layer_norm(values, gain_row):
    average = jnp.mean(values, axis=-1, keepdims=True)
    centred = values - average
    spread = jnp.mean(centred * centred, axis=-1, keepdims=True)
    return centred * lax.rsqrt(spread + epsilon) * gain_row


def split(values, terms):
    parts = []
    for _ in range(terms):
        part = values.astype(BF16)
        parts.append(part)
        values = values - part.astype(F32)
    return parts


def gather_kernel(
    tokens, w_pq, w_pk, w_pv, w_po, lq_ref,
    out_ref,
    buf, pq, pk, pv, po,
    kp_scr, ex_scr, s_scr, v_scr, p_scr, px_scr, sc_scr, keep, kstat, snum, rnum, sstat, rstat,
    fnum, gnum, fstat, gstat, att_scr,
    w_sem, own_sem, tok_send, tok_recv, num_send, num_recv, stat_send, stat_recv,
    far_send, far_recv, fst_send, fst_recv,
):
    var = lax.axis_index("var")
    tile = lax.axis_index("tile")
    y, x = var // RING, var % RING
    west = lax.rem(tile + N_TILE - 1, N_TILE)
    east = lax.rem(tile + 1, N_TILE)

    barrier = pltpu.get_barrier_semaphore()

    def greet(there, at):
        pl.semaphore_signal(
            barrier, inc=1, device_id={"var": there, "tile": at}, device_id_type=MESH
        )

    for d in (1, 3):
        greet(y * RING + lax.rem(x + d, RING), tile)
    for d in (1, 2, 3):
        greet(lax.rem(y + d, RING) * RING + x, tile)
    for d in range(RING):
        greet(y * RING + lax.rem(x + d, RING), east)

    def slot_of(half, k):
        return lax.rem((y if half == 0 else x) + 1 + k, RING)

    def partners(half, slot):
        a = x if half == 0 else y
        odd = lax.rem(slot, 2)
        one, three = a + 1 - 2 * lax.rem(a, 2), 3 - a
        return one + odd * (three - one), three + odd * (one - three)

    def along(half, place):
        return y * RING + place if half == 0 else place * RING + x

    def send_tokens(half, k, own=False):
        slot = slot_of(half, k)
        a = x if half == 0 else y
        lon = HALF if half == 0 else 0
        first, second = partners(half, slot)
        for which, owner in ((0, a), (1, second)) if own else ((0, first), (1, lax.rem(a + 2, RING))):
            src_at = 0 if own else 1
            band = slot * RING + owner if half == 0 else owner * RING + slot
            upper = WLAT * band + WLAT // 2
            lower = lax.rem(WLAT * band + WLAT, WLAT * N_VAR)
            for part, row in ((0, upper), (1, lower)):
                src = tokens.at[pl.ds(row, WLAT // 2), pl.ds(lon, HALF)]
                dst = buf.at[half, slot, src_at, which, pl.ds(part * (WLAT // 2), WLAT // 2)]
                if own:
                    pltpu.make_async_copy(src, dst, own_sem.at[half, slot]).start()
                else:
                    pltpu.make_async_remote_copy(
                        src_ref=src,
                        dst_ref=dst,
                        send_sem=tok_send.at[half, slot],
                        recv_sem=tok_recv.at[half, slot],
                        device_id={"var": along(half, first), "tile": tile},
                        device_id_type=MESH,
                    ).start()

    weights = ((w_pq, pq), (w_pk, pk), (w_pv, pv), (w_po, po))
    loads = [pltpu.make_async_copy(src, dst, w_sem.at[i]) for i, (src, dst) in enumerate(weights)]
    for load in loads:
        load.start()
    order = [(half, k) for k in range(RING) for half in (1, 0)]
    for half, k in order:
        send_tokens(half, k, own=True)
    pl.semaphore_wait(barrier, 9)
    for half, k in order[:4]:
        send_tokens(half, k)

    row = lax.broadcasted_iota(jnp.int32, (STATS, LATENT * D), 0)
    col = lax.broadcasted_iota(jnp.int32, (STATS, LATENT * D), 1)
    ex_scr[...] = jnp.where(
        (row & (STATS // 2 - 1)) == (col >> 9) * HEADS + ((col & (D - 1)) >> 5), 1.0, 0.0
    ).astype(BF16)
    loads[0].wait()
    queries = dot(lq_ref[...], pq[...])
    head_row = lax.broadcasted_iota(jnp.int32, (HEADS, D), 0)
    head_col = lax.broadcasted_iota(jnp.int32, (HEADS, D), 1) >> 5
    spread = jnp.concatenate(
        [jnp.where(head_row == head_col, queries[j : j + 1], 0.0) for j in range(LATENT)]
        + [jnp.zeros((STATS - LATENT * HEADS, D), F32)],
        axis=0,
    )
    loads[1].wait()
    probe = sum(last_by_last(part, pk[...]) for part in split(spread, 3))
    kp_scr[...] = (probe / math.sqrt(HD)).astype(BF16)
    loads[2].wait()

    lane = lax.broadcasted_iota(jnp.int32, (PAD, STATS), 1)

    def widen(scales):
        head = scales.astype(BF16).astype(F32)
        rest = pltpu.roll(scales - head, STATS // 2, 1)
        low = lax.broadcasted_iota(jnp.int32, scales.shape, 1) < STATS // 2
        return dot(jnp.where(low, head, rest).astype(BF16), ex_scr[...])

    lane_wide = lax.broadcasted_iota(jnp.int32, (BOTH, STATS), 1)

    def products(half, k, src):
        index = half * RING + k
        rows = buf[half, slot_of(half, k), src].reshape(BOTH * LEVS, D)
        at = src * BOTH * LEVS
        s_scr[index, at : at + BOTH * LEVS, :] = last_by_last(rows, kp_scr[...])
        values = dot(rows, pv[...])
        for lanes in range(D // 128):
            v_scr[index, lanes, at : at + BOTH * LEVS, :] = values[:, lanes * 128 : (lanes + 1) * 128]

    def arrive(half, k):
        slot = slot_of(half, k)
        arrived = buf.at[half, slot, 1]
        pltpu.make_async_copy(arrived, arrived, tok_recv.at[half, slot]).wait()
        if k + 2 < RING:
            send_tokens(half, k + 2)

    def work(half, k):
        slot = slot_of(half, k)
        index = half * RING + k
        members = [
            pl.ds(src * BOTH * LEVS + t, BOTH, stride=LEVS)
            for src in range(2)
            for t in range(LEVS)
        ]
        scores = [s_scr[index, member, :] for member in members]
        top = functools.reduce(jnp.maximum, scores)
        total = jnp.zeros_like(top)
        for n, score in enumerate(scores):
            weight = jnp.exp(score - top)
            total = total + weight
            p_scr[half, n * BOTH : (n + 1) * BOTH, :] = jnp.where(lane_wide < STATS // 2, weight, 0.0).astype(BF16)
        stats = jnp.where(lane_wide < STATS // 2, top, pltpu.roll(total, STATS // 2, 1))
        kstat[index, 0:PATCHES, :] = stats[:PATCHES]
        sstat[index, 0:PATCHES, :] = stats[PATCHES:]
        for at in range(0, LATENT * D, 256):
            wide = dot(p_scr[half], ex_scr[:, at : at + 256])
            for side in range(2):
                lanes = (at % D) // 128 + side
                here = sum(
                    v_scr[index, lanes, member, :]
                    * wide[n * BOTH : (n + 1) * BOTH, side * 128 : (side + 1) * 128]
                    for n, member in enumerate(members)
                )
                columns = slice(at + side * 128, at + (side + 1) * 128)
                keep[index, 0:PATCHES, columns] = here[:PATCHES]
                snum[index, 0:PATCHES, columns] = here[PATCHES:].astype(BF16)
        _, second = partners(half, slot)
        for src, dst, send, recv in (
            (snum, rnum, num_send, num_recv), (sstat, rstat, stat_send, stat_recv)
        ):
            pltpu.make_async_remote_copy(
                src_ref=src.at[index],
                dst_ref=dst.at[index],
                send_sem=send.at[index],
                recv_sem=recv.at[index],
                device_id={"var": along(half, second), "tile": tile},
                device_id_type=MESH,
            ).start()

    def merge(half, k):
        slot = slot_of(half, k)
        index = half * RING + k
        pltpu.make_async_copy(rstat.at[index], rstat.at[index], stat_recv.at[index]).wait()
        mine, theirs = kstat[index], rstat[index]
        top = jnp.maximum(mine, theirs)
        my_scale, their_scale = jnp.exp(mine - top), jnp.exp(theirs - top)
        total = (
            pltpu.roll(mine, STATS // 2, 1) * my_scale
            + pltpu.roll(theirs, STATS // 2, 1) * their_scale
        )
        fstat[index] = jnp.where(lane < STATS // 2, top, pltpu.roll(total, STATS // 2, 1))
        scales = jnp.concatenate([my_scale, their_scale], axis=0)
        scales = widen(scales)
        pltpu.make_async_copy(rnum.at[index], rnum.at[index], num_recv.at[index]).wait()
        fnum[index] = (
            keep[index] * scales[:PAD] + rnum[index].astype(F32) * scales[PAD:]
        ).astype(BF16)
        source = y if half == 0 else x
        there = slot * RING + x if half == 0 else y * RING + slot
        for src, dst, send, recv in (
            (fnum, gnum, far_send, far_recv), (fstat, gstat, fst_send, fst_recv)
        ):
            if half == 0 and k == RING - 1:
                pltpu.make_async_copy(src.at[index], dst.at[half, source], recv.at[half]).start()
            else:
                pltpu.make_async_remote_copy(
                    src_ref=src.at[index],
                    dst_ref=dst.at[half, source],
                    send_sem=send.at[index],
                    recv_sem=recv.at[half],
                    device_id={"var": there, "tile": tile if half == 0 else west},
                    device_id_type=MESH,
                ).start()

    for half, k in order:
        own = buf.at[half, slot_of(half, k), 0]
        pltpu.make_async_copy(own, own, own_sem.at[half, slot_of(half, k)]).wait()
        products(half, k, 0)
    for k in range(RING):
        for half in (1, 0):
            arrive(half, k)
        for half in (1, 0):
            products(half, k, 1)
        for half in (1, 0):
            work(half, k)
            if k > 0:
                merge(half, k - 1)
    for half in (1, 0):
        merge(half, RING - 1)

    inside = lax.broadcasted_iota(jnp.int32, (PAD, STATS), 0) < PATCHES
    for half in range(2):
        pltpu.make_async_copy(gnum.at[half], gnum.at[half], far_recv.at[half]).wait()
        pltpu.make_async_copy(gstat.at[half], gstat.at[half], fst_recv.at[half]).wait()
        stats = [gstat[half, src] for src in range(RING)]
        top = functools.reduce(jnp.maximum, stats)
        scales = [jnp.exp(stat - top) for stat in stats]
        denominator = sum(
            pltpu.roll(stat, STATS // 2, 1) * scale for stat, scale in zip(stats, scales)
        )
        valid = (lane < LATENT * HEADS) & inside
        for src in range(RING):
            sc_scr[pl.ds(src * PAD, PAD), :] = jnp.where(valid, scales[src] / denominator, 0.0)
        px_scr[0 : RING * PAD] = widen(sc_scr[...])
        inside_wide = lax.broadcasted_iota(jnp.int32, (PAD, D), 0) < PATCHES
        for j in range(LATENT):
            share = sum(
                gnum[half, src, :, j * D : (j + 1) * D].astype(F32)
                * px_scr[pl.ds(src * PAD, PAD), j * D : (j + 1) * D]
                for src in range(RING)
            )
            att_scr[pl.ds((half * LATENT + j) * PAD, PAD), :] = jnp.where(inside_wide, share, 0.0)

    loads[3].wait()
    latent = dot(att_scr[...].astype(BF16), po[...])
    start = jnp.concatenate(
        [
            jnp.broadcast_to(lq_ref[j : j + 1, :].astype(F32), (PAD, D))
            for _ in range(2)
            for j in range(LATENT)
        ],
        axis=0,
    )
    out_ref[...] = (start + latent).astype(BF16)

    for half in range(2):
        for k in range(RING):
            slot = slot_of(half, k)
            index = half * RING + k
            sent = buf.at[half, slot, 1]
            pltpu.make_async_copy(sent, sent, tok_send.at[half, slot]).wait()
            pltpu.make_async_copy(snum.at[index], snum.at[index], num_send.at[index]).wait()
            pltpu.make_async_copy(sstat.at[index], sstat.at[index], stat_send.at[index]).wait()
            if half == 1 or k < RING - 1:
                pltpu.make_async_copy(fnum.at[index], fnum.at[index], far_send.at[index]).wait()
                pltpu.make_async_copy(fstat.at[index], fstat.at[index], fst_send.at[index]).wait()


def window_kernel(
    latent_ref, gains_ref, w_sq, w_skv, w_so, w_up, w_down, out_ref,
    sq, skv, so, up, down, vt_scr, mix_scr, turn_scr, w_sem,
):
    weights = ((w_sq, sq), (w_skv, skv), (w_so, so), (w_up, up), (w_down, down))
    loads = [pltpu.make_async_copy(src, dst, w_sem.at[i]) for i, (src, dst) in enumerate(weights)]
    for load in loads:
        load.start()
    var = lax.axis_index("var")
    residual = latent_ref[...].astype(F32)
    normed = layer_norm(residual, gains_ref[0:1, :]).astype(BF16)
    loads[0].wait()
    queries = dot(normed, sq[...]).astype(BF16)
    loads[1].wait()
    keyvals = dot(normed, skv[...])
    keys = keyvals[:, :D]
    vt_scr[...] = jnp.transpose(keyvals[:, D:]).astype(BF16)

    def place(shape, axis):
        index = lax.broadcasted_iota(jnp.int32, shape, axis)
        for b in range(2 * LATENT - 1, 0, -1):
            index = jnp.where(index >= b * PAD, index - b * PAD, index)
        return index

    key_at = place((ROWS, ROWS), 0)
    query_at = place((ROWS, ROWS), 1)
    cut = WLAT // 2 * HALF
    apart = (key_at >= cut) != (query_at >= cut)
    excluded = (key_at >= PATCHES) | (apart & (var == N_VAR - 1))
    bias = jnp.where(excluded, -jnp.inf, 0.0)
    lane_head = lax.broadcasted_iota(jnp.int32, (ROWS, 256), 1) >> 5
    for h in range(HEADS):
        at = h // 8 * 256
        key_part = jnp.where(lane_head == h % 8, keys[:, at : at + 256], 0.0).astype(BF16)
        logits = last_by_last(key_part, queries[:, at : at + 256]) + bias
        top = jnp.max(logits, axis=0, keepdims=True)
        exponent = jnp.exp2((logits - top) * (math.log2(math.e) / math.sqrt(HD)))
        probs = (exponent * (1.0 / jnp.sum(exponent, axis=0, keepdims=True))).astype(BF16)
        mix_scr[h * HD : (h + 1) * HD, :] = dot(vt_scr[h * HD : (h + 1) * HD, :], probs)
    mixed = jnp.transpose(mix_scr[...]).astype(BF16)
    loads[2].wait()
    residual = residual + dot(mixed, so[...])
    normed = layer_norm(residual, gains_ref[1:2, :]).astype(BF16)
    loads[3].wait()
    loads[4].wait()
    chunk = 512
    for c in range(0, FF, chunk):
        wide = dot(normed, up[:, c : c + chunk])
        hidden = (0.5 * wide * (1.0 + lax.erf(wide * math.sqrt(0.5)))).astype(BF16)
        residual = residual + dot(hidden, down[c : c + chunk, :])
    lanes = D // 128
    for b in range(2 * LATENT):
        half, j = b // LATENT, b % LATENT
        for l in range(lanes):
            turn_scr[l, pl.ds(half * PATCHES * 4 + j, PATCHES, stride=4), :] = residual[
                b * PAD : b * PAD + PATCHES, l * 128 : (l + 1) * 128
            ]
    for half in range(2):
        for r in range(WLAT):
            for l in range(lanes):
                rows = turn_scr[l, pl.ds((half * PATCHES + r * HALF) * 4, HALF * 4), :]
                rows = rows.reshape(HALF, 4, 128)[:, :LATENT]
                out_ref[r, half * HALF : (half + 1) * HALF, :, l * 128 : (l + 1) * 128] = rows.astype(BF16)


def body(
    tokens, latent_queries, perc_query, perc_key, perc_value, perc_out, norm_gains, swin_query,
    swin_keyvalue, swin_out, mlp_up, mlp_down,
):
    whole = pl.BlockSpec(memory_space=pltpu.HBM)
    near = pl.BlockSpec(memory_space=pltpu.VMEM)
    matrices = (perc_query, perc_key, perc_value, perc_out)
    pieces = 2 * RING
    latent = pl.pallas_call(
        gather_kernel,
        out_shape=jax.ShapeDtypeStruct((ROWS, D), BF16),
        in_specs=[whole] * (1 + len(matrices)) + [near],
        out_specs=near,
        scratch_shapes=[
            pltpu.VMEM((2, RING, 2, 2, WLAT, HALF, LEVS, D), BF16),
            *[pltpu.VMEM(m.shape, m.dtype) for m in matrices],
            pltpu.VMEM((STATS, D), BF16),
            pltpu.VMEM((STATS, LATENT * D), BF16),
            pltpu.VMEM((pieces, GATHERED, STATS), F32),
            pltpu.VMEM((pieces, D // 128, GATHERED, 128), F32),
            pltpu.VMEM((2, GATHERED, STATS), BF16),
            pltpu.VMEM((RING * PAD, LATENT * D), F32),
            pltpu.VMEM((RING * PAD, STATS), F32),
            pltpu.VMEM((pieces, PAD, LATENT * D), F32),
            pltpu.VMEM((pieces, PAD, STATS), F32),
            pltpu.VMEM((pieces, PAD, LATENT * D), BF16),
            pltpu.VMEM((pieces, PAD, LATENT * D), BF16),
            pltpu.VMEM((pieces, PAD, STATS), F32),
            pltpu.VMEM((pieces, PAD, STATS), F32),
            pltpu.VMEM((pieces, PAD, LATENT * D), BF16),
            pltpu.VMEM((2, RING, PAD, LATENT * D), BF16),
            pltpu.VMEM((pieces, PAD, STATS), F32),
            pltpu.VMEM((2, RING, PAD, STATS), F32),
            pltpu.VMEM((ROWS, D), F32),
            pltpu.SemaphoreType.DMA((len(matrices),)),
            pltpu.SemaphoreType.DMA((2, RING)),
            pltpu.SemaphoreType.DMA((2, RING)),
            pltpu.SemaphoreType.DMA((2, RING)),
            pltpu.SemaphoreType.DMA((pieces,)),
            pltpu.SemaphoreType.DMA((pieces,)),
            pltpu.SemaphoreType.DMA((pieces,)),
            pltpu.SemaphoreType.DMA((pieces,)),
            pltpu.SemaphoreType.DMA((pieces,)),
            pltpu.SemaphoreType.DMA((2,)),
            pltpu.SemaphoreType.DMA((pieces,)),
            pltpu.SemaphoreType.DMA((2,)),
        ],
        compiler_params=pltpu.CompilerParams(
            collective_id=0, has_side_effects=True, vmem_limit_bytes=107 * 512 * 1024
        ),
        cost_estimate=pl.CostEstimate(
            flops=8_000_000_000, bytes_accessed=100_000_000, transcendentals=0
        ),
    )(tokens, *matrices, latent_queries)
    block = (swin_query, swin_keyvalue, swin_out, mlp_up, mlp_down)
    return pl.pallas_call(
        window_kernel,
        out_shape=jax.ShapeDtypeStruct((WLAT, 2 * HALF, LATENT, D), BF16),
        in_specs=[near, near] + [whole] * len(block),
        out_specs=near,
        scratch_shapes=[
            *[pltpu.VMEM(m.shape, m.dtype) for m in block],
            pltpu.VMEM((D, ROWS), BF16),
            pltpu.VMEM((D, ROWS), F32),
            pltpu.VMEM((D // 128, 2 * PATCHES * 4, 128), F32),
            pltpu.SemaphoreType.DMA((len(block),)),
        ],
        compiler_params=pltpu.CompilerParams(vmem_limit_bytes=40 * 1024 * 1024),
        cost_estimate=pl.CostEstimate(
            flops=2_000_000_000, bytes_accessed=7_000_000, transcendentals=0
        ),
    )(latent, norm_gains, *block)


def solution(mesh):
    placed = (P(None, "tile", "var", None), P(), P(), P(), P(), P(), P(), P(), P(), P(), P(), P())
    return jax.shard_map(
        body, mesh=mesh, in_specs=placed, out_specs=P("var", "tile", None, None), check_vma=False
    )
```

```python
import functools
import math

import jax
import jax.numpy as jnp
from jax import lax
from jax.experimental import pallas as pl
from jax.experimental.pallas import tpu as pltpu
from jax.sharding import PartitionSpec as P

F32 = jnp.float32
BF16 = jnp.bfloat16
D = 512
HEADS = 16
HD = 32
LATENT = 3
LEVS = 4
WLAT = 6
HALF = 6
RING = 4
N_VAR = RING * RING
N_TILE = 8
FF = 2048
PATCHES = WLAT * HALF
BOTH = 2 * PATCHES
GATHERED = 2 * BOTH * LEVS
PAD = 40
ROWS = 2 * LATENT * PAD
STATS = 128
MESH = pl.DeviceIdType.MESH
epsilon = 1e-05


def last_by_last(a, b):
    return lax.dot_general(a, b, (((1,), (1,)), ((), ())), preferred_element_type=F32)


def dot(a, b):
    return jnp.dot(a, b, preferred_element_type=F32)


def layer_norm(values, gain_row):
    average = jnp.mean(values, axis=-1, keepdims=True)
    centred = values - average
    spread = jnp.mean(centred * centred, axis=-1, keepdims=True)
    return centred * lax.rsqrt(spread + epsilon) * gain_row


def split(values, terms):
    parts = []
    for _ in range(terms):
        part = values.astype(BF16)
        parts.append(part)
        values = values - part.astype(F32)
    return parts


def gather_kernel(
    tokens, w_pq, w_pk, w_pv, w_po, lq_ref,
    out_ref,
    buf, pq, pk, pv, po,
    kp_scr, ex_scr, s_scr, v_scr, p_scr, px_scr, sc_scr, keep, kstat, snum, rnum, sstat, rstat,
    fnum, gnum, fstat, gstat, att_scr,
    w_sem, own_sem, tok_send, tok_recv, num_send, num_recv, stat_send, stat_recv,
    far_send, far_recv, fst_send, fst_recv,
):
    var = lax.axis_index("var")
    tile = lax.axis_index("tile")
    y, x = var // RING, var % RING
    west = lax.rem(tile + N_TILE - 1, N_TILE)
    east = lax.rem(tile + 1, N_TILE)

    barrier = pltpu.get_barrier_semaphore()

    def greet(there, at):
        pl.semaphore_signal(
            barrier, inc=1, device_id={"var": there, "tile": at}, device_id_type=MESH
        )

    for d in (1, 3):
        greet(y * RING + lax.rem(x + d, RING), tile)
    for d in (1, 2, 3):
        greet(lax.rem(y + d, RING) * RING + x, tile)
    for d in range(RING):
        greet(y * RING + lax.rem(x + d, RING), east)

    def slot_of(half, k):
        return lax.rem((y if half == 0 else x) + 1 + k, RING)

    def partners(half, slot):
        a = x if half == 0 else y
        odd = lax.rem(slot, 2)
        one, three = a + 1 - 2 * lax.rem(a, 2), 3 - a
        return one + odd * (three - one), three + odd * (one - three)

    def along(half, place):
        return y * RING + place if half == 0 else place * RING + x

    def send_tokens(half, k, own=False):
        slot = slot_of(half, k)
        a = x if half == 0 else y
        lon = HALF if half == 0 else 0
        first, second = partners(half, slot)
        for which, owner in ((0, a), (1, second)) if own else ((0, first), (1, lax.rem(a + 2, RING))):
            src_at = 0 if own else 1
            band = slot * RING + owner if half == 0 else owner * RING + slot
            upper = WLAT * band + WLAT // 2
            lower = lax.rem(WLAT * band + WLAT, WLAT * N_VAR)
            for part, row in ((0, upper), (1, lower)):
                src = tokens.at[pl.ds(row, WLAT // 2), pl.ds(lon, HALF)]
                dst = buf.at[half, slot, src_at, which, pl.ds(part * (WLAT // 2), WLAT // 2)]
                if own:
                    pltpu.make_async_copy(src, dst, own_sem.at[half, slot]).start()
                else:
                    pltpu.make_async_remote_copy(
                        src_ref=src,
                        dst_ref=dst,
                        send_sem=tok_send.at[half, slot],
                        recv_sem=tok_recv.at[half, slot],
                        device_id={"var": along(half, first), "tile": tile},
                        device_id_type=MESH,
                    ).start()

    weights = ((w_pq, pq), (w_pk, pk), (w_pv, pv), (w_po, po))
    loads = [pltpu.make_async_copy(src, dst, w_sem.at[i]) for i, (src, dst) in enumerate(weights)]
    for load in loads:
        load.start()
    order = [(half, k) for k in range(RING) for half in (1, 0)]
    for half, k in order:
        send_tokens(half, k, own=True)
    pl.semaphore_wait(barrier, 9)
    for half, k in order[:4]:
        send_tokens(half, k)

    row = lax.broadcasted_iota(jnp.int32, (STATS, LATENT * D), 0)
    col = lax.broadcasted_iota(jnp.int32, (STATS, LATENT * D), 1)
    ex_scr[...] = jnp.where(
        (row & (STATS // 2 - 1)) == (col >> 9) * HEADS + ((col & (D - 1)) >> 5), 1.0, 0.0
    ).astype(BF16)
    loads[0].wait()
    queries = dot(lq_ref[...], pq[...])
    head_row = lax.broadcasted_iota(jnp.int32, (HEADS, D), 0)
    head_col = lax.broadcasted_iota(jnp.int32, (HEADS, D), 1) >> 5
    spread = jnp.concatenate(
        [jnp.where(head_row == head_col, queries[j : j + 1], 0.0) for j in range(LATENT)]
        + [jnp.zeros((STATS - LATENT * HEADS, D), F32)],
        axis=0,
    )
    loads[1].wait()
    probe = sum(last_by_last(part, pk[...]) for part in split(spread, 3))
    kp_scr[...] = (probe / math.sqrt(HD)).astype(BF16)
    loads[2].wait()

    lane = lax.broadcasted_iota(jnp.int32, (PAD, STATS), 1)

    def widen(scales):
        head = scales.astype(BF16).astype(F32)
        rest = pltpu.roll(scales - head, STATS // 2, 1)
        low = lax.broadcasted_iota(jnp.int32, scales.shape, 1) < STATS // 2
        return dot(jnp.where(low, head, rest).astype(BF16), ex_scr[...])

    lane_wide = lax.broadcasted_iota(jnp.int32, (BOTH, STATS), 1)

    def products(half, k, src):
        index = half * RING + k
        rows = buf[half, slot_of(half, k), src].reshape(BOTH * LEVS, D)
        at = src * BOTH * LEVS
        s_scr[index, at : at + BOTH * LEVS, :] = last_by_last(rows, kp_scr[...])
        values = dot(rows, pv[...])
        for lanes in range(D // 128):
            v_scr[index, lanes, at : at + BOTH * LEVS, :] = values[:, lanes * 128 : (lanes + 1) * 128]

    def arrive(half, k):
        slot = slot_of(half, k)
        arrived = buf.at[half, slot, 1]
        pltpu.make_async_copy(arrived, arrived, tok_recv.at[half, slot]).wait()
        if k + 2 < RING:
            send_tokens(half, k + 2)

    def work(half, k):
        slot = slot_of(half, k)
        index = half * RING + k
        members = [
            pl.ds(src * BOTH * LEVS + t, BOTH, stride=LEVS)
            for src in range(2)
            for t in range(LEVS)
        ]
        scores = [s_scr[index, member, :] for member in members]
        top = functools.reduce(jnp.maximum, scores)
        total = jnp.zeros_like(top)
        for n, score in enumerate(scores):
            weight = jnp.exp(score - top)
            total = total + weight
            p_scr[half, n * BOTH : (n + 1) * BOTH, :] = weight.astype(BF16).astype(F32)
        stats = jnp.where(lane_wide < STATS // 2, top, pltpu.roll(total, STATS // 2, 1))
        kstat[index, 0:PATCHES, :] = stats[:PATCHES]
        sstat[index, 0:PATCHES, :] = stats[PATCHES:]
        for lanes in range(D // 128):
            sums = [jnp.zeros((BOTH, 128), F32) for _ in range(LATENT)]
            for n, member in enumerate(members):
                value = v_scr[index, lanes, member, :]
                weight = p_scr[half, n * BOTH : (n + 1) * BOTH, :]
                for j in range(LATENT):
                    column = (lane_wide >> 5) + (j * HEADS + lanes * 4)
                    sums[j] += value * jnp.take_along_axis(
                        weight, column, axis=1, mode="promise_in_bounds"
                    )
            for j in range(LATENT):
                columns = slice(j * D + lanes * 128, j * D + (lanes + 1) * 128)
                keep[index, 0:PATCHES, columns] = sums[j][:PATCHES]
                snum[index, 0:PATCHES, columns] = sums[j][PATCHES:].astype(BF16)
        _, second = partners(half, slot)
        for src, dst, send, recv in (
            (snum, rnum, num_send, num_recv), (sstat, rstat, stat_send, stat_recv)
        ):
            pltpu.make_async_remote_copy(
                src_ref=src.at[index],
                dst_ref=dst.at[index],
                send_sem=send.at[index],
                recv_sem=recv.at[index],
                device_id={"var": along(half, second), "tile": tile},
                device_id_type=MESH,
            ).start()

    def merge(half, k):
        slot = slot_of(half, k)
        index = half * RING + k
        pltpu.make_async_copy(rstat.at[index], rstat.at[index], stat_recv.at[index]).wait()
        mine, theirs = kstat[index], rstat[index]
        top = jnp.maximum(mine, theirs)
        my_scale, their_scale = jnp.exp(mine - top), jnp.exp(theirs - top)
        total = (
            pltpu.roll(mine, STATS // 2, 1) * my_scale
            + pltpu.roll(theirs, STATS // 2, 1) * their_scale
        )
        fstat[index] = jnp.where(lane < STATS // 2, top, pltpu.roll(total, STATS // 2, 1))
        scales = jnp.concatenate([my_scale, their_scale], axis=0)
        scales = widen(scales)
        pltpu.make_async_copy(rnum.at[index], rnum.at[index], num_recv.at[index]).wait()
        fnum[index] = (
            keep[index] * scales[:PAD] + rnum[index].astype(F32) * scales[PAD:]
        ).astype(BF16)
        source = y if half == 0 else x
        there = slot * RING + x if half == 0 else y * RING + slot
        for src, dst, send, recv in (
            (fnum, gnum, far_send, far_recv), (fstat, gstat, fst_send, fst_recv)
        ):
            if half == 0 and k == RING - 1:
                pltpu.make_async_copy(src.at[index], dst.at[half, source], recv.at[half]).start()
            else:
                pltpu.make_async_remote_copy(
                    src_ref=src.at[index],
                    dst_ref=dst.at[half, source],
                    send_sem=send.at[index],
                    recv_sem=recv.at[half],
                    device_id={"var": there, "tile": tile if half == 0 else west},
                    device_id_type=MESH,
                ).start()

    for half, k in order:
        own = buf.at[half, slot_of(half, k), 0]
        pltpu.make_async_copy(own, own, own_sem.at[half, slot_of(half, k)]).wait()
        products(half, k, 0)
    for k in range(RING):
        for half in (1, 0):
            arrive(half, k)
        for half in (1, 0):
            products(half, k, 1)
        for half in (1, 0):
            work(half, k)
            if k > 0:
                merge(half, k - 1)
    for half in (1, 0):
        merge(half, RING - 1)

    inside = lax.broadcasted_iota(jnp.int32, (PAD, STATS), 0) < PATCHES
    for half in range(2):
        pltpu.make_async_copy(gnum.at[half], gnum.at[half], far_recv.at[half]).wait()
        pltpu.make_async_copy(gstat.at[half], gstat.at[half], fst_recv.at[half]).wait()
        stats = [gstat[half, src] for src in range(RING)]
        top = functools.reduce(jnp.maximum, stats)
        scales = [jnp.exp(stat - top) for stat in stats]
        denominator = sum(
            pltpu.roll(stat, STATS // 2, 1) * scale for stat, scale in zip(stats, scales)
        )
        valid = (lane < LATENT * HEADS) & inside
        for src in range(RING):
            sc_scr[pl.ds(src * PAD, PAD), :] = jnp.where(valid, scales[src] / denominator, 0.0)
        px_scr[0 : RING * PAD] = widen(sc_scr[...])
        inside_wide = lax.broadcasted_iota(jnp.int32, (PAD, D), 0) < PATCHES
        for j in range(LATENT):
            share = sum(
                gnum[half, src, :, j * D : (j + 1) * D].astype(F32)
                * px_scr[pl.ds(src * PAD, PAD), j * D : (j + 1) * D]
                for src in range(RING)
            )
            att_scr[pl.ds((half * LATENT + j) * PAD, PAD), :] = jnp.where(inside_wide, share, 0.0)

    loads[3].wait()
    latent = dot(att_scr[...].astype(BF16), po[...])
    start = jnp.concatenate(
        [
            jnp.broadcast_to(lq_ref[j : j + 1, :].astype(F32), (PAD, D))
            for _ in range(2)
            for j in range(LATENT)
        ],
        axis=0,
    )
    out_ref[...] = (start + latent).astype(BF16)

    for half in range(2):
        for k in range(RING):
            slot = slot_of(half, k)
            index = half * RING + k
            sent = buf.at[half, slot, 1]
            pltpu.make_async_copy(sent, sent, tok_send.at[half, slot]).wait()
            pltpu.make_async_copy(snum.at[index], snum.at[index], num_send.at[index]).wait()
            pltpu.make_async_copy(sstat.at[index], sstat.at[index], stat_send.at[index]).wait()
            if half == 1 or k < RING - 1:
                pltpu.make_async_copy(fnum.at[index], fnum.at[index], far_send.at[index]).wait()
                pltpu.make_async_copy(fstat.at[index], fstat.at[index], fst_send.at[index]).wait()


def window_kernel(
    latent_ref, gains_ref, w_sq, w_skv, w_so, w_up, w_down, out_ref,
    sq, skv, so, up, down, vt_scr, mix_scr, turn_scr, w_sem,
):
    weights = ((w_sq, sq), (w_skv, skv), (w_so, so), (w_up, up), (w_down, down))
    loads = [pltpu.make_async_copy(src, dst, w_sem.at[i]) for i, (src, dst) in enumerate(weights)]
    for load in loads:
        load.start()
    var = lax.axis_index("var")
    residual = latent_ref[...].astype(F32)
    normed = layer_norm(residual, gains_ref[0:1, :]).astype(BF16)
    loads[0].wait()
    queries = dot(normed, sq[...]).astype(BF16)
    loads[1].wait()
    keyvals = dot(normed, skv[...])
    keys = keyvals[:, :D]
    vt_scr[...] = jnp.transpose(keyvals[:, D:]).astype(BF16)

    def place(shape, axis):
        index = lax.broadcasted_iota(jnp.int32, shape, axis)
        for b in range(2 * LATENT - 1, 0, -1):
            index = jnp.where(index >= b * PAD, index - b * PAD, index)
        return index

    key_at = place((ROWS, ROWS), 0)
    query_at = place((ROWS, ROWS), 1)
    cut = WLAT // 2 * HALF
    apart = (key_at >= cut) != (query_at >= cut)
    excluded = (key_at >= PATCHES) | (apart & (var == N_VAR - 1))
    bias = jnp.where(excluded, -jnp.inf, 0.0)
    lane_head = lax.broadcasted_iota(jnp.int32, (ROWS, 256), 1) >> 5
    for h in range(HEADS):
        at = h // 8 * 256
        key_part = jnp.where(lane_head == h % 8, keys[:, at : at + 256], 0.0).astype(BF16)
        logits = last_by_last(key_part, queries[:, at : at + 256]) + bias
        top = jnp.max(logits, axis=0, keepdims=True)
        exponent = jnp.exp2((logits - top) * (math.log2(math.e) / math.sqrt(HD)))
        probs = (exponent * (1.0 / jnp.sum(exponent, axis=0, keepdims=True))).astype(BF16)
        mix_scr[h * HD : (h + 1) * HD, :] = dot(vt_scr[h * HD : (h + 1) * HD, :], probs)
    mixed = jnp.transpose(mix_scr[...]).astype(BF16)
    loads[2].wait()
    residual = residual + dot(mixed, so[...])
    normed = layer_norm(residual, gains_ref[1:2, :]).astype(BF16)
    loads[3].wait()
    loads[4].wait()
    chunk = 512
    for c in range(0, FF, chunk):
        wide = dot(normed, up[:, c : c + chunk])
        hidden = (0.5 * wide * (1.0 + lax.erf(wide * math.sqrt(0.5)))).astype(BF16)
        residual = residual + dot(hidden, down[c : c + chunk, :])
    lanes = D // 128
    for b in range(2 * LATENT):
        half, j = b // LATENT, b % LATENT
        for l in range(lanes):
            turn_scr[l, pl.ds(half * PATCHES * 4 + j, PATCHES, stride=4), :] = residual[
                b * PAD : b * PAD + PATCHES, l * 128 : (l + 1) * 128
            ]
    for half in range(2):
        for r in range(WLAT):
            for l in range(lanes):
                rows = turn_scr[l, pl.ds((half * PATCHES + r * HALF) * 4, HALF * 4), :]
                rows = rows.reshape(HALF, 4, 128)[:, :LATENT]
                out_ref[r, half * HALF : (half + 1) * HALF, :, l * 128 : (l + 1) * 128] = rows.astype(BF16)


def body(
    tokens, latent_queries, perc_query, perc_key, perc_value, perc_out, norm_gains, swin_query,
    swin_keyvalue, swin_out, mlp_up, mlp_down,
):
    whole = pl.BlockSpec(memory_space=pltpu.HBM)
    near = pl.BlockSpec(memory_space=pltpu.VMEM)
    matrices = (perc_query, perc_key, perc_value, perc_out)
    pieces = 2 * RING
    latent = pl.pallas_call(
        gather_kernel,
        out_shape=jax.ShapeDtypeStruct((ROWS, D), BF16),
        in_specs=[whole] * (1 + len(matrices)) + [near],
        out_specs=near,
        scratch_shapes=[
            pltpu.VMEM((2, RING, 2, 2, WLAT, HALF, LEVS, D), BF16),
            *[pltpu.VMEM(m.shape, m.dtype) for m in matrices],
            pltpu.VMEM((STATS, D), BF16),
            pltpu.VMEM((STATS, LATENT * D), BF16),
            pltpu.VMEM((pieces, GATHERED, STATS), F32),
            pltpu.VMEM((pieces, D // 128, GATHERED, 128), F32),
            pltpu.VMEM((2, GATHERED, STATS), F32),
            pltpu.VMEM((RING * PAD, LATENT * D), F32),
            pltpu.VMEM((RING * PAD, STATS), F32),
            pltpu.VMEM((pieces, PAD, LATENT * D), F32),
            pltpu.VMEM((pieces, PAD, STATS), F32),
            pltpu.VMEM((pieces, PAD, LATENT * D), BF16),
            pltpu.VMEM((pieces, PAD, LATENT * D), BF16),
            pltpu.VMEM((pieces, PAD, STATS), F32),
            pltpu.VMEM((pieces, PAD, STATS), F32),
            pltpu.VMEM((pieces, PAD, LATENT * D), BF16),
            pltpu.VMEM((2, RING, PAD, LATENT * D), BF16),
            pltpu.VMEM((pieces, PAD, STATS), F32),
            pltpu.VMEM((2, RING, PAD, STATS), F32),
            pltpu.VMEM((ROWS, D), F32),
            pltpu.SemaphoreType.DMA((len(matrices),)),
            pltpu.SemaphoreType.DMA((2, RING)),
            pltpu.SemaphoreType.DMA((2, RING)),
            pltpu.SemaphoreType.DMA((2, RING)),
            pltpu.SemaphoreType.DMA((pieces,)),
            pltpu.SemaphoreType.DMA((pieces,)),
            pltpu.SemaphoreType.DMA((pieces,)),
            pltpu.SemaphoreType.DMA((pieces,)),
            pltpu.SemaphoreType.DMA((pieces,)),
            pltpu.SemaphoreType.DMA((2,)),
            pltpu.SemaphoreType.DMA((pieces,)),
            pltpu.SemaphoreType.DMA((2,)),
        ],
        compiler_params=pltpu.CompilerParams(
            collective_id=0, has_side_effects=True, vmem_limit_bytes=107 * 512 * 1024
        ),
        cost_estimate=pl.CostEstimate(
            flops=8_000_000_000, bytes_accessed=100_000_000, transcendentals=0
        ),
    )(tokens, *matrices, latent_queries)
    block = (swin_query, swin_keyvalue, swin_out, mlp_up, mlp_down)
    return pl.pallas_call(
        window_kernel,
        out_shape=jax.ShapeDtypeStruct((WLAT, 2 * HALF, LATENT, D), BF16),
        in_specs=[near, near] + [whole] * len(block),
        out_specs=near,
        scratch_shapes=[
            *[pltpu.VMEM(m.shape, m.dtype) for m in block],
            pltpu.VMEM((D, ROWS), BF16),
            pltpu.VMEM((D, ROWS), F32),
            pltpu.VMEM((D // 128, 2 * PATCHES * 4, 128), F32),
            pltpu.SemaphoreType.DMA((len(block),)),
        ],
        compiler_params=pltpu.CompilerParams(vmem_limit_bytes=40 * 1024 * 1024),
        cost_estimate=pl.CostEstimate(
            flops=2_000_000_000, bytes_accessed=7_000_000, transcendentals=0
        ),
    )(latent, norm_gains, *block)


def solution(mesh):
    placed = (P(None, "tile", "var", None), P(), P(), P(), P(), P(), P(), P(), P(), P(), P(), P())
    return jax.shard_map(
        body, mesh=mesh, in_specs=placed, out_specs=P("var", "tile", None, None), check_vma=False
    )
```

```python
import functools
import math

import jax
import jax.numpy as jnp
from jax import lax
from jax.experimental import pallas as pl
from jax.experimental.pallas import tpu as pltpu
from jax.sharding import PartitionSpec as P

F32 = jnp.float32
BF16 = jnp.bfloat16
D = 512
HEADS = 16
HD = 32
LATENT = 3
LEVS = 4
WLAT = 6
HALF = 6
RING = 4
N_VAR = RING * RING
N_TILE = 8
FF = 2048
PATCHES = WLAT * HALF
BOTH = 2 * PATCHES
GATHERED = 2 * BOTH * LEVS
PAD = 40
ROWS = 2 * LATENT * PAD
STATS = 128
MESH = pl.DeviceIdType.MESH
epsilon = 1e-05


def last_by_last(a, b):
    return lax.dot_general(a, b, (((1,), (1,)), ((), ())), preferred_element_type=F32)


def dot(a, b):
    return jnp.dot(a, b, preferred_element_type=F32)


def layer_norm(values, gain_row):
    average = jnp.mean(values, axis=-1, keepdims=True)
    centred = values - average
    spread = jnp.mean(centred * centred, axis=-1, keepdims=True)
    return centred * lax.rsqrt(spread + epsilon) * gain_row


def split(values, terms):
    parts = []
    for _ in range(terms):
        part = values.astype(BF16)
        parts.append(part)
        values = values - part.astype(F32)
    return parts


def gather_kernel(
    tokens, w_pq, w_pk, w_pv, w_po, lq_ref,
    out_ref,
    buf, pq, pk, pv, po,
    kp_scr, ex_scr, s_scr, v_scr, p_scr, px_scr, sc_scr, keep, kstat, snum, rnum, sstat, rstat,
    fnum, gnum, fstat, gstat, att_scr,
    w_sem, own_sem, tok_send, tok_recv, num_send, num_recv, stat_send, stat_recv,
    far_send, far_recv, fst_send, fst_recv,
):
    var = lax.axis_index("var")
    tile = lax.axis_index("tile")
    y, x = var // RING, var % RING
    west = lax.rem(tile + N_TILE - 1, N_TILE)
    east = lax.rem(tile + 1, N_TILE)

    barrier = pltpu.get_barrier_semaphore()

    def greet(there, at):
        pl.semaphore_signal(
            barrier, inc=1, device_id={"var": there, "tile": at}, device_id_type=MESH
        )

    for d in (1, 3):
        greet(y * RING + lax.rem(x + d, RING), tile)
    for d in (1, 2, 3):
        greet(lax.rem(y + d, RING) * RING + x, tile)
    for d in range(RING):
        greet(y * RING + lax.rem(x + d, RING), east)

    def slot_of(half, k):
        return lax.rem((y if half == 0 else x) + 1 + k, RING)

    def partners(half, slot):
        a = x if half == 0 else y
        odd = lax.rem(slot, 2)
        one, three = a + 1 - 2 * lax.rem(a, 2), 3 - a
        return one + odd * (three - one), three + odd * (one - three)

    def along(half, place):
        return y * RING + place if half == 0 else place * RING + x

    def send_tokens(half, k, own=False):
        slot = slot_of(half, k)
        a = x if half == 0 else y
        lon = HALF if half == 0 else 0
        first, second = partners(half, slot)
        for which, owner in ((0, a), (1, second)) if own else ((0, first), (1, lax.rem(a + 2, RING))):
            src_at = 0 if own else 1
            band = slot * RING + owner if half == 0 else owner * RING + slot
            upper = WLAT * band + WLAT // 2
            lower = lax.rem(WLAT * band + WLAT, WLAT * N_VAR)
            for part, row in ((0, upper), (1, lower)):
                src = tokens.at[pl.ds(row, WLAT // 2), pl.ds(lon, HALF)]
                dst = buf.at[half, slot, src_at, which, pl.ds(part * (WLAT // 2), WLAT // 2)]
                if own:
                    pltpu.make_async_copy(src, dst, own_sem.at[half, slot]).start()
                else:
                    pltpu.make_async_remote_copy(
                        src_ref=src,
                        dst_ref=dst,
                        send_sem=tok_send.at[half, slot],
                        recv_sem=tok_recv.at[half, slot],
                        device_id={"var": along(half, first), "tile": tile},
                        device_id_type=MESH,
                    ).start()

    weights = ((w_pq, pq), (w_pk, pk), (w_pv, pv), (w_po, po))
    loads = [pltpu.make_async_copy(src, dst, w_sem.at[i]) for i, (src, dst) in enumerate(weights)]
    for load in loads:
        load.start()
    order = [(half, k) for k in range(RING) for half in (1, 0)]
    for half, k in order:
        send_tokens(half, k, own=True)
    pl.semaphore_wait(barrier, 9)
    for half, k in order[:4]:
        send_tokens(half, k)

    row = lax.broadcasted_iota(jnp.int32, (STATS, LATENT * D), 0)
    col = lax.broadcasted_iota(jnp.int32, (STATS, LATENT * D), 1)
    ex_scr[...] = jnp.where(
        (row & (STATS // 2 - 1)) == (col >> 9) * HEADS + ((col & (D - 1)) >> 5), 1.0, 0.0
    ).astype(BF16)
    loads[0].wait()
    queries = dot(lq_ref[...], pq[...])
    head_row = lax.broadcasted_iota(jnp.int32, (HEADS, D), 0)
    head_col = lax.broadcasted_iota(jnp.int32, (HEADS, D), 1) >> 5
    spread = jnp.concatenate(
        [jnp.where(head_row == head_col, queries[j : j + 1], 0.0) for j in range(LATENT)]
        + [jnp.zeros((STATS - LATENT * HEADS, D), F32)],
        axis=0,
    )
    loads[1].wait()
    probe = sum(last_by_last(part, pk[...]) for part in split(spread, 3))
    kp_scr[...] = (probe / math.sqrt(HD)).astype(BF16)
    loads[2].wait()

    lane = lax.broadcasted_iota(jnp.int32, (PAD, STATS), 1)

    def widen(scales):
        head = scales.astype(BF16).astype(F32)
        rest = pltpu.roll(scales - head, STATS // 2, 1)
        low = lax.broadcasted_iota(jnp.int32, scales.shape, 1) < STATS // 2
        return dot(jnp.where(low, head, rest).astype(BF16), ex_scr[...])

    lane_wide = lax.broadcasted_iota(jnp.int32, (BOTH, STATS), 1)

    def products(half, k, src):
        index = half * RING + k
        rows = buf[half, slot_of(half, k), src].reshape(BOTH * LEVS, D)
        at = src * BOTH * LEVS
        s_scr[index, at : at + BOTH * LEVS, :] = last_by_last(rows, kp_scr[...])
        values = dot(rows, pv[...])
        for lanes in range(D // 128):
            v_scr[index, lanes, at : at + BOTH * LEVS, :] = values[:, lanes * 128 : (lanes + 1) * 128]

    def arrive(half, k):
        slot = slot_of(half, k)
        arrived = buf.at[half, slot, 1]
        pltpu.make_async_copy(arrived, arrived, tok_recv.at[half, slot]).wait()
        if k + 2 < RING:
            send_tokens(half, k + 2)

    def work(half, k):
        slot = slot_of(half, k)
        index = half * RING + k
        members = [
            pl.ds(src * BOTH * LEVS + t, BOTH, stride=LEVS)
            for src in range(2)
            for t in range(LEVS)
        ]
        scores = [s_scr[index, member, :] for member in members]
        top = functools.reduce(jnp.maximum, scores)
        total = jnp.zeros_like(top)
        for n, score in enumerate(scores):
            weight = jnp.exp(score - top)
            total = total + weight
            p_scr[half, n * BOTH : (n + 1) * BOTH, :] = jnp.where(lane_wide < STATS // 2, weight, 0.0).astype(BF16)
        stats = jnp.where(lane_wide < STATS // 2, top, pltpu.roll(total, STATS // 2, 1))
        kstat[index, 0:PATCHES, :] = stats[:PATCHES]
        sstat[index, 0:PATCHES, :] = stats[PATCHES:]
        for at in range(0, LATENT * D, 256):
            wide = dot(p_scr[half], ex_scr[:, at : at + 256])
            for side in range(2):
                lanes = (at % D) // 128 + side
                here = sum(
                    v_scr[index, lanes, member, :]
                    * wide[n * BOTH : (n + 1) * BOTH, side * 128 : (side + 1) * 128]
                    for n, member in enumerate(members)
                )
                columns = slice(at + side * 128, at + (side + 1) * 128)
                keep[index, 0:PATCHES, columns] = here[:PATCHES]
                snum[index, 0:PATCHES, columns] = here[PATCHES:].astype(BF16)
        _, second = partners(half, slot)
        for src, dst, send, recv in (
            (snum, rnum, num_send, num_recv), (sstat, rstat, stat_send, stat_recv)
        ):
            pltpu.make_async_remote_copy(
                src_ref=src.at[index],
                dst_ref=dst.at[index],
                send_sem=send.at[index],
                recv_sem=recv.at[index],
                device_id={"var": along(half, second), "tile": tile},
                device_id_type=MESH,
            ).start()

    def merge(half, k):
        slot = slot_of(half, k)
        index = half * RING + k
        pltpu.make_async_copy(rstat.at[index], rstat.at[index], stat_recv.at[index]).wait()
        mine, theirs = kstat[index], rstat[index]
        top = jnp.maximum(mine, theirs)
        my_scale, their_scale = jnp.exp(mine - top), jnp.exp(theirs - top)
        total = (
            pltpu.roll(mine, STATS // 2, 1) * my_scale
            + pltpu.roll(theirs, STATS // 2, 1) * their_scale
        )
        fstat[index] = jnp.where(lane < STATS // 2, top, pltpu.roll(total, STATS // 2, 1))
        scales = jnp.concatenate([my_scale, their_scale], axis=0)
        scales = widen(scales)
        pltpu.make_async_copy(rnum.at[index], rnum.at[index], num_recv.at[index]).wait()
        fnum[index] = (
            keep[index] * scales[:PAD] + rnum[index].astype(F32) * scales[PAD:]
        ).astype(BF16)
        source = y if half == 0 else x
        there = slot * RING + x if half == 0 else y * RING + slot
        for src, dst, send, recv in (
            (fnum, gnum, far_send, far_recv), (fstat, gstat, fst_send, fst_recv)
        ):
            if half == 0 and k == RING - 1:
                pltpu.make_async_copy(src.at[index], dst.at[half, source], recv.at[half]).start()
            else:
                pltpu.make_async_remote_copy(
                    src_ref=src.at[index],
                    dst_ref=dst.at[half, source],
                    send_sem=send.at[index],
                    recv_sem=recv.at[half],
                    device_id={"var": there, "tile": tile if half == 0 else west},
                    device_id_type=MESH,
                ).start()

    def own_products(half, k):
        slot = slot_of(half, k)
        own = buf.at[half, slot, 0]
        pltpu.make_async_copy(own, own, own_sem.at[half, slot]).wait()
        products(half, k, 0)

    for half, k in order[:4]:
        own_products(half, k)
    for k in range(2):
        for half in (1, 0):
            arrive(half, k)
        for half in (1, 0):
            own_products(half, k + 2)
    for k in range(RING):
        for half in (1, 0):
            if k >= 2:
                arrive(half, k)
        for half in (1, 0):
            products(half, k, 1)
        for half in (1, 0):
            work(half, k)
            if k > 0:
                merge(half, k - 1)
    for half in (1, 0):
        merge(half, RING - 1)

    inside = lax.broadcasted_iota(jnp.int32, (PAD, STATS), 0) < PATCHES
    for half in range(2):
        pltpu.make_async_copy(gnum.at[half], gnum.at[half], far_recv.at[half]).wait()
        pltpu.make_async_copy(gstat.at[half], gstat.at[half], fst_recv.at[half]).wait()
        stats = [gstat[half, src] for src in range(RING)]
        top = functools.reduce(jnp.maximum, stats)
        scales = [jnp.exp(stat - top) for stat in stats]
        denominator = sum(
            pltpu.roll(stat, STATS // 2, 1) * scale for stat, scale in zip(stats, scales)
        )
        valid = (lane < LATENT * HEADS) & inside
        for src in range(RING):
            sc_scr[pl.ds(src * PAD, PAD), :] = jnp.where(valid, scales[src] / denominator, 0.0)
        px_scr[0 : RING * PAD] = widen(sc_scr[...])
        inside_wide = lax.broadcasted_iota(jnp.int32, (PAD, D), 0) < PATCHES
        for j in range(LATENT):
            share = sum(
                gnum[half, src, :, j * D : (j + 1) * D].astype(F32)
                * px_scr[pl.ds(src * PAD, PAD), j * D : (j + 1) * D]
                for src in range(RING)
            )
            att_scr[pl.ds((half * LATENT + j) * PAD, PAD), :] = jnp.where(inside_wide, share, 0.0)

    loads[3].wait()
    latent = dot(att_scr[...].astype(BF16), po[...])
    start = jnp.concatenate(
        [
            jnp.broadcast_to(lq_ref[j : j + 1, :].astype(F32), (PAD, D))
            for _ in range(2)
            for j in range(LATENT)
        ],
        axis=0,
    )
    out_ref[...] = (start + latent).astype(BF16)

    for half in range(2):
        for k in range(RING):
            slot = slot_of(half, k)
            index = half * RING + k
            sent = buf.at[half, slot, 1]
            pltpu.make_async_copy(sent, sent, tok_send.at[half, slot]).wait()
            pltpu.make_async_copy(snum.at[index], snum.at[index], num_send.at[index]).wait()
            pltpu.make_async_copy(sstat.at[index], sstat.at[index], stat_send.at[index]).wait()
            if half == 1 or k < RING - 1:
                pltpu.make_async_copy(fnum.at[index], fnum.at[index], far_send.at[index]).wait()
                pltpu.make_async_copy(fstat.at[index], fstat.at[index], fst_send.at[index]).wait()


def window_kernel(
    latent_ref, gains_ref, w_sq, w_skv, w_so, w_up, w_down, out_ref,
    sq, skv, so, up, down, vt_scr, mix_scr, turn_scr, w_sem,
):
    weights = ((w_sq, sq), (w_skv, skv), (w_so, so), (w_up, up), (w_down, down))
    loads = [pltpu.make_async_copy(src, dst, w_sem.at[i]) for i, (src, dst) in enumerate(weights)]
    for load in loads:
        load.start()
    var = lax.axis_index("var")
    residual = latent_ref[...].astype(F32)
    normed = layer_norm(residual, gains_ref[0:1, :]).astype(BF16)
    loads[0].wait()
    queries = dot(normed, sq[...]).astype(BF16)
    loads[1].wait()
    keyvals = dot(normed, skv[...])
    keys = keyvals[:, :D]
    vt_scr[...] = jnp.transpose(keyvals[:, D:]).astype(BF16)

    def place(shape, axis):
        index = lax.broadcasted_iota(jnp.int32, shape, axis)
        for b in range(2 * LATENT - 1, 0, -1):
            index = jnp.where(index >= b * PAD, index - b * PAD, index)
        return index

    key_at = place((ROWS, ROWS), 0)
    query_at = place((ROWS, ROWS), 1)
    cut = WLAT // 2 * HALF
    apart = (key_at >= cut) != (query_at >= cut)
    excluded = (key_at >= PATCHES) | (apart & (var == N_VAR - 1))
    bias = jnp.where(excluded, -jnp.inf, 0.0)
    lane_head = lax.broadcasted_iota(jnp.int32, (ROWS, 256), 1) >> 5
    for h in range(HEADS):
        at = h // 8 * 256
        key_part = jnp.where(lane_head == h % 8, keys[:, at : at + 256], 0.0).astype(BF16)
        logits = last_by_last(key_part, queries[:, at : at + 256]) + bias
        top = jnp.max(logits, axis=0, keepdims=True)
        exponent = jnp.exp2((logits - top) * (math.log2(math.e) / math.sqrt(HD)))
        probs = (exponent * (1.0 / jnp.sum(exponent, axis=0, keepdims=True))).astype(BF16)
        mix_scr[h * HD : (h + 1) * HD, :] = dot(vt_scr[h * HD : (h + 1) * HD, :], probs)
    mixed = jnp.transpose(mix_scr[...]).astype(BF16)
    loads[2].wait()
    residual = residual + dot(mixed, so[...])
    normed = layer_norm(residual, gains_ref[1:2, :]).astype(BF16)
    loads[3].wait()
    loads[4].wait()
    chunk = 512
    for c in range(0, FF, chunk):
        wide = dot(normed, up[:, c : c + chunk])
        hidden = (0.5 * wide * (1.0 + lax.erf(wide * math.sqrt(0.5)))).astype(BF16)
        residual = residual + dot(hidden, down[c : c + chunk, :])
    lanes = D // 128
    for b in range(2 * LATENT):
        half, j = b // LATENT, b % LATENT
        for l in range(lanes):
            turn_scr[l, pl.ds(half * PATCHES * 4 + j, PATCHES, stride=4), :] = residual[
                b * PAD : b * PAD + PATCHES, l * 128 : (l + 1) * 128
            ]
    for half in range(2):
        for r in range(WLAT):
            for l in range(lanes):
                rows = turn_scr[l, pl.ds((half * PATCHES + r * HALF) * 4, HALF * 4), :]
                rows = rows.reshape(HALF, 4, 128)[:, :LATENT]
                out_ref[r, half * HALF : (half + 1) * HALF, :, l * 128 : (l + 1) * 128] = rows.astype(BF16)


def body(
    tokens, latent_queries, perc_query, perc_key, perc_value, perc_out, norm_gains, swin_query,
    swin_keyvalue, swin_out, mlp_up, mlp_down,
):
    whole = pl.BlockSpec(memory_space=pltpu.HBM)
    near = pl.BlockSpec(memory_space=pltpu.VMEM)
    matrices = (perc_query, perc_key, perc_value, perc_out)
    pieces = 2 * RING
    latent = pl.pallas_call(
        gather_kernel,
        out_shape=jax.ShapeDtypeStruct((ROWS, D), BF16),
        in_specs=[whole] * (1 + len(matrices)) + [near],
        out_specs=near,
        scratch_shapes=[
            pltpu.VMEM((2, RING, 2, 2, WLAT, HALF, LEVS, D), BF16),
            *[pltpu.VMEM(m.shape, m.dtype) for m in matrices],
            pltpu.VMEM((STATS, D), BF16),
            pltpu.VMEM((STATS, LATENT * D), BF16),
            pltpu.VMEM((pieces, GATHERED, STATS), F32),
            pltpu.VMEM((pieces, D // 128, GATHERED, 128), F32),
            pltpu.VMEM((2, GATHERED, STATS), BF16),
            pltpu.VMEM((RING * PAD, LATENT * D), F32),
            pltpu.VMEM((RING * PAD, STATS), F32),
            pltpu.VMEM((pieces, PAD, LATENT * D), F32),
            pltpu.VMEM((pieces, PAD, STATS), F32),
            pltpu.VMEM((pieces, PAD, LATENT * D), BF16),
            pltpu.VMEM((pieces, PAD, LATENT * D), BF16),
            pltpu.VMEM((pieces, PAD, STATS), F32),
            pltpu.VMEM((pieces, PAD, STATS), F32),
            pltpu.VMEM((pieces, PAD, LATENT * D), BF16),
            pltpu.VMEM((2, RING, PAD, LATENT * D), BF16),
            pltpu.VMEM((pieces, PAD, STATS), F32),
            pltpu.VMEM((2, RING, PAD, STATS), F32),
            pltpu.VMEM((ROWS, D), F32),
            pltpu.SemaphoreType.DMA((len(matrices),)),
            pltpu.SemaphoreType.DMA((2, RING)),
            pltpu.SemaphoreType.DMA((2, RING)),
            pltpu.SemaphoreType.DMA((2, RING)),
            pltpu.SemaphoreType.DMA((pieces,)),
            pltpu.SemaphoreType.DMA((pieces,)),
            pltpu.SemaphoreType.DMA((pieces,)),
            pltpu.SemaphoreType.DMA((pieces,)),
            pltpu.SemaphoreType.DMA((pieces,)),
            pltpu.SemaphoreType.DMA((2,)),
            pltpu.SemaphoreType.DMA((pieces,)),
            pltpu.SemaphoreType.DMA((2,)),
        ],
        compiler_params=pltpu.CompilerParams(
            collective_id=0, has_side_effects=True, vmem_limit_bytes=107 * 512 * 1024
        ),
        cost_estimate=pl.CostEstimate(
            flops=8_000_000_000, bytes_accessed=100_000_000, transcendentals=0
        ),
    )(tokens, *matrices, latent_queries)
    block = (swin_query, swin_keyvalue, swin_out, mlp_up, mlp_down)
    return pl.pallas_call(
        window_kernel,
        out_shape=jax.ShapeDtypeStruct((WLAT, 2 * HALF, LATENT, D), BF16),
        in_specs=[near, near] + [whole] * len(block),
        out_specs=near,
        scratch_shapes=[
            *[pltpu.VMEM(m.shape, m.dtype) for m in block],
            pltpu.VMEM((D, ROWS), BF16),
            pltpu.VMEM((D, ROWS), F32),
            pltpu.VMEM((D // 128, 2 * PATCHES * 4, 128), F32),
            pltpu.SemaphoreType.DMA((len(block),)),
        ],
        compiler_params=pltpu.CompilerParams(vmem_limit_bytes=40 * 1024 * 1024),
        cost_estimate=pl.CostEstimate(
            flops=2_000_000_000, bytes_accessed=7_000_000, transcendentals=0
        ),
    )(latent, norm_gains, *block)


def solution(mesh):
    placed = (P(None, "tile", "var", None), P(), P(), P(), P(), P(), P(), P(), P(), P(), P(), P())
    return jax.shard_map(
        body, mesh=mesh, in_specs=placed, out_specs=P("var", "tile", None, None), check_vma=False
    )
```

```python
import functools
import math

import jax
import jax.numpy as jnp
from jax import lax
from jax.experimental import pallas as pl
from jax.experimental.pallas import tpu as pltpu
from jax.sharding import PartitionSpec as P

F32 = jnp.float32
BF16 = jnp.bfloat16
D = 512
HEADS = 16
HD = 32
LATENT = 3
LEVS = 4
WLAT = 6
HALF = 6
RING = 4
N_VAR = RING * RING
N_TILE = 8
FF = 2048
PATCHES = WLAT * HALF
BOTH = 2 * PATCHES
GATHERED = 2 * BOTH * LEVS
PAD = 40
ROWS = 2 * LATENT * PAD
STATS = 128
FULL = 32
WIDTH = LATENT * D + 256
FOLD = 24
MESH = pl.DeviceIdType.MESH
epsilon = 1e-05


def last_by_last(a, b):
    return lax.dot_general(a, b, (((1,), (1,)), ((), ())), preferred_element_type=F32)


def dot(a, b):
    return jnp.dot(a, b, preferred_element_type=F32)


def layer_norm(values, gain_row):
    average = jnp.mean(values, axis=-1, keepdims=True)
    centred = values - average
    spread = jnp.mean(centred * centred, axis=-1, keepdims=True)
    return centred * lax.rsqrt(spread + epsilon) * gain_row


def split(values, terms):
    parts = []
    for _ in range(terms):
        part = values.astype(BF16)
        parts.append(part)
        values = values - part.astype(F32)
    return parts


def gather_kernel(
    tokens, w_pq, w_pk, w_pv, w_po, lq_ref,
    out_ref,
    buf, pq, pk, pv, po,
    kp_scr, ex_scr, s_scr, v_scr, p_scr, px_scr, sc_scr, keep, kstat, t_scr, snum, rnum, sstat, rstat,
    fnum, gnum, fstat, gstat, att_scr,
    w_sem, own_sem, tok_send, tok_recv, num_send, num_recv, stat_send, stat_recv,
    far_send, far_recv, fst_send, fst_recv,
):
    var = lax.axis_index("var")
    tile = lax.axis_index("tile")
    y, x = var // RING, var % RING
    west = lax.rem(tile + N_TILE - 1, N_TILE)
    east = lax.rem(tile + 1, N_TILE)

    barrier = pltpu.get_barrier_semaphore()

    def greet(there, at):
        pl.semaphore_signal(
            barrier, inc=1, device_id={"var": there, "tile": at}, device_id_type=MESH
        )

    for d in (1, 3):
        greet(y * RING + lax.rem(x + d, RING), tile)
    for d in (1, 2, 3):
        greet(lax.rem(y + d, RING) * RING + x, tile)
    for d in range(RING):
        greet(y * RING + lax.rem(x + d, RING), east)

    def slot_of(half, k):
        return lax.rem((y if half == 0 else x) + 1 + k, RING)

    def partners(half, slot):
        a = x if half == 0 else y
        odd = lax.rem(slot, 2)
        one, three = a + 1 - 2 * lax.rem(a, 2), 3 - a
        return one + odd * (three - one), three + odd * (one - three)

    def along(half, place):
        return y * RING + place if half == 0 else place * RING + x

    def send_tokens(half, k, own=False):
        slot = slot_of(half, k)
        a = x if half == 0 else y
        lon = HALF if half == 0 else 0
        first, second = partners(half, slot)
        for which, owner in ((0, a), (1, second)) if own else ((0, first), (1, lax.rem(a + 2, RING))):
            src_at = 0 if own else 1
            band = slot * RING + owner if half == 0 else owner * RING + slot
            upper = WLAT * band + WLAT // 2
            lower = lax.rem(WLAT * band + WLAT, WLAT * N_VAR)
            for part, row in ((0, upper), (1, lower)):
                src = tokens.at[pl.ds(row, WLAT // 2), pl.ds(lon, HALF)]
                dst = buf.at[half, slot, src_at, which, pl.ds(part * (WLAT // 2), WLAT // 2)]
                if own:
                    pltpu.make_async_copy(src, dst, own_sem.at[half, slot]).start()
                else:
                    pltpu.make_async_remote_copy(
                        src_ref=src,
                        dst_ref=dst,
                        send_sem=tok_send.at[half, slot],
                        recv_sem=tok_recv.at[half, slot],
                        device_id={"var": along(half, first), "tile": tile},
                        device_id_type=MESH,
                    ).start()

    weights = ((w_pq, pq), (w_pk, pk), (w_pv, pv), (w_po, po))
    loads = [pltpu.make_async_copy(src, dst, w_sem.at[i]) for i, (src, dst) in enumerate(weights)]
    for load in loads:
        load.start()
    order = [(half, k) for k in range(RING) for half in (1, 0)]
    for half, k in order:
        send_tokens(half, k, own=True)
    pl.semaphore_wait(barrier, 9)
    for half, k in order[:4]:
        send_tokens(half, k)

    row = lax.broadcasted_iota(jnp.int32, (STATS, LATENT * D), 0)
    col = lax.broadcasted_iota(jnp.int32, (STATS, LATENT * D), 1)
    ex_scr[...] = jnp.where(
        (row & (STATS // 2 - 1)) == (col >> 9) * HEADS + ((col & (D - 1)) >> 5), 1.0, 0.0
    ).astype(BF16)
    loads[0].wait()
    queries = dot(lq_ref[...], pq[...])
    head_row = lax.broadcasted_iota(jnp.int32, (HEADS, D), 0)
    head_col = lax.broadcasted_iota(jnp.int32, (HEADS, D), 1) >> 5
    spread = jnp.concatenate(
        [jnp.where(head_row == head_col, queries[j : j + 1], 0.0) for j in range(LATENT)]
        + [jnp.zeros((STATS - LATENT * HEADS, D), F32)],
        axis=0,
    )
    loads[1].wait()
    probe = sum(last_by_last(part, pk[...]) for part in split(spread, 3))
    kp_scr[...] = (probe / math.sqrt(HD)).astype(BF16)
    loads[2].wait()

    lane = lax.broadcasted_iota(jnp.int32, (PAD, STATS), 1)

    def widen(scales):
        head = scales.astype(BF16).astype(F32)
        rest = pltpu.roll(scales - head, STATS // 2, 1)
        low = lax.broadcasted_iota(jnp.int32, scales.shape, 1) < STATS // 2
        return dot(jnp.where(low, head, rest).astype(BF16), ex_scr[...])

    def fold(stats):
        low = lax.broadcasted_iota(jnp.int32, (PAD - FOLD, STATS), 1) < STATS // 2
        rest = pltpu.roll(stats[FOLD:PAD], STATS // 2, 1)
        return jnp.concatenate(
            [jnp.where(low, stats[: PAD - FOLD], rest), stats[PAD - FOLD : FOLD]], axis=0
        )

    def unfold(stats):
        return jnp.concatenate([stats, pltpu.roll(stats[: PAD - FOLD], STATS // 2, 1)], axis=0)

    def pack(ref, at, group, rows):
        rows = rows.astype(BF16)
        ref[at, 0:FULL, group * 256 : (group + 1) * 256] = rows[:FULL]
        ref[at, group * 4 : group * 4 + 4, LATENT * D :] = rows[FULL:PATCHES]

    def unpack(rows, group):
        rest = rows[:, LATENT * D :].astype(F32)[group * 4 : group * 4 + 4]
        return jnp.concatenate(
            [rows[:, group * 256 : (group + 1) * 256].astype(F32), rest], axis=0
        )

    lane_wide = lax.broadcasted_iota(jnp.int32, (BOTH, STATS), 1)

    def products(half, k, src):
        index = half * RING + k
        rows = buf[half, slot_of(half, k), src].reshape(BOTH * LEVS, D)
        at = src * BOTH * LEVS
        s_scr[index, at : at + BOTH * LEVS, :] = last_by_last(rows, kp_scr[...])
        values = dot(rows, pv[...])
        for lanes in range(D // 128):
            v_scr[index, lanes, at : at + BOTH * LEVS, :] = values[:, lanes * 128 : (lanes + 1) * 128]

    def arrive(half, k):
        slot = slot_of(half, k)
        arrived = buf.at[half, slot, 1]
        pltpu.make_async_copy(arrived, arrived, tok_recv.at[half, slot]).wait()
        if k + 2 < RING:
            send_tokens(half, k + 2)

    def work(half, k):
        slot = slot_of(half, k)
        index = half * RING + k
        members = [
            pl.ds(src * BOTH * LEVS + t, BOTH, stride=LEVS)
            for src in range(2)
            for t in range(LEVS)
        ]
        scores = [s_scr[index, member, :] for member in members]
        top = functools.reduce(jnp.maximum, scores)
        weights = [jnp.exp(score - top) for score in scores]
        total = sum(weights)
        inverse = jnp.where(lane_wide < STATS // 2, 1.0 / total, 0.0)
        for n, weight in enumerate(weights):
            p_scr[half, n * BOTH : (n + 1) * BOTH, :] = (weight * inverse).astype(BF16)
        stats = top + jnp.log(total)
        kstat[index, 0:PATCHES, :] = stats[:PATCHES]
        t_scr[half, 0:PATCHES, :] = stats[PATCHES:]
        sstat[index] = fold(t_scr[half])
        for at in range(0, LATENT * D, 256):
            wide = dot(p_scr[half], ex_scr[:, at : at + 256])
            sides = [
                sum(
                    v_scr[index, (at % D) // 128 + side, member, :]
                    * wide[n * BOTH : (n + 1) * BOTH, side * 128 : (side + 1) * 128]
                    for n, member in enumerate(members)
                )
                for side in range(2)
            ]
            here = jnp.concatenate(sides, axis=1)
            keep[index, 0:PATCHES, at : at + 256] = here[:PATCHES]
            pack(snum, index, at // 256, here[PATCHES:])
        _, second = partners(half, slot)
        for src, dst, send, recv in (
            (snum, rnum, num_send, num_recv), (sstat, rstat, stat_send, stat_recv)
        ):
            pltpu.make_async_remote_copy(
                src_ref=src.at[index],
                dst_ref=dst.at[index],
                send_sem=send.at[index],
                recv_sem=recv.at[index],
                device_id={"var": along(half, second), "tile": tile},
                device_id_type=MESH,
            ).start()

    def merge(half, k):
        slot = slot_of(half, k)
        index = half * RING + k
        pltpu.make_async_copy(rstat.at[index], rstat.at[index], stat_recv.at[index]).wait()
        mine, theirs = kstat[index], unfold(rstat[index])
        top = jnp.maximum(mine, theirs)
        my_scale, their_scale = jnp.exp(mine - top), jnp.exp(theirs - top)
        total = my_scale + their_scale
        fstat[index] = fold(top + jnp.log(total))
        scales = widen(jnp.concatenate([my_scale / total, their_scale / total], axis=0))
        pltpu.make_async_copy(rnum.at[index], rnum.at[index], num_recv.at[index]).wait()
        theirs = rnum[index]
        for group in range(LATENT * D // 256):
            columns = slice(group * 256, (group + 1) * 256)
            merged = (
                keep[index, 0:PATCHES, columns] * scales[0:PATCHES, columns]
                + unpack(theirs, group) * scales[PAD : PAD + PATCHES, columns]
            )
            pack(fnum, index, group, merged)
        source = y if half == 0 else x
        there = slot * RING + x if half == 0 else y * RING + slot
        for src, dst, send, recv in (
            (fnum, gnum, far_send, far_recv), (fstat, gstat, fst_send, fst_recv)
        ):
            if half == 0 and k == RING - 1:
                pltpu.make_async_copy(src.at[index], dst.at[half, source], recv.at[half]).start()
            else:
                pltpu.make_async_remote_copy(
                    src_ref=src.at[index],
                    dst_ref=dst.at[half, source],
                    send_sem=send.at[index],
                    recv_sem=recv.at[half],
                    device_id={"var": there, "tile": tile if half == 0 else west},
                    device_id_type=MESH,
                ).start()

    for half, k in order:
        own = buf.at[half, slot_of(half, k), 0]
        pltpu.make_async_copy(own, own, own_sem.at[half, slot_of(half, k)]).wait()
        products(half, k, 0)
    for k in range(RING):
        for half in (1, 0):
            arrive(half, k)
        for half in (1, 0):
            products(half, k, 1)
        for half in (1, 0):
            work(half, k)
            if k > 0:
                merge(half, k - 1)
    for half in (1, 0):
        merge(half, RING - 1)

    att_scr[...] = jnp.zeros_like(att_scr)
    inside = lax.broadcasted_iota(jnp.int32, (PAD, STATS), 0) < PATCHES
    for half in range(2):
        pltpu.make_async_copy(gnum.at[half], gnum.at[half], far_recv.at[half]).wait()
        pltpu.make_async_copy(gstat.at[half], gstat.at[half], fst_recv.at[half]).wait()
        stats = [unfold(gstat[half, src]) for src in range(RING)]
        top = functools.reduce(jnp.maximum, stats)
        scales = [jnp.exp(stat - top) for stat in stats]
        denominator = sum(scales)
        valid = (lane < LATENT * HEADS) & inside
        for src in range(RING):
            sc_scr[pl.ds(src * PAD, PAD), :] = jnp.where(valid, scales[src] / denominator, 0.0)
        px_scr[0 : RING * PAD] = widen(sc_scr[...])
        gathered = [gnum[half, src] for src in range(RING)]
        for group in range(LATENT * D // 256):
            share = sum(
                unpack(gathered[src], group)
                * px_scr[pl.ds(src * PAD, PATCHES), group * 256 : (group + 1) * 256]
                for src in range(RING)
            )
            at = (half * LATENT + group // 2) * PAD
            att_scr[at : at + PATCHES, group % 2 * 256 : (group % 2 + 1) * 256] = share
    loads[3].wait()
    latent = dot(att_scr[...].astype(BF16), po[...])
    start = jnp.concatenate(
        [
            jnp.broadcast_to(lq_ref[j : j + 1, :].astype(F32), (PAD, D))
            for _ in range(2)
            for j in range(LATENT)
        ],
        axis=0,
    )
    out_ref[...] = (start + latent).astype(BF16)

    for half in range(2):
        for k in range(RING):
            slot = slot_of(half, k)
            index = half * RING + k
            sent = buf.at[half, slot, 1]
            pltpu.make_async_copy(sent, sent, tok_send.at[half, slot]).wait()
            pltpu.make_async_copy(snum.at[index], snum.at[index], num_send.at[index]).wait()
            pltpu.make_async_copy(sstat.at[index], sstat.at[index], stat_send.at[index]).wait()
            if half == 1 or k < RING - 1:
                pltpu.make_async_copy(fnum.at[index], fnum.at[index], far_send.at[index]).wait()
                pltpu.make_async_copy(fstat.at[index], fstat.at[index], fst_send.at[index]).wait()


def window_kernel(
    latent_ref, gains_ref, w_sq, w_skv, w_so, w_up, w_down, out_ref,
    sq, skv, so, up, down, vt_scr, mix_scr, turn_scr, w_sem,
):
    weights = ((w_sq, sq), (w_skv, skv), (w_so, so), (w_up, up), (w_down, down))
    loads = [pltpu.make_async_copy(src, dst, w_sem.at[i]) for i, (src, dst) in enumerate(weights)]
    for load in loads:
        load.start()
    var = lax.axis_index("var")
    residual = latent_ref[...].astype(F32)
    normed = layer_norm(residual, gains_ref[0:1, :]).astype(BF16)
    loads[0].wait()
    queries = dot(normed, sq[...]).astype(BF16)
    loads[1].wait()
    keyvals = dot(normed, skv[...])
    keys = keyvals[:, :D]
    vt_scr[...] = jnp.transpose(keyvals[:, D:]).astype(BF16)

    def place(shape, axis):
        index = lax.broadcasted_iota(jnp.int32, shape, axis)
        for b in range(2 * LATENT - 1, 0, -1):
            index = jnp.where(index >= b * PAD, index - b * PAD, index)
        return index

    key_at = place((ROWS, ROWS), 0)
    query_at = place((ROWS, ROWS), 1)
    cut = WLAT // 2 * HALF
    apart = (key_at >= cut) != (query_at >= cut)
    excluded = (key_at >= PATCHES) | (apart & (var == N_VAR - 1))
    bias = jnp.where(excluded, -jnp.inf, 0.0)
    lane_head = lax.broadcasted_iota(jnp.int32, (ROWS, 256), 1) >> 5
    for h in range(HEADS):
        at = h // 8 * 256
        key_part = jnp.where(lane_head == h % 8, keys[:, at : at + 256], 0.0).astype(BF16)
        logits = last_by_last(key_part, queries[:, at : at + 256]) + bias
        top = jnp.max(logits, axis=0, keepdims=True)
        exponent = jnp.exp2((logits - top) * (math.log2(math.e) / math.sqrt(HD)))
        probs = (exponent * (1.0 / jnp.sum(exponent, axis=0, keepdims=True))).astype(BF16)
        mix_scr[h * HD : (h + 1) * HD, :] = dot(vt_scr[h * HD : (h + 1) * HD, :], probs)
    mixed = jnp.transpose(mix_scr[...]).astype(BF16)
    loads[2].wait()
    residual = residual + dot(mixed, so[...])
    normed = layer_norm(residual, gains_ref[1:2, :]).astype(BF16)
    loads[3].wait()
    loads[4].wait()
    chunk = 512
    for c in range(0, FF, chunk):
        wide = dot(normed, up[:, c : c + chunk])
        hidden = (0.5 * wide * (1.0 + lax.erf(wide * math.sqrt(0.5)))).astype(BF16)
        residual = residual + dot(hidden, down[c : c + chunk, :])
    lanes = D // 128
    for b in range(2 * LATENT):
        half, j = b // LATENT, b % LATENT
        for l in range(lanes):
            turn_scr[l, pl.ds(half * PATCHES * 4 + j, PATCHES, stride=4), :] = residual[
                b * PAD : b * PAD + PATCHES, l * 128 : (l + 1) * 128
            ]
    for half in range(2):
        for r in range(WLAT):
            for l in range(lanes):
                rows = turn_scr[l, pl.ds((half * PATCHES + r * HALF) * 4, HALF * 4), :]
                rows = rows.reshape(HALF, 4, 128)[:, :LATENT]
                out_ref[r, half * HALF : (half + 1) * HALF, :, l * 128 : (l + 1) * 128] = rows.astype(BF16)


def body(
    tokens, latent_queries, perc_query, perc_key, perc_value, perc_out, norm_gains, swin_query,
    swin_keyvalue, swin_out, mlp_up, mlp_down,
):
    whole = pl.BlockSpec(memory_space=pltpu.HBM)
    near = pl.BlockSpec(memory_space=pltpu.VMEM)
    matrices = (perc_query, perc_key, perc_value, perc_out)
    pieces = 2 * RING
    latent = pl.pallas_call(
        gather_kernel,
        out_shape=jax.ShapeDtypeStruct((ROWS, D), BF16),
        in_specs=[whole] * (1 + len(matrices)) + [near],
        out_specs=near,
        scratch_shapes=[
            pltpu.VMEM((2, RING, 2, 2, WLAT, HALF, LEVS, D), BF16),
            *[pltpu.VMEM(m.shape, m.dtype) for m in matrices],
            pltpu.VMEM((STATS, D), BF16),
            pltpu.VMEM((STATS, LATENT * D), BF16),
            pltpu.VMEM((pieces, GATHERED, STATS), F32),
            pltpu.VMEM((pieces, D // 128, GATHERED, 128), F32),
            pltpu.VMEM((2, GATHERED, STATS), BF16),
            pltpu.VMEM((RING * PAD, LATENT * D), F32),
            pltpu.VMEM((RING * PAD, STATS), F32),
            pltpu.VMEM((pieces, PAD, LATENT * D), F32),
            pltpu.VMEM((pieces, PAD, STATS), F32),
            pltpu.VMEM((2, PAD, STATS), F32),
            pltpu.VMEM((pieces, FULL, WIDTH), BF16),
            pltpu.VMEM((pieces, FULL, WIDTH), BF16),
            pltpu.VMEM((pieces, FOLD, STATS), F32),
            pltpu.VMEM((pieces, FOLD, STATS), F32),
            pltpu.VMEM((pieces, FULL, WIDTH), BF16),
            pltpu.VMEM((2, RING, FULL, WIDTH), BF16),
            pltpu.VMEM((pieces, FOLD, STATS), F32),
            pltpu.VMEM((2, RING, FOLD, STATS), F32),
            pltpu.VMEM((ROWS, D), F32),
            pltpu.SemaphoreType.DMA((len(matrices),)),
            pltpu.SemaphoreType.DMA((2, RING)),
            pltpu.SemaphoreType.DMA((2, RING)),
            pltpu.SemaphoreType.DMA((2, RING)),
            pltpu.SemaphoreType.DMA((pieces,)),
            pltpu.SemaphoreType.DMA((pieces,)),
            pltpu.SemaphoreType.DMA((pieces,)),
            pltpu.SemaphoreType.DMA((pieces,)),
            pltpu.SemaphoreType.DMA((pieces,)),
            pltpu.SemaphoreType.DMA((2,)),
            pltpu.SemaphoreType.DMA((pieces,)),
            pltpu.SemaphoreType.DMA((2,)),
        ],
        compiler_params=pltpu.CompilerParams(
            collective_id=0, has_side_effects=True, vmem_limit_bytes=107 * 512 * 1024
        ),
        cost_estimate=pl.CostEstimate(
            flops=8_000_000_000, bytes_accessed=100_000_000, transcendentals=0
        ),
    )(tokens, *matrices, latent_queries)
    block = (swin_query, swin_keyvalue, swin_out, mlp_up, mlp_down)
    return pl.pallas_call(
        window_kernel,
        out_shape=jax.ShapeDtypeStruct((WLAT, 2 * HALF, LATENT, D), BF16),
        in_specs=[near, near] + [whole] * len(block),
        out_specs=near,
        scratch_shapes=[
            *[pltpu.VMEM(m.shape, m.dtype) for m in block],
            pltpu.VMEM((D, ROWS), BF16),
            pltpu.VMEM((D, ROWS), F32),
            pltpu.VMEM((D // 128, 2 * PATCHES * 4, 128), F32),
            pltpu.SemaphoreType.DMA((len(block),)),
        ],
        compiler_params=pltpu.CompilerParams(vmem_limit_bytes=40 * 1024 * 1024),
        cost_estimate=pl.CostEstimate(
            flops=2_000_000_000, bytes_accessed=7_000_000, transcendentals=0
        ),
    )(latent, norm_gains, *block)


def solution(mesh):
    placed = (P(None, "tile", "var", None), P(), P(), P(), P(), P(), P(), P(), P(), P(), P(), P())
    return jax.shard_map(
        body, mesh=mesh, in_specs=placed, out_specs=P("var", "tile", None, None), check_vma=False
    )
```

```python
import functools
import math

import jax
import jax.numpy as jnp
from jax import lax
from jax.experimental import pallas as pl
from jax.experimental.pallas import tpu as pltpu
from jax.sharding import PartitionSpec as P

F32 = jnp.float32
BF16 = jnp.bfloat16
D = 512
HEADS = 16
HD = 32
LATENT = 3
LEVS = 4
WLAT = 6
HALF = 6
RING = 4
N_VAR = RING * RING
N_TILE = 8
FF = 2048
PATCHES = WLAT * HALF
BOTH = 2 * PATCHES
GATHERED = 2 * BOTH * LEVS
PAD = 40
ROWS = 2 * LATENT * PATCHES
STATS = 128
FULL = 32
WIDTH = LATENT * D + 256
FOLD = 24
MESH = pl.DeviceIdType.MESH
epsilon = 1e-05


def last_by_last(a, b):
    return lax.dot_general(a, b, (((1,), (1,)), ((), ())), preferred_element_type=F32)


def dot(a, b):
    return jnp.dot(a, b, preferred_element_type=F32)


def layer_norm(values, gain_row):
    average = jnp.mean(values, axis=-1, keepdims=True)
    centred = values - average
    spread = jnp.mean(centred * centred, axis=-1, keepdims=True)
    return centred * lax.rsqrt(spread + epsilon) * gain_row


def split(values, terms):
    parts = []
    for _ in range(terms):
        part = values.astype(BF16)
        parts.append(part)
        values = values - part.astype(F32)
    return parts


def gather_kernel(
    tokens, w_pq, w_pk, w_pv, w_po, lq_ref,
    out_ref,
    buf, pq, pk, pv, po, lq_scr,
    kp_scr, ex_scr, s_scr, v_scr, p_scr, px_scr, sc_scr, keep, kstat, t_scr, snum, rnum, sstat, rstat,
    fnum, gnum, fstat, gstat, att_scr,
    w_sem, own_sem, tok_send, tok_recv, num_send, num_recv, stat_send, stat_recv,
    far_send, far_recv, fst_send, fst_recv,
):
    var = lax.axis_index("var")
    tile = lax.axis_index("tile")
    y, x = var // RING, var % RING
    west = lax.rem(tile + N_TILE - 1, N_TILE)
    east = lax.rem(tile + 1, N_TILE)

    barrier = pltpu.get_barrier_semaphore()

    def greet(there, at):
        pl.semaphore_signal(
            barrier, inc=1, device_id={"var": there, "tile": at}, device_id_type=MESH
        )

    for d in (1, 3):
        greet(y * RING + lax.rem(x + d, RING), tile)
    for d in (1, 2, 3):
        greet(lax.rem(y + d, RING) * RING + x, tile)
    for d in range(RING):
        greet(y * RING + lax.rem(x + d, RING), east)

    def slot_of(half, k):
        return lax.rem((y if half == 0 else x) + 1 + k, RING)

    def partners(half, slot):
        a = x if half == 0 else y
        odd = lax.rem(slot, 2)
        one, three = a + 1 - 2 * lax.rem(a, 2), 3 - a
        return one + odd * (three - one), three + odd * (one - three)

    def along(half, place):
        return y * RING + place if half == 0 else place * RING + x

    def send_tokens(half, k, own=False):
        slot = slot_of(half, k)
        a = x if half == 0 else y
        lon = HALF if half == 0 else 0
        first, second = partners(half, slot)
        for which, owner in ((0, a), (1, second)) if own else ((0, first), (1, lax.rem(a + 2, RING))):
            src_at = 0 if own else 1
            band = slot * RING + owner if half == 0 else owner * RING + slot
            upper = WLAT * band + WLAT // 2
            lower = lax.rem(WLAT * band + WLAT, WLAT * N_VAR)
            for part, row in ((0, upper), (1, lower)):
                src = tokens.at[pl.ds(row, WLAT // 2), pl.ds(lon, HALF)]
                dst = buf.at[half, slot, src_at, which, pl.ds(part * (WLAT // 2), WLAT // 2)]
                if own:
                    pltpu.make_async_copy(src, dst, own_sem.at[half, slot]).start()
                else:
                    pltpu.make_async_remote_copy(
                        src_ref=src,
                        dst_ref=dst,
                        send_sem=tok_send.at[half, slot],
                        recv_sem=tok_recv.at[half, slot],
                        device_id={"var": along(half, first), "tile": tile},
                        device_id_type=MESH,
                    ).start()

    weights = ((w_pq, pq), (w_pk, pk), (w_pv, pv), (w_po, po), (lq_ref, lq_scr))
    loads = [pltpu.make_async_copy(src, dst, w_sem.at[i]) for i, (src, dst) in enumerate(weights)]
    for load in loads:
        load.start()
    order = [(half, k) for k in range(RING) for half in (1, 0)]
    for half, k in order:
        send_tokens(half, k, own=True)
    pl.semaphore_wait(barrier, 9)
    for half, k in order[:4]:
        send_tokens(half, k)

    row = lax.broadcasted_iota(jnp.int32, (STATS, LATENT * D), 0)
    col = lax.broadcasted_iota(jnp.int32, (STATS, LATENT * D), 1)
    ex_scr[...] = jnp.where(
        (row & (STATS // 2 - 1)) == (col >> 9) * HEADS + ((col & (D - 1)) >> 5), 1.0, 0.0
    ).astype(BF16)
    loads[0].wait()
    loads[4].wait()
    queries = dot(lq_scr[...], pq[...])
    head_row = lax.broadcasted_iota(jnp.int32, (HEADS, D), 0)
    head_col = lax.broadcasted_iota(jnp.int32, (HEADS, D), 1) >> 5
    spread = jnp.concatenate(
        [jnp.where(head_row == head_col, queries[j : j + 1], 0.0) for j in range(LATENT)]
        + [jnp.zeros((STATS - LATENT * HEADS, D), F32)],
        axis=0,
    )
    loads[1].wait()
    probe = sum(last_by_last(part, pk[...]) for part in split(spread, 3))
    kp_scr[...] = (probe / math.sqrt(HD)).astype(BF16)
    loads[2].wait()

    lane = lax.broadcasted_iota(jnp.int32, (PAD, STATS), 1)

    def widen(scales):
        head = scales.astype(BF16).astype(F32)
        rest = pltpu.roll(scales - head, STATS // 2, 1)
        low = lax.broadcasted_iota(jnp.int32, scales.shape, 1) < STATS // 2
        return dot(jnp.where(low, head, rest).astype(BF16), ex_scr[...])

    def fold(stats):
        low = lax.broadcasted_iota(jnp.int32, (PAD - FOLD, STATS), 1) < STATS // 2
        rest = pltpu.roll(stats[FOLD:PAD], STATS // 2, 1)
        return jnp.concatenate(
            [jnp.where(low, stats[: PAD - FOLD], rest), stats[PAD - FOLD : FOLD]], axis=0
        )

    def unfold(stats):
        return jnp.concatenate([stats, pltpu.roll(stats[: PAD - FOLD], STATS // 2, 1)], axis=0)

    def pack(ref, at, group, rows):
        rows = rows.astype(BF16)
        ref[at, 0:FULL, group * 256 : (group + 1) * 256] = rows[:FULL]
        ref[at, group * 4 : group * 4 + 4, LATENT * D :] = rows[FULL:PATCHES]

    def unpack(rows, group):
        rest = rows[:, LATENT * D :].astype(F32)[group * 4 : group * 4 + 4]
        return jnp.concatenate(
            [rows[:, group * 256 : (group + 1) * 256].astype(F32), rest], axis=0
        )

    lane_wide = lax.broadcasted_iota(jnp.int32, (BOTH, STATS), 1)

    def products(half, k, src):
        index = half * RING + k
        rows = buf[half, slot_of(half, k), src].reshape(BOTH * LEVS, D)
        at = src * BOTH * LEVS
        s_scr[index, at : at + BOTH * LEVS, :] = last_by_last(rows, kp_scr[...])
        values = dot(rows, pv[...])
        for lanes in range(D // 128):
            v_scr[index, lanes, at : at + BOTH * LEVS, :] = values[:, lanes * 128 : (lanes + 1) * 128]

    def arrive(half, k):
        slot = slot_of(half, k)
        arrived = buf.at[half, slot, 1]
        pltpu.make_async_copy(arrived, arrived, tok_recv.at[half, slot]).wait()
        if k + 2 < RING:
            send_tokens(half, k + 2)

    def work(half, k):
        slot = slot_of(half, k)
        index = half * RING + k
        members = [
            pl.ds(src * BOTH * LEVS + t, BOTH, stride=LEVS)
            for src in range(2)
            for t in range(LEVS)
        ]
        scores = [s_scr[index, member, :] for member in members]
        top = functools.reduce(jnp.maximum, scores)
        weights = [jnp.exp(score - top) for score in scores]
        total = sum(weights)
        inverse = jnp.where(lane_wide < STATS // 2, 1.0 / total, 0.0)
        for n, weight in enumerate(weights):
            p_scr[half, n * BOTH : (n + 1) * BOTH, :] = (weight * inverse).astype(BF16)
        stats = top + jnp.log(total)
        kstat[index, 0:PATCHES, :] = stats[:PATCHES]
        t_scr[half, 0:PATCHES, :] = stats[PATCHES:]
        sstat[index] = fold(t_scr[half])
        for at in range(0, LATENT * D, 256):
            wide = dot(p_scr[half], ex_scr[:, at : at + 256])
            sides = [
                sum(
                    v_scr[index, (at % D) // 128 + side, member, :]
                    * wide[n * BOTH : (n + 1) * BOTH, side * 128 : (side + 1) * 128]
                    for n, member in enumerate(members)
                )
                for side in range(2)
            ]
            here = jnp.concatenate(sides, axis=1)
            keep[index, 0:PATCHES, at : at + 256] = here[:PATCHES]
            pack(snum, index, at // 256, here[PATCHES:])
        _, second = partners(half, slot)
        for src, dst, send, recv in (
            (snum, rnum, num_send, num_recv), (sstat, rstat, stat_send, stat_recv)
        ):
            pltpu.make_async_remote_copy(
                src_ref=src.at[index],
                dst_ref=dst.at[index],
                send_sem=send.at[index],
                recv_sem=recv.at[index],
                device_id={"var": along(half, second), "tile": tile},
                device_id_type=MESH,
            ).start()

    def merge(half, k):
        slot = slot_of(half, k)
        index = half * RING + k
        pltpu.make_async_copy(rstat.at[index], rstat.at[index], stat_recv.at[index]).wait()
        mine, theirs = kstat[index], unfold(rstat[index])
        top = jnp.maximum(mine, theirs)
        my_scale, their_scale = jnp.exp(mine - top), jnp.exp(theirs - top)
        total = my_scale + their_scale
        fstat[index] = fold(top + jnp.log(total))
        scales = widen(jnp.concatenate([my_scale / total, their_scale / total], axis=0))
        pltpu.make_async_copy(rnum.at[index], rnum.at[index], num_recv.at[index]).wait()
        theirs = rnum[index]
        for group in range(LATENT * D // 256):
            columns = slice(group * 256, (group + 1) * 256)
            merged = (
                keep[index, 0:PATCHES, columns] * scales[0:PATCHES, columns]
                + unpack(theirs, group) * scales[PAD : PAD + PATCHES, columns]
            )
            pack(fnum, index, group, merged)
        source = y if half == 0 else x
        there = slot * RING + x if half == 0 else y * RING + slot
        for src, dst, send, recv in (
            (fnum, gnum, far_send, far_recv), (fstat, gstat, fst_send, fst_recv)
        ):
            if half == 0 and k == RING - 1:
                pltpu.make_async_copy(src.at[index], dst.at[half, source], recv.at[half]).start()
            else:
                pltpu.make_async_remote_copy(
                    src_ref=src.at[index],
                    dst_ref=dst.at[half, source],
                    send_sem=send.at[index],
                    recv_sem=recv.at[half],
                    device_id={"var": there, "tile": tile if half == 0 else west},
                    device_id_type=MESH,
                ).start()

    for half, k in order:
        own = buf.at[half, slot_of(half, k), 0]
        pltpu.make_async_copy(own, own, own_sem.at[half, slot_of(half, k)]).wait()
        products(half, k, 0)
    for k in range(RING):
        for half in (1, 0):
            arrive(half, k)
        for half in (1, 0):
            products(half, k, 1)
        for half in (1, 0):
            work(half, k)
            if k > 0:
                merge(half, k - 1)
    for half in (1, 0):
        merge(half, RING - 1)

    inside = lax.broadcasted_iota(jnp.int32, (PAD, STATS), 0) < PATCHES
    for half in range(2):
        pltpu.make_async_copy(gnum.at[half], gnum.at[half], far_recv.at[half]).wait()
        pltpu.make_async_copy(gstat.at[half], gstat.at[half], fst_recv.at[half]).wait()
        stats = [unfold(gstat[half, src]) for src in range(RING)]
        top = functools.reduce(jnp.maximum, stats)
        scales = [jnp.exp(stat - top) for stat in stats]
        denominator = sum(scales)
        valid = (lane < LATENT * HEADS) & inside
        for src in range(RING):
            sc_scr[pl.ds(src * PAD, PAD), :] = jnp.where(valid, scales[src] / denominator, 0.0)
        px_scr[0 : RING * PAD] = widen(sc_scr[...])
        gathered = [gnum[half, src] for src in range(RING)]
        for group in range(LATENT * D // 256):
            share = sum(
                unpack(gathered[src], group)
                * px_scr[pl.ds(src * PAD, PATCHES), group * 256 : (group + 1) * 256]
                for src in range(RING)
            )
            at = (half * LATENT + group // 2) * PATCHES
            att_scr[at : at + PATCHES, group % 2 * 256 : (group % 2 + 1) * 256] = share
    loads[3].wait()
    latent = dot(att_scr[...].astype(BF16), po[...])
    token = lax.broadcasted_iota(jnp.int32, (ROWS, D), 0)
    block = sum((token >= b * PATCHES).astype(jnp.int32) for b in range(1, 2 * LATENT))
    level = jnp.where(block >= LATENT, block - LATENT, block)
    start = jnp.zeros((ROWS, D), F32)
    for j in range(LATENT):
        start = jnp.where(level == j, lq_scr[j : j + 1, :].astype(F32), start)
    out_ref[...] = (start + latent).astype(BF16)

    for half in range(2):
        for k in range(RING):
            slot = slot_of(half, k)
            index = half * RING + k
            sent = buf.at[half, slot, 1]
            pltpu.make_async_copy(sent, sent, tok_send.at[half, slot]).wait()
            pltpu.make_async_copy(snum.at[index], snum.at[index], num_send.at[index]).wait()
            pltpu.make_async_copy(sstat.at[index], sstat.at[index], stat_send.at[index]).wait()
            if half == 1 or k < RING - 1:
                pltpu.make_async_copy(fnum.at[index], fnum.at[index], far_send.at[index]).wait()
                pltpu.make_async_copy(fstat.at[index], fstat.at[index], fst_send.at[index]).wait()


def window_kernel(
    latent_ref, gains_ref, w_sq, w_skv, w_so, w_up, w_down, out_ref,
    sq, skv, so, up, down, vt_scr, mix_scr, turn_scr, w_sem,
):
    weights = ((w_sq, sq), (w_skv, skv), (w_so, so), (w_up, up), (w_down, down))
    loads = [pltpu.make_async_copy(src, dst, w_sem.at[i]) for i, (src, dst) in enumerate(weights)]
    for load in loads:
        load.start()
    var = lax.axis_index("var")
    residual = latent_ref[...].astype(F32)
    normed = layer_norm(residual, gains_ref[0:1, :]).astype(BF16)
    loads[0].wait()
    queries = dot(normed, sq[...]).astype(BF16)
    loads[1].wait()
    keyvals = dot(normed, skv[...])
    keys = keyvals[:, :D]
    vt_scr[...] = jnp.transpose(keyvals[:, D:]).astype(BF16)

    def southern(shape, axis):
        index = lax.broadcasted_iota(jnp.int32, shape, axis)
        for b in range(2 * LATENT - 1, 0, -1):
            index = jnp.where(index >= b * PATCHES, index - b * PATCHES, index)
        return index >= WLAT // 2 * HALF

    apart = southern((ROWS, ROWS), 0) != southern((ROWS, ROWS), 1)
    bias = jnp.where(apart & (var == N_VAR - 1), -jnp.inf, 0.0)
    lane_head = lax.broadcasted_iota(jnp.int32, (ROWS, 256), 1) >> 5
    for h in range(HEADS):
        at = h // 8 * 256
        key_part = jnp.where(lane_head == h % 8, keys[:, at : at + 256], 0.0).astype(BF16)
        logits = last_by_last(key_part, queries[:, at : at + 256]) + bias
        top = jnp.max(logits, axis=0, keepdims=True)
        exponent = jnp.exp2((logits - top) * (math.log2(math.e) / math.sqrt(HD)))
        probs = (exponent * (1.0 / jnp.sum(exponent, axis=0, keepdims=True))).astype(BF16)
        mix_scr[h * HD : (h + 1) * HD, :] = dot(vt_scr[h * HD : (h + 1) * HD, :], probs)
    mixed = jnp.transpose(mix_scr[...]).astype(BF16)
    loads[2].wait()
    residual = residual + dot(mixed, so[...])
    normed = layer_norm(residual, gains_ref[1:2, :]).astype(BF16)
    loads[3].wait()
    loads[4].wait()
    chunk = 512
    for c in range(0, FF, chunk):
        wide = dot(normed, up[:, c : c + chunk])
        hidden = (0.5 * wide * (1.0 + lax.erf(wide * math.sqrt(0.5)))).astype(BF16)
        residual = residual + dot(hidden, down[c : c + chunk, :])
    lanes = D // 128
    for b in range(2 * LATENT):
        half, j = b // LATENT, b % LATENT
        for l in range(lanes):
            turn_scr[l, pl.ds(half * PATCHES * 4 + j, PATCHES, stride=4), :] = residual[
                b * PATCHES : (b + 1) * PATCHES, l * 128 : (l + 1) * 128
            ]
    for half in range(2):
        for r in range(WLAT):
            for l in range(lanes):
                rows = turn_scr[l, pl.ds((half * PATCHES + r * HALF) * 4, HALF * 4), :]
                rows = rows.reshape(HALF, 4, 128)[:, :LATENT]
                out_ref[r, half * HALF : (half + 1) * HALF, :, l * 128 : (l + 1) * 128] = rows.astype(BF16)


def body(
    tokens, latent_queries, perc_query, perc_key, perc_value, perc_out, norm_gains, swin_query,
    swin_keyvalue, swin_out, mlp_up, mlp_down,
):
    whole = pl.BlockSpec(memory_space=pltpu.HBM)
    near = pl.BlockSpec(memory_space=pltpu.VMEM)
    matrices = (perc_query, perc_key, perc_value, perc_out)
    pieces = 2 * RING
    latent = pl.pallas_call(
        gather_kernel,
        out_shape=jax.ShapeDtypeStruct((ROWS, D), BF16),
        in_specs=[whole] * (2 + len(matrices)),
        out_specs=near,
        scratch_shapes=[
            pltpu.VMEM((2, RING, 2, 2, WLAT, HALF, LEVS, D), BF16),
            *[pltpu.VMEM(m.shape, m.dtype) for m in (*matrices, latent_queries)],
            pltpu.VMEM((STATS, D), BF16),
            pltpu.VMEM((STATS, LATENT * D), BF16),
            pltpu.VMEM((pieces, GATHERED, STATS), F32),
            pltpu.VMEM((pieces, D // 128, GATHERED, 128), F32),
            pltpu.VMEM((2, GATHERED, STATS), BF16),
            pltpu.VMEM((RING * PAD, LATENT * D), F32),
            pltpu.VMEM((RING * PAD, STATS), F32),
            pltpu.VMEM((pieces, PAD, LATENT * D), F32),
            pltpu.VMEM((pieces, PAD, STATS), F32),
            pltpu.VMEM((2, PAD, STATS), F32),
            pltpu.VMEM((pieces, FULL, WIDTH), BF16),
            pltpu.VMEM((pieces, FULL, WIDTH), BF16),
            pltpu.VMEM((pieces, FOLD, STATS), F32),
            pltpu.VMEM((pieces, FOLD, STATS), F32),
            pltpu.VMEM((pieces, FULL, WIDTH), BF16),
            pltpu.VMEM((2, RING, FULL, WIDTH), BF16),
            pltpu.VMEM((pieces, FOLD, STATS), F32),
            pltpu.VMEM((2, RING, FOLD, STATS), F32),
            pltpu.VMEM((ROWS, D), F32),
            pltpu.SemaphoreType.DMA((1 + len(matrices),)),
            pltpu.SemaphoreType.DMA((2, RING)),
            pltpu.SemaphoreType.DMA((2, RING)),
            pltpu.SemaphoreType.DMA((2, RING)),
            pltpu.SemaphoreType.DMA((pieces,)),
            pltpu.SemaphoreType.DMA((pieces,)),
            pltpu.SemaphoreType.DMA((pieces,)),
            pltpu.SemaphoreType.DMA((pieces,)),
            pltpu.SemaphoreType.DMA((pieces,)),
            pltpu.SemaphoreType.DMA((2,)),
            pltpu.SemaphoreType.DMA((pieces,)),
            pltpu.SemaphoreType.DMA((2,)),
        ],
        compiler_params=pltpu.CompilerParams(
            collective_id=0, has_side_effects=True, vmem_limit_bytes=107 * 512 * 1024
        ),
        cost_estimate=pl.CostEstimate(
            flops=8_000_000_000, bytes_accessed=100_000_000, transcendentals=0
        ),
    )(tokens, *matrices, latent_queries)
    block = (swin_query, swin_keyvalue, swin_out, mlp_up, mlp_down)
    return pl.pallas_call(
        window_kernel,
        out_shape=jax.ShapeDtypeStruct((WLAT, 2 * HALF, LATENT, D), BF16),
        in_specs=[near, near] + [whole] * len(block),
        out_specs=near,
        scratch_shapes=[
            *[pltpu.VMEM(m.shape, m.dtype) for m in block],
            pltpu.VMEM((D, ROWS), BF16),
            pltpu.VMEM((D, ROWS), F32),
            pltpu.VMEM((D // 128, 2 * PATCHES * 4, 128), F32),
            pltpu.SemaphoreType.DMA((len(block),)),
        ],
        compiler_params=pltpu.CompilerParams(vmem_limit_bytes=40 * 1024 * 1024),
        cost_estimate=pl.CostEstimate(
            flops=2_000_000_000, bytes_accessed=7_000_000, transcendentals=0
        ),
    )(latent, norm_gains, *block)


def solution(mesh):
    placed = (P(None, "tile", "var", None), P(), P(), P(), P(), P(), P(), P(), P(), P(), P(), P())
    return jax.shard_map(
        body, mesh=mesh, in_specs=placed, out_specs=P("var", "tile", None, None), check_vma=False
    )
```

```python
import functools
import math

import jax
import jax.numpy as jnp
from jax import lax
from jax.experimental import pallas as pl
from jax.experimental.pallas import tpu as pltpu
from jax.sharding import PartitionSpec as P

F32 = jnp.float32
BF16 = jnp.bfloat16
D = 512
HEADS = 16
HD = 32
LATENT = 3
LEVS = 4
WLAT = 6
HALF = 6
RING = 4
N_VAR = RING * RING
N_TILE = 8
FF = 2048
PATCHES = WLAT * HALF
BOTH = 2 * PATCHES
GATHERED = 2 * BOTH * LEVS
PAD = 40
ROWS = 2 * LATENT * PATCHES
STATS = 128
FULL = 32
WIDTH = LATENT * D + 256
FOLD = 24
MESH = pl.DeviceIdType.MESH
epsilon = 1e-05


def last_by_last(a, b):
    return lax.dot_general(a, b, (((1,), (1,)), ((), ())), preferred_element_type=F32)


def dot(a, b):
    return jnp.dot(a, b, preferred_element_type=F32)


def layer_norm(values, gain_row):
    average = jnp.mean(values, axis=-1, keepdims=True)
    centred = values - average
    spread = jnp.mean(centred * centred, axis=-1, keepdims=True)
    return centred * lax.rsqrt(spread + epsilon) * gain_row


def split(values, terms):
    parts = []
    for _ in range(terms):
        part = values.astype(BF16)
        parts.append(part)
        values = values - part.astype(F32)
    return parts


def gather_kernel(
    tokens, w_pq, w_pk, w_pv, w_po, lq_ref,
    out_ref,
    buf, pq, pk, pv, po, lq_scr,
    kp_scr, ex_scr, s_scr, v_scr, p_scr, px_scr, sc_scr, keep, kstat, t_scr, snum, rnum, sstat, rstat,
    fnum, gnum, fstat, gstat, att_scr,
    w_sem, own_sem, tok_send, tok_recv, num_send, num_recv, stat_send, stat_recv,
    far_send, far_recv, fst_send, fst_recv,
):
    var = lax.axis_index("var")
    tile = lax.axis_index("tile")
    y, x = var // RING, var % RING
    west = lax.rem(tile + N_TILE - 1, N_TILE)
    east = lax.rem(tile + 1, N_TILE)

    barrier = pltpu.get_barrier_semaphore()

    def greet(there, at):
        pl.semaphore_signal(
            barrier, inc=1, device_id={"var": there, "tile": at}, device_id_type=MESH
        )

    for d in (1, 3):
        greet(y * RING + lax.rem(x + d, RING), tile)
    for d in (1, 2, 3):
        greet(lax.rem(y + d, RING) * RING + x, tile)
    for d in range(RING):
        greet(y * RING + lax.rem(x + d, RING), east)

    def slot_of(half, k):
        return lax.rem((y if half == 0 else x) + 1 + k, RING)

    def partners(half, slot):
        a = x if half == 0 else y
        odd = lax.rem(slot, 2)
        one, three = a + 1 - 2 * lax.rem(a, 2), 3 - a
        return one + odd * (three - one), three + odd * (one - three)

    def along(half, place):
        return y * RING + place if half == 0 else place * RING + x

    def send_tokens(half, k, own=False):
        slot = slot_of(half, k)
        a = x if half == 0 else y
        lon = HALF if half == 0 else 0
        first, second = partners(half, slot)
        for which, owner in ((0, a), (1, second)) if own else ((0, first), (1, lax.rem(a + 2, RING))):
            src_at = 0 if own else 1
            band = slot * RING + owner if half == 0 else owner * RING + slot
            upper = WLAT * band + WLAT // 2
            lower = lax.rem(WLAT * band + WLAT, WLAT * N_VAR)
            for part, row in ((0, upper), (1, lower)):
                src = tokens.at[pl.ds(row, WLAT // 2), pl.ds(lon, HALF)]
                dst = buf.at[half, slot, src_at, which, pl.ds(part * (WLAT // 2), WLAT // 2)]
                if own:
                    pltpu.make_async_copy(src, dst, own_sem.at[half, slot]).start()
                else:
                    pltpu.make_async_remote_copy(
                        src_ref=src,
                        dst_ref=dst,
                        send_sem=tok_send.at[half, slot],
                        recv_sem=tok_recv.at[half, slot],
                        device_id={"var": along(half, first), "tile": tile},
                        device_id_type=MESH,
                    ).start()

    weights = ((w_pq, pq), (w_pk, pk), (w_pv, pv), (w_po, po), (lq_ref, lq_scr))
    loads = [pltpu.make_async_copy(src, dst, w_sem.at[i]) for i, (src, dst) in enumerate(weights)]
    for load in loads:
        load.start()
    order = [(half, k) for k in range(RING) for half in (1, 0)]
    for half, k in order:
        send_tokens(half, k, own=True)
    pl.semaphore_wait(barrier, 9)
    for half, k in order[:4]:
        send_tokens(half, k)

    row = lax.broadcasted_iota(jnp.int32, (STATS, LATENT * D), 0)
    col = lax.broadcasted_iota(jnp.int32, (STATS, LATENT * D), 1)
    ex_scr[...] = jnp.where(
        (row & (STATS // 2 - 1)) == (col >> 9) * HEADS + ((col & (D - 1)) >> 5), 1.0, 0.0
    ).astype(BF16)
    loads[0].wait()
    loads[4].wait()
    queries = dot(lq_scr[...], pq[...])
    head_row = lax.broadcasted_iota(jnp.int32, (HEADS, D), 0)
    head_col = lax.broadcasted_iota(jnp.int32, (HEADS, D), 1) >> 5
    spread = jnp.concatenate(
        [jnp.where(head_row == head_col, queries[j : j + 1], 0.0) for j in range(LATENT)]
        + [jnp.zeros((STATS - LATENT * HEADS, D), F32)],
        axis=0,
    )
    loads[1].wait()
    probe = sum(last_by_last(part, pk[...]) for part in split(spread, 3))
    kp_scr[...] = (probe / math.sqrt(HD)).astype(BF16)
    loads[2].wait()

    lane = lax.broadcasted_iota(jnp.int32, (PAD, STATS), 1)

    def widen(scales):
        head = scales.astype(BF16).astype(F32)
        rest = pltpu.roll(scales - head, STATS // 2, 1)
        low = lax.broadcasted_iota(jnp.int32, scales.shape, 1) < STATS // 2
        return dot(jnp.where(low, head, rest).astype(BF16), ex_scr[...])

    def fold(stats):
        low = lax.broadcasted_iota(jnp.int32, (PAD - FOLD, STATS), 1) < STATS // 2
        rest = pltpu.roll(stats[FOLD:PAD], STATS // 2, 1)
        return jnp.concatenate(
            [jnp.where(low, stats[: PAD - FOLD], rest), stats[PAD - FOLD : FOLD]], axis=0
        )

    def unfold(stats):
        return jnp.concatenate([stats, pltpu.roll(stats[: PAD - FOLD], STATS // 2, 1)], axis=0)

    def pack(ref, at, group, rows):
        rows = rows.astype(BF16)
        ref[at, 0:FULL, group * 256 : (group + 1) * 256] = rows[:FULL]
        ref[at, group * 4 : group * 4 + 4, LATENT * D :] = rows[FULL:PATCHES]

    def unpack(rows, group):
        rest = rows[:, LATENT * D :].astype(F32)[group * 4 : group * 4 + 4]
        return jnp.concatenate(
            [rows[:, group * 256 : (group + 1) * 256].astype(F32), rest], axis=0
        )

    lane_part = lax.broadcasted_iota(jnp.int32, (PATCHES, STATS), 1)

    def products(half, k, src):
        index = half * RING + k
        rows = buf[half, slot_of(half, k), src].reshape(BOTH * LEVS, D)
        at = src * BOTH * LEVS
        s_scr[index, at : at + BOTH * LEVS, :] = last_by_last(rows, kp_scr[...])
        values = dot(rows, pv[...])
        for lanes in range(D // 128):
            v_scr[index, lanes, at : at + BOTH * LEVS, :] = values[:, lanes * 128 : (lanes + 1) * 128]

    def arrive(half, k):
        slot = slot_of(half, k)
        arrived = buf.at[half, slot, 1]
        pltpu.make_async_copy(arrived, arrived, tok_recv.at[half, slot]).wait()
        if k + 2 < RING:
            send_tokens(half, k + 2)

    def sums(half, k, which):
        index = half * RING + k
        members = [
            pl.ds((src * BOTH + which * PATCHES) * LEVS + t, PATCHES, stride=LEVS)
            for src in range(2)
            for t in range(LEVS)
        ]
        scores = [s_scr[index, member, :] for member in members]
        top = functools.reduce(jnp.maximum, scores)
        weights = [jnp.exp(score - top) for score in scores]
        total = sum(weights)
        inverse = jnp.where(lane_part < STATS // 2, 1.0 / total, 0.0)
        at_p = 2 * half + which
        for n, weight in enumerate(weights):
            p_scr[at_p, n * PAD : n * PAD + PATCHES, :] = (weight * inverse).astype(BF16)
        stats = top + jnp.log(total)
        if which == 0:
            kstat[index, 0:PATCHES, :] = stats
        else:
            t_scr[half, 0:PATCHES, :] = stats
            sstat[index] = fold(t_scr[half])
        for at in range(0, LATENT * D, 256):
            wide = dot(p_scr[at_p], ex_scr[:, at : at + 256])
            sides = [
                sum(
                    v_scr[index, (at % D) // 128 + side, member, :]
                    * wide[n * PAD : n * PAD + PATCHES, side * 128 : (side + 1) * 128]
                    for n, member in enumerate(members)
                )
                for side in range(2)
            ]
            here = jnp.concatenate(sides, axis=1)
            if which == 0:
                keep[index, 0:PATCHES, at : at + 256] = here
            else:
                pack(snum, index, at // 256, here)

    def work(half, k):
        slot = slot_of(half, k)
        index = half * RING + k
        sums(half, k, 1)
        _, second = partners(half, slot)
        for src, dst, send, recv in (
            (snum, rnum, num_send, num_recv), (sstat, rstat, stat_send, stat_recv)
        ):
            pltpu.make_async_remote_copy(
                src_ref=src.at[index],
                dst_ref=dst.at[index],
                send_sem=send.at[index],
                recv_sem=recv.at[index],
                device_id={"var": along(half, second), "tile": tile},
                device_id_type=MESH,
            ).start()

    def merge(half, k):
        slot = slot_of(half, k)
        index = half * RING + k
        pltpu.make_async_copy(rstat.at[index], rstat.at[index], stat_recv.at[index]).wait()
        mine, theirs = kstat[index], unfold(rstat[index])
        top = jnp.maximum(mine, theirs)
        my_scale, their_scale = jnp.exp(mine - top), jnp.exp(theirs - top)
        total = my_scale + their_scale
        fstat[index] = fold(top + jnp.log(total))
        scales = widen(jnp.concatenate([my_scale / total, their_scale / total], axis=0))
        pltpu.make_async_copy(rnum.at[index], rnum.at[index], num_recv.at[index]).wait()
        theirs = rnum[index]
        for group in range(LATENT * D // 256):
            columns = slice(group * 256, (group + 1) * 256)
            merged = (
                keep[index, 0:PATCHES, columns] * scales[0:PATCHES, columns]
                + unpack(theirs, group) * scales[PAD : PAD + PATCHES, columns]
            )
            pack(fnum, index, group, merged)
        source = y if half == 0 else x
        there = slot * RING + x if half == 0 else y * RING + slot
        for src, dst, send, recv in (
            (fnum, gnum, far_send, far_recv), (fstat, gstat, fst_send, fst_recv)
        ):
            if half == 0 and k == RING - 1:
                pltpu.make_async_copy(src.at[index], dst.at[half, source], recv.at[half]).start()
            else:
                pltpu.make_async_remote_copy(
                    src_ref=src.at[index],
                    dst_ref=dst.at[half, source],
                    send_sem=send.at[index],
                    recv_sem=recv.at[half],
                    device_id={"var": there, "tile": tile if half == 0 else west},
                    device_id_type=MESH,
                ).start()

    for half, k in order:
        own = buf.at[half, slot_of(half, k), 0]
        pltpu.make_async_copy(own, own, own_sem.at[half, slot_of(half, k)]).wait()
        products(half, k, 0)
    for k in range(RING):
        for half in (1, 0):
            arrive(half, k)
        for half in (1, 0):
            products(half, k, 1)
        for half in (1, 0):
            work(half, k)
        for half in (1, 0):
            if k > 0:
                merge(half, k - 1)
        for half in (1, 0):
            sums(half, k, 0)
    for half in (1, 0):
        merge(half, RING - 1)

    inside = lax.broadcasted_iota(jnp.int32, (PAD, STATS), 0) < PATCHES
    for half in range(2):
        pltpu.make_async_copy(gnum.at[half], gnum.at[half], far_recv.at[half]).wait()
        pltpu.make_async_copy(gstat.at[half], gstat.at[half], fst_recv.at[half]).wait()
        stats = [unfold(gstat[half, src]) for src in range(RING)]
        top = functools.reduce(jnp.maximum, stats)
        scales = [jnp.exp(stat - top) for stat in stats]
        denominator = sum(scales)
        valid = (lane < LATENT * HEADS) & inside
        for src in range(RING):
            sc_scr[pl.ds(src * PAD, PAD), :] = jnp.where(valid, scales[src] / denominator, 0.0)
        px_scr[0 : RING * PAD] = widen(sc_scr[...])
        gathered = [gnum[half, src] for src in range(RING)]
        for group in range(LATENT * D // 256):
            share = sum(
                unpack(gathered[src], group)
                * px_scr[pl.ds(src * PAD, PATCHES), group * 256 : (group + 1) * 256]
                for src in range(RING)
            )
            at = (half * LATENT + group // 2) * PATCHES
            att_scr[at : at + PATCHES, group % 2 * 256 : (group % 2 + 1) * 256] = share
    loads[3].wait()
    latent = dot(att_scr[...].astype(BF16), po[...])
    token = lax.broadcasted_iota(jnp.int32, (ROWS, D), 0)
    block = sum((token >= b * PATCHES).astype(jnp.int32) for b in range(1, 2 * LATENT))
    level = jnp.where(block >= LATENT, block - LATENT, block)
    start = jnp.zeros((ROWS, D), F32)
    for j in range(LATENT):
        start = jnp.where(level == j, lq_scr[j : j + 1, :].astype(F32), start)
    out_ref[...] = (start + latent).astype(BF16)

    for half in range(2):
        for k in range(RING):
            slot = slot_of(half, k)
            index = half * RING + k
            sent = buf.at[half, slot, 1]
            pltpu.make_async_copy(sent, sent, tok_send.at[half, slot]).wait()
            pltpu.make_async_copy(snum.at[index], snum.at[index], num_send.at[index]).wait()
            pltpu.make_async_copy(sstat.at[index], sstat.at[index], stat_send.at[index]).wait()
            if half == 1 or k < RING - 1:
                pltpu.make_async_copy(fnum.at[index], fnum.at[index], far_send.at[index]).wait()
                pltpu.make_async_copy(fstat.at[index], fstat.at[index], fst_send.at[index]).wait()


def window_kernel(
    latent_ref, gains_ref, w_sq, w_skv, w_so, w_up, w_down, out_ref,
    sq, skv, so, up, down, vt_scr, mix_scr, turn_scr, w_sem,
):
    weights = ((w_sq, sq), (w_skv, skv), (w_so, so), (w_up, up), (w_down, down))
    loads = [pltpu.make_async_copy(src, dst, w_sem.at[i]) for i, (src, dst) in enumerate(weights)]
    for load in loads:
        load.start()
    var = lax.axis_index("var")
    residual = latent_ref[...].astype(F32)
    normed = layer_norm(residual, gains_ref[0:1, :]).astype(BF16)
    loads[0].wait()
    queries = dot(normed, sq[...]).astype(BF16)
    loads[1].wait()
    keyvals = dot(normed, skv[...])
    keys = keyvals[:, :D]
    vt_scr[...] = jnp.transpose(keyvals[:, D:]).astype(BF16)

    def southern(shape, axis):
        index = lax.broadcasted_iota(jnp.int32, shape, axis)
        for b in range(2 * LATENT - 1, 0, -1):
            index = jnp.where(index >= b * PATCHES, index - b * PATCHES, index)
        return index >= WLAT // 2 * HALF

    apart = southern((ROWS, ROWS), 0) != southern((ROWS, ROWS), 1)
    bias = jnp.where(apart & (var == N_VAR - 1), -jnp.inf, 0.0)
    lane_head = lax.broadcasted_iota(jnp.int32, (ROWS, 256), 1) >> 5
    for h in range(HEADS):
        at = h // 8 * 256
        key_part = jnp.where(lane_head == h % 8, keys[:, at : at + 256], 0.0).astype(BF16)
        logits = last_by_last(key_part, queries[:, at : at + 256]) + bias
        top = jnp.max(logits, axis=0, keepdims=True)
        exponent = jnp.exp2((logits - top) * (math.log2(math.e) / math.sqrt(HD)))
        probs = (exponent * (1.0 / jnp.sum(exponent, axis=0, keepdims=True))).astype(BF16)
        mix_scr[h * HD : (h + 1) * HD, :] = dot(vt_scr[h * HD : (h + 1) * HD, :], probs)
    mixed = jnp.transpose(mix_scr[...]).astype(BF16)
    loads[2].wait()
    residual = residual + dot(mixed, so[...])
    normed = layer_norm(residual, gains_ref[1:2, :]).astype(BF16)
    loads[3].wait()
    loads[4].wait()
    chunk = 512
    for c in range(0, FF, chunk):
        wide = dot(normed, up[:, c : c + chunk])
        hidden = (0.5 * wide * (1.0 + lax.erf(wide * math.sqrt(0.5)))).astype(BF16)
        residual = residual + dot(hidden, down[c : c + chunk, :])
    lanes = D // 128
    for b in range(2 * LATENT):
        half, j = b // LATENT, b % LATENT
        for l in range(lanes):
            turn_scr[l, pl.ds(half * PATCHES * 4 + j, PATCHES, stride=4), :] = residual[
                b * PATCHES : (b + 1) * PATCHES, l * 128 : (l + 1) * 128
            ]
    for half in range(2):
        for r in range(WLAT):
            for l in range(lanes):
                rows = turn_scr[l, pl.ds((half * PATCHES + r * HALF) * 4, HALF * 4), :]
                rows = rows.reshape(HALF, 4, 128)[:, :LATENT]
                out_ref[r, half * HALF : (half + 1) * HALF, :, l * 128 : (l + 1) * 128] = rows.astype(BF16)


def body(
    tokens, latent_queries, perc_query, perc_key, perc_value, perc_out, norm_gains, swin_query,
    swin_keyvalue, swin_out, mlp_up, mlp_down,
):
    whole = pl.BlockSpec(memory_space=pltpu.HBM)
    near = pl.BlockSpec(memory_space=pltpu.VMEM)
    matrices = (perc_query, perc_key, perc_value, perc_out)
    pieces = 2 * RING
    latent = pl.pallas_call(
        gather_kernel,
        out_shape=jax.ShapeDtypeStruct((ROWS, D), BF16),
        in_specs=[whole] * (2 + len(matrices)),
        out_specs=near,
        scratch_shapes=[
            pltpu.VMEM((2, RING, 2, 2, WLAT, HALF, LEVS, D), BF16),
            *[pltpu.VMEM(m.shape, m.dtype) for m in (*matrices, latent_queries)],
            pltpu.VMEM((STATS, D), BF16),
            pltpu.VMEM((STATS, LATENT * D), BF16),
            pltpu.VMEM((pieces, GATHERED, STATS), F32),
            pltpu.VMEM((pieces, D // 128, GATHERED, 128), F32),
            pltpu.VMEM((4, 2 * LEVS * PAD, STATS), BF16),
            pltpu.VMEM((RING * PAD, LATENT * D), F32),
            pltpu.VMEM((RING * PAD, STATS), F32),
            pltpu.VMEM((pieces, PAD, LATENT * D), F32),
            pltpu.VMEM((pieces, PAD, STATS), F32),
            pltpu.VMEM((2, PAD, STATS), F32),
            pltpu.VMEM((pieces, FULL, WIDTH), BF16),
            pltpu.VMEM((pieces, FULL, WIDTH), BF16),
            pltpu.VMEM((pieces, FOLD, STATS), F32),
            pltpu.VMEM((pieces, FOLD, STATS), F32),
            pltpu.VMEM((pieces, FULL, WIDTH), BF16),
            pltpu.VMEM((2, RING, FULL, WIDTH), BF16),
            pltpu.VMEM((pieces, FOLD, STATS), F32),
            pltpu.VMEM((2, RING, FOLD, STATS), F32),
            pltpu.VMEM((ROWS, D), F32),
            pltpu.SemaphoreType.DMA((1 + len(matrices),)),
            pltpu.SemaphoreType.DMA((2, RING)),
            pltpu.SemaphoreType.DMA((2, RING)),
            pltpu.SemaphoreType.DMA((2, RING)),
            pltpu.SemaphoreType.DMA((pieces,)),
            pltpu.SemaphoreType.DMA((pieces,)),
            pltpu.SemaphoreType.DMA((pieces,)),
            pltpu.SemaphoreType.DMA((pieces,)),
            pltpu.SemaphoreType.DMA((pieces,)),
            pltpu.SemaphoreType.DMA((2,)),
            pltpu.SemaphoreType.DMA((pieces,)),
            pltpu.SemaphoreType.DMA((2,)),
        ],
        compiler_params=pltpu.CompilerParams(
            collective_id=0, has_side_effects=True, vmem_limit_bytes=107 * 512 * 1024
        ),
        cost_estimate=pl.CostEstimate(
            flops=8_000_000_000, bytes_accessed=100_000_000, transcendentals=0
        ),
    )(tokens, *matrices, latent_queries)
    block = (swin_query, swin_keyvalue, swin_out, mlp_up, mlp_down)
    return pl.pallas_call(
        window_kernel,
        out_shape=jax.ShapeDtypeStruct((WLAT, 2 * HALF, LATENT, D), BF16),
        in_specs=[near, near] + [whole] * len(block),
        out_specs=near,
        scratch_shapes=[
            *[pltpu.VMEM(m.shape, m.dtype) for m in block],
            pltpu.VMEM((D, ROWS), BF16),
            pltpu.VMEM((D, ROWS), F32),
            pltpu.VMEM((D // 128, 2 * PATCHES * 4, 128), F32),
            pltpu.SemaphoreType.DMA((len(block),)),
        ],
        compiler_params=pltpu.CompilerParams(vmem_limit_bytes=40 * 1024 * 1024),
        cost_estimate=pl.CostEstimate(
            flops=2_000_000_000, bytes_accessed=7_000_000, transcendentals=0
        ),
    )(latent, norm_gains, *block)


def solution(mesh):
    placed = (P(None, "tile", "var", None), P(), P(), P(), P(), P(), P(), P(), P(), P(), P(), P())
    return jax.shard_map(
        body, mesh=mesh, in_specs=placed, out_specs=P("var", "tile", None, None), check_vma=False
    )
```

```python
import functools
import math

import jax
import jax.numpy as jnp
from jax import lax
from jax.experimental import pallas as pl
from jax.experimental.pallas import tpu as pltpu
from jax.sharding import PartitionSpec as P

F32 = jnp.float32
BF16 = jnp.bfloat16
D = 512
HEADS = 16
HD = 32
LATENT = 3
LEVS = 4
WLAT = 6
HALF = 6
RING = 4
N_VAR = RING * RING
N_TILE = 8
FF = 2048
PATCHES = WLAT * HALF
BOTH = 2 * PATCHES
GATHERED = 2 * BOTH * LEVS
PAD = 40
ROWS = 2 * LATENT * PATCHES
STATS = 128
FULL = 32
WIDTH = LATENT * D + 256
FOLD = 24
MESH = pl.DeviceIdType.MESH
epsilon = 1e-05


def last_by_last(a, b):
    return lax.dot_general(a, b, (((1,), (1,)), ((), ())), preferred_element_type=F32)


def dot(a, b):
    return jnp.dot(a, b, preferred_element_type=F32)


def layer_norm(values, gain_row):
    average = jnp.mean(values, axis=-1, keepdims=True)
    centred = values - average
    spread = jnp.mean(centred * centred, axis=-1, keepdims=True)
    return centred * lax.rsqrt(spread + epsilon) * gain_row


def split(values, terms):
    parts = []
    for _ in range(terms):
        part = values.astype(BF16)
        parts.append(part)
        values = values - part.astype(F32)
    return parts


def gather_kernel(
    tokens, w_pq, w_pk, w_pv, w_po, lq_ref,
    out_ref,
    buf, pq, pk, pv, po, lq_scr,
    kp_scr, ex_scr, s_scr, v_scr, p_scr, px_scr, sc_scr, keep, kstat, t_scr, snum, rnum, sstat, rstat,
    fnum, gnum, fstat, gstat, att_scr,
    w_sem, own_sem, tok_send, tok_recv, num_send, num_recv, stat_send, stat_recv,
    far_send, far_recv, fst_send, fst_recv,
):
    var = lax.axis_index("var")
    tile = lax.axis_index("tile")
    y, x = var // RING, var % RING
    west = lax.rem(tile + N_TILE - 1, N_TILE)
    east = lax.rem(tile + 1, N_TILE)

    barrier = pltpu.get_barrier_semaphore()

    def greet(there, at):
        pl.semaphore_signal(
            barrier, inc=1, device_id={"var": there, "tile": at}, device_id_type=MESH
        )

    for d in (1, 3):
        greet(y * RING + lax.rem(x + d, RING), tile)
    for d in (1, 2, 3):
        greet(lax.rem(y + d, RING) * RING + x, tile)
    for d in range(RING):
        greet(y * RING + lax.rem(x + d, RING), east)

    def slot_of(half, k):
        return lax.rem((y if half == 0 else x) + 1 + k, RING)

    def partners(half, slot):
        a = x if half == 0 else y
        odd = lax.rem(slot, 2)
        one, three = a + 1 - 2 * lax.rem(a, 2), 3 - a
        return one + odd * (three - one), three + odd * (one - three)

    def along(half, place):
        return y * RING + place if half == 0 else place * RING + x

    def send_tokens(half, k, own=False):
        slot = slot_of(half, k)
        a = x if half == 0 else y
        lon = HALF if half == 0 else 0
        first, second = partners(half, slot)
        for which, owner in ((0, a), (1, second)) if own else ((0, first), (1, lax.rem(a + 2, RING))):
            src_at = 0 if own else 1
            band = slot * RING + owner if half == 0 else owner * RING + slot
            upper = WLAT * band + WLAT // 2
            lower = lax.rem(WLAT * band + WLAT, WLAT * N_VAR)
            for part, row in ((0, upper), (1, lower)):
                src = tokens.at[pl.ds(row, WLAT // 2), pl.ds(lon, HALF)]
                dst = buf.at[half, slot, src_at, which, pl.ds(part * (WLAT // 2), WLAT // 2)]
                if own:
                    pltpu.make_async_copy(src, dst, own_sem.at[half, slot]).start()
                else:
                    pltpu.make_async_remote_copy(
                        src_ref=src,
                        dst_ref=dst,
                        send_sem=tok_send.at[half, slot],
                        recv_sem=tok_recv.at[half, slot],
                        device_id={"var": along(half, first), "tile": tile},
                        device_id_type=MESH,
                    ).start()

    weights = ((w_pq, pq), (w_pk, pk), (w_pv, pv), (w_po, po), (lq_ref, lq_scr))
    loads = [pltpu.make_async_copy(src, dst, w_sem.at[i]) for i, (src, dst) in enumerate(weights)]
    for load in loads:
        load.start()
    order = [(half, k) for k in range(RING) for half in (1, 0)]
    for half, k in order:
        send_tokens(half, k, own=True)
    pl.semaphore_wait(barrier, 9)
    for half, k in order[:4]:
        send_tokens(half, k)

    row = lax.broadcasted_iota(jnp.int32, (STATS, LATENT * D), 0)
    col = lax.broadcasted_iota(jnp.int32, (STATS, LATENT * D), 1)
    ex_scr[...] = jnp.where(
        (row & (STATS // 2 - 1)) == (col >> 9) * HEADS + ((col & (D - 1)) >> 5), 1.0, 0.0
    ).astype(BF16)
    loads[0].wait()
    loads[4].wait()
    queries = dot(lq_scr[...], pq[...])
    head_row = lax.broadcasted_iota(jnp.int32, (HEADS, D), 0)
    head_col = lax.broadcasted_iota(jnp.int32, (HEADS, D), 1) >> 5
    spread = jnp.concatenate(
        [jnp.where(head_row == head_col, queries[j : j + 1], 0.0) for j in range(LATENT)]
        + [jnp.zeros((STATS - LATENT * HEADS, D), F32)],
        axis=0,
    )
    loads[1].wait()
    probe = sum(last_by_last(part, pk[...]) for part in split(spread, 3))
    kp_scr[...] = (probe / math.sqrt(HD)).astype(BF16)
    loads[2].wait()

    lane = lax.broadcasted_iota(jnp.int32, (PAD, STATS), 1)

    def widen(scales):
        head = scales.astype(BF16).astype(F32)
        rest = pltpu.roll(scales - head, STATS // 2, 1)
        low = lax.broadcasted_iota(jnp.int32, scales.shape, 1) < STATS // 2
        return dot(jnp.where(low, head, rest).astype(BF16), ex_scr[...])

    def fold(stats):
        low = lax.broadcasted_iota(jnp.int32, (PAD - FOLD, STATS), 1) < STATS // 2
        rest = pltpu.roll(stats[FOLD:PAD], STATS // 2, 1)
        return jnp.concatenate(
            [jnp.where(low, stats[: PAD - FOLD], rest), stats[PAD - FOLD : FOLD]], axis=0
        )

    def unfold(stats):
        return jnp.concatenate([stats, pltpu.roll(stats[: PAD - FOLD], STATS // 2, 1)], axis=0)

    def pack(ref, at, group, rows):
        rows = rows.astype(BF16)
        ref[at, 0:FULL, group * 256 : (group + 1) * 256] = rows[:FULL]
        ref[at, group * 4 : group * 4 + 4, LATENT * D :] = rows[FULL:PATCHES]

    def unpack(rows, group):
        rest = rows[:, LATENT * D :].astype(F32)[group * 4 : group * 4 + 4]
        return jnp.concatenate(
            [rows[:, group * 256 : (group + 1) * 256].astype(F32), rest], axis=0
        )

    lane_part = lax.broadcasted_iota(jnp.int32, (PATCHES, STATS), 1)

    def products(half, k, src):
        index = half * RING + k
        rows = buf[half, slot_of(half, k), src].reshape(BOTH * LEVS, D)
        at = src * BOTH * LEVS
        s_scr[index, at : at + BOTH * LEVS, :] = last_by_last(rows, kp_scr[...])
        values = dot(rows, pv[...])
        for lanes in range(D // 128):
            v_scr[index, lanes, at : at + BOTH * LEVS, :] = values[:, lanes * 128 : (lanes + 1) * 128]

    def arrive(half, k):
        slot = slot_of(half, k)
        arrived = buf.at[half, slot, 1]
        pltpu.make_async_copy(arrived, arrived, tok_recv.at[half, slot]).wait()
        if k + 2 < RING:
            send_tokens(half, k + 2)

    def sums(half, k, which):
        index = half * RING + k
        members = [
            pl.ds((src * BOTH + which * PATCHES) * LEVS + t, PATCHES, stride=LEVS)
            for src in range(2)
            for t in range(LEVS)
        ]
        scores = [s_scr[index, member, :] for member in members]
        top = functools.reduce(jnp.maximum, scores)
        weights = [jnp.exp(score - top) for score in scores]
        total = sum(weights)
        inverse = jnp.where(lane_part < STATS // 2, 1.0 / total, 0.0)
        at_p = 2 * half + which
        for n, weight in enumerate(weights):
            p_scr[at_p, n * PAD : n * PAD + PATCHES, :] = (weight * inverse).astype(BF16)
        stats = top + jnp.log(total)
        if which == 0:
            kstat[index, 0:PATCHES, :] = stats
        else:
            t_scr[half, 0:PATCHES, :] = stats
            sstat[index] = fold(t_scr[half])
        for at in range(0, LATENT * D, 256):
            wide = dot(p_scr[at_p], ex_scr[:, at : at + 256])
            sides = [
                sum(
                    v_scr[index, (at % D) // 128 + side, member, :]
                    * wide[n * PAD : n * PAD + PATCHES, side * 128 : (side + 1) * 128]
                    for n, member in enumerate(members)
                )
                for side in range(2)
            ]
            here = jnp.concatenate(sides, axis=1)
            if which == 0:
                keep[index, 0:PATCHES, at : at + 256] = here
            else:
                pack(snum, index, at // 256, here)

    def work(half, k):
        slot = slot_of(half, k)
        index = half * RING + k
        sums(half, k, 1)
        _, second = partners(half, slot)
        for src, dst, send, recv in (
            (snum, rnum, num_send, num_recv), (sstat, rstat, stat_send, stat_recv)
        ):
            pltpu.make_async_remote_copy(
                src_ref=src.at[index],
                dst_ref=dst.at[index],
                send_sem=send.at[index],
                recv_sem=recv.at[index],
                device_id={"var": along(half, second), "tile": tile},
                device_id_type=MESH,
            ).start()

    def merge(half, k):
        slot = slot_of(half, k)
        index = half * RING + k
        pltpu.make_async_copy(rstat.at[index], rstat.at[index], stat_recv.at[index]).wait()
        mine, theirs = kstat[index], unfold(rstat[index])
        top = jnp.maximum(mine, theirs)
        my_scale, their_scale = jnp.exp(mine - top), jnp.exp(theirs - top)
        total = my_scale + their_scale
        fstat[index] = fold(top + jnp.log(total))
        scales = widen(jnp.concatenate([my_scale / total, their_scale / total], axis=0))
        pltpu.make_async_copy(rnum.at[index], rnum.at[index], num_recv.at[index]).wait()
        theirs = rnum[index]
        for group in range(LATENT * D // 256):
            columns = slice(group * 256, (group + 1) * 256)
            merged = (
                keep[index, 0:PATCHES, columns] * scales[0:PATCHES, columns]
                + unpack(theirs, group) * scales[PAD : PAD + PATCHES, columns]
            )
            pack(fnum, index, group, merged)
        source = y if half == 0 else x
        there = slot * RING + x if half == 0 else y * RING + slot
        for src, dst, send, recv in (
            (fnum, gnum, far_send, far_recv), (fstat, gstat, fst_send, fst_recv)
        ):
            if half == 0 and k == RING - 1:
                pltpu.make_async_copy(src.at[index], dst.at[half, source], recv.at[half]).start()
            else:
                pltpu.make_async_remote_copy(
                    src_ref=src.at[index],
                    dst_ref=dst.at[half, source],
                    send_sem=send.at[index],
                    recv_sem=recv.at[half],
                    device_id={"var": there, "tile": tile if half == 0 else west},
                    device_id_type=MESH,
                ).start()

    for half, k in order:
        own = buf.at[half, slot_of(half, k), 0]
        pltpu.make_async_copy(own, own, own_sem.at[half, slot_of(half, k)]).wait()
        products(half, k, 0)
    for k in range(RING):
        for half in (1, 0):
            arrive(half, k)
        for half in (1, 0):
            products(half, k, 1)
            work(half, k)
        for half in (1, 0):
            if k > 0:
                merge(half, k - 1)
        for half in (1, 0):
            sums(half, k, 0)
    for half in (1, 0):
        merge(half, RING - 1)

    inside = lax.broadcasted_iota(jnp.int32, (PAD, STATS), 0) < PATCHES
    for half in range(2):
        pltpu.make_async_copy(gnum.at[half], gnum.at[half], far_recv.at[half]).wait()
        pltpu.make_async_copy(gstat.at[half], gstat.at[half], fst_recv.at[half]).wait()
        stats = [unfold(gstat[half, src]) for src in range(RING)]
        top = functools.reduce(jnp.maximum, stats)
        scales = [jnp.exp(stat - top) for stat in stats]
        denominator = sum(scales)
        valid = (lane < LATENT * HEADS) & inside
        for src in range(RING):
            sc_scr[pl.ds(src * PAD, PAD), :] = jnp.where(valid, scales[src] / denominator, 0.0)
        px_scr[0 : RING * PAD] = widen(sc_scr[...])
        gathered = [gnum[half, src] for src in range(RING)]
        for group in range(LATENT * D // 256):
            share = sum(
                unpack(gathered[src], group)
                * px_scr[pl.ds(src * PAD, PATCHES), group * 256 : (group + 1) * 256]
                for src in range(RING)
            )
            at = (half * LATENT + group // 2) * PATCHES
            att_scr[at : at + PATCHES, group % 2 * 256 : (group % 2 + 1) * 256] = share
    loads[3].wait()
    latent = dot(att_scr[...].astype(BF16), po[...])
    token = lax.broadcasted_iota(jnp.int32, (ROWS, D), 0)
    block = sum((token >= b * PATCHES).astype(jnp.int32) for b in range(1, 2 * LATENT))
    level = jnp.where(block >= LATENT, block - LATENT, block)
    start = jnp.zeros((ROWS, D), F32)
    for j in range(LATENT):
        start = jnp.where(level == j, lq_scr[j : j + 1, :].astype(F32), start)
    out_ref[...] = (start + latent).astype(BF16)

    for half in range(2):
        for k in range(RING):
            slot = slot_of(half, k)
            index = half * RING + k
            sent = buf.at[half, slot, 1]
            pltpu.make_async_copy(sent, sent, tok_send.at[half, slot]).wait()
            pltpu.make_async_copy(snum.at[index], snum.at[index], num_send.at[index]).wait()
            pltpu.make_async_copy(sstat.at[index], sstat.at[index], stat_send.at[index]).wait()
            if half == 1 or k < RING - 1:
                pltpu.make_async_copy(fnum.at[index], fnum.at[index], far_send.at[index]).wait()
                pltpu.make_async_copy(fstat.at[index], fstat.at[index], fst_send.at[index]).wait()


def window_kernel(
    latent_ref, gains_ref, w_sq, w_skv, w_so, w_up, w_down, out_ref,
    sq, skv, so, up, down, vt_scr, mix_scr, turn_scr, w_sem,
):
    weights = ((w_sq, sq), (w_skv, skv), (w_so, so), (w_up, up), (w_down, down))
    loads = [pltpu.make_async_copy(src, dst, w_sem.at[i]) for i, (src, dst) in enumerate(weights)]
    for load in loads:
        load.start()
    var = lax.axis_index("var")
    residual = latent_ref[...].astype(F32)
    normed = layer_norm(residual, gains_ref[0:1, :]).astype(BF16)
    loads[0].wait()
    queries = dot(normed, sq[...]).astype(BF16)
    loads[1].wait()
    keyvals = dot(normed, skv[...])
    keys = keyvals[:, :D]
    vt_scr[...] = jnp.transpose(keyvals[:, D:]).astype(BF16)

    def southern(shape, axis):
        index = lax.broadcasted_iota(jnp.int32, shape, axis)
        for b in range(2 * LATENT - 1, 0, -1):
            index = jnp.where(index >= b * PATCHES, index - b * PATCHES, index)
        return index >= WLAT // 2 * HALF

    apart = southern((ROWS, ROWS), 0) != southern((ROWS, ROWS), 1)
    bias = jnp.where(apart & (var == N_VAR - 1), -jnp.inf, 0.0)
    lane_head = lax.broadcasted_iota(jnp.int32, (ROWS, 256), 1) >> 5
    for h in range(HEADS):
        at = h // 8 * 256
        key_part = jnp.where(lane_head == h % 8, keys[:, at : at + 256], 0.0).astype(BF16)
        logits = last_by_last(key_part, queries[:, at : at + 256]) + bias
        top = jnp.max(logits, axis=0, keepdims=True)
        exponent = jnp.exp2((logits - top) * (math.log2(math.e) / math.sqrt(HD)))
        probs = (exponent * (1.0 / jnp.sum(exponent, axis=0, keepdims=True))).astype(BF16)
        mix_scr[h * HD : (h + 1) * HD, :] = dot(vt_scr[h * HD : (h + 1) * HD, :], probs)
    mixed = jnp.transpose(mix_scr[...]).astype(BF16)
    loads[2].wait()
    residual = residual + dot(mixed, so[...])
    normed = layer_norm(residual, gains_ref[1:2, :]).astype(BF16)
    loads[3].wait()
    loads[4].wait()
    chunk = 512
    for c in range(0, FF, chunk):
        wide = dot(normed, up[:, c : c + chunk])
        hidden = (0.5 * wide * (1.0 + lax.erf(wide * math.sqrt(0.5)))).astype(BF16)
        residual = residual + dot(hidden, down[c : c + chunk, :])
    lanes = D // 128
    for b in range(2 * LATENT):
        half, j = b // LATENT, b % LATENT
        for l in range(lanes):
            turn_scr[l, pl.ds(half * PATCHES * 4 + j, PATCHES, stride=4), :] = residual[
                b * PATCHES : (b + 1) * PATCHES, l * 128 : (l + 1) * 128
            ]
    for half in range(2):
        for r in range(WLAT):
            for l in range(lanes):
                rows = turn_scr[l, pl.ds((half * PATCHES + r * HALF) * 4, HALF * 4), :]
                rows = rows.reshape(HALF, 4, 128)[:, :LATENT]
                out_ref[r, half * HALF : (half + 1) * HALF, :, l * 128 : (l + 1) * 128] = rows.astype(BF16)


def body(
    tokens, latent_queries, perc_query, perc_key, perc_value, perc_out, norm_gains, swin_query,
    swin_keyvalue, swin_out, mlp_up, mlp_down,
):
    whole = pl.BlockSpec(memory_space=pltpu.HBM)
    near = pl.BlockSpec(memory_space=pltpu.VMEM)
    matrices = (perc_query, perc_key, perc_value, perc_out)
    pieces = 2 * RING
    latent = pl.pallas_call(
        gather_kernel,
        out_shape=jax.ShapeDtypeStruct((ROWS, D), BF16),
        in_specs=[whole] * (2 + len(matrices)),
        out_specs=near,
        scratch_shapes=[
            pltpu.VMEM((2, RING, 2, 2, WLAT, HALF, LEVS, D), BF16),
            *[pltpu.VMEM(m.shape, m.dtype) for m in (*matrices, latent_queries)],
            pltpu.VMEM((STATS, D), BF16),
            pltpu.VMEM((STATS, LATENT * D), BF16),
            pltpu.VMEM((pieces, GATHERED, STATS), F32),
            pltpu.VMEM((pieces, D // 128, GATHERED, 128), F32),
            pltpu.VMEM((4, 2 * LEVS * PAD, STATS), BF16),
            pltpu.VMEM((RING * PAD, LATENT * D), F32),
            pltpu.VMEM((RING * PAD, STATS), F32),
            pltpu.VMEM((pieces, PAD, LATENT * D), F32),
            pltpu.VMEM((pieces, PAD, STATS), F32),
            pltpu.VMEM((2, PAD, STATS), F32),
            pltpu.VMEM((pieces, FULL, WIDTH), BF16),
            pltpu.VMEM((pieces, FULL, WIDTH), BF16),
            pltpu.VMEM((pieces, FOLD, STATS), F32),
            pltpu.VMEM((pieces, FOLD, STATS), F32),
            pltpu.VMEM((pieces, FULL, WIDTH), BF16),
            pltpu.VMEM((2, RING, FULL, WIDTH), BF16),
            pltpu.VMEM((pieces, FOLD, STATS), F32),
            pltpu.VMEM((2, RING, FOLD, STATS), F32),
            pltpu.VMEM((ROWS, D), F32),
            pltpu.SemaphoreType.DMA((1 + len(matrices),)),
            pltpu.SemaphoreType.DMA((2, RING)),
            pltpu.SemaphoreType.DMA((2, RING)),
            pltpu.SemaphoreType.DMA((2, RING)),
            pltpu.SemaphoreType.DMA((pieces,)),
            pltpu.SemaphoreType.DMA((pieces,)),
            pltpu.SemaphoreType.DMA((pieces,)),
            pltpu.SemaphoreType.DMA((pieces,)),
            pltpu.SemaphoreType.DMA((pieces,)),
            pltpu.SemaphoreType.DMA((2,)),
            pltpu.SemaphoreType.DMA((pieces,)),
            pltpu.SemaphoreType.DMA((2,)),
        ],
        compiler_params=pltpu.CompilerParams(
            collective_id=0, has_side_effects=True, vmem_limit_bytes=107 * 512 * 1024
        ),
        cost_estimate=pl.CostEstimate(
            flops=8_000_000_000, bytes_accessed=100_000_000, transcendentals=0
        ),
    )(tokens, *matrices, latent_queries)
    block = (swin_query, swin_keyvalue, swin_out, mlp_up, mlp_down)
    return pl.pallas_call(
        window_kernel,
        out_shape=jax.ShapeDtypeStruct((WLAT, 2 * HALF, LATENT, D), BF16),
        in_specs=[near, near] + [whole] * len(block),
        out_specs=near,
        scratch_shapes=[
            *[pltpu.VMEM(m.shape, m.dtype) for m in block],
            pltpu.VMEM((D, ROWS), BF16),
            pltpu.VMEM((D, ROWS), F32),
            pltpu.VMEM((D // 128, 2 * PATCHES * 4, 128), F32),
            pltpu.SemaphoreType.DMA((len(block),)),
        ],
        compiler_params=pltpu.CompilerParams(vmem_limit_bytes=40 * 1024 * 1024),
        cost_estimate=pl.CostEstimate(
            flops=2_000_000_000, bytes_accessed=7_000_000, transcendentals=0
        ),
    )(latent, norm_gains, *block)


def solution(mesh):
    placed = (P(None, "tile", "var", None), P(), P(), P(), P(), P(), P(), P(), P(), P(), P(), P())
    return jax.shard_map(
        body, mesh=mesh, in_specs=placed, out_specs=P("var", "tile", None, None), check_vma=False
    )
```
